128 devices in a mesh: row: 16 (over x, z_hi, core), col: 8 (over y, z_lo).
Axes of the slice: x: 4, y: 4, z: 4 (z_hi: 2, z_lo: 2; z = z_hi * 2 + z_lo), core: 2. Of those that a mesh axis runs over, the one named last changes fastest.
Arguments:
- nodes: bfloat16 [131072, 256], P(('row', 'col')), may hold values from -6 to 6
- tiles: bfloat16 [1024, 8, 4, 128, 128], P('row', 'col'), may hold values from -0.12988281 to 0.12988281
- tile_col: int32 [1024, 8, 4], P('row', 'col'), may hold values from 0 to 127, as said below
- tile_count: int32 [1024, 8], P('row', 'col'), may hold values from 0 to 4, as said below
- w_in: bfloat16 [512, 256], replicated, may hold values from -0.25 to 0.25
- bias_in: float32 [256], replicated, may hold values from -3 to 3
- w_out: bfloat16 [256, 256], replicated, may hold values from -0.375 to 0.375
- ln_gain: float32 [256], replicated, may hold values from 0.1 to 1.9
- ln_shift: float32 [256], replicated, may hold values from -3 to 3
- cotangent: bfloat16 [131072, 256], P(('row', 'col')), may hold values from -6 to 6
Outputs:
- updated: bfloat16 [131072, 256], P(('row', 'col'))
- grad_nodes: bfloat16 [131072, 256], P(('row', 'col'))
- grad_tiles: bfloat16 [1024, 8, 4, 128, 128], P('row', 'col')
- grad_w_in: float32 [512, 256], replicated
- grad_w_out: float32 [256, 256], replicated
- grad_vectors: float32 [3, 256], replicated
The draws below stay inside these ranges and needn't reach their ends.
Inputs may be any that keep to these rules, and one draw needn't show every extreme that they name: `tile_col`: index within the column group; slots at or past the block row's tile_count are ignored. `tile_count`: loads differ between devices; 4 is reached in every draw.
All inputs are finite; a program needn't handle non-finite values.
Results may differ from the reference program's by a relative error of at most 0.02.
Values may be sent and summed in bfloat16 or wider, within the bound.
A program may use at most 256 MiB of HBM per device.

```python
import jax
import jax.numpy as jnp
from jax import lax

D = 256
BS = 128
KS = 4
BPD = 8
NODES = 131072
NB = 1024
RB = 64
CB = 128
N_ROW = 16
N_COL = 8


def draw_tile_col(key, part):
    key = jax.random.fold_in(key, 11)
    return jax.random.randint(key, (NB, N_COL, KS), 0, CB).astype(jnp.int32)


def draw_tile_count(key, part):
    key = jax.random.fold_in(key, 23)
    level_key, count_key = jax.random.split(key)
    groups = NB // RB
    levels = jax.random.randint(level_key, (groups, 1, N_COL), 1, KS + 1)
    counts = jax.random.randint(count_key, (groups, RB, N_COL), 0, KS + 1)
    counts = jnp.minimum(counts, levels).reshape(NB, N_COL)
    return counts.at[0, 0].set(KS).astype(jnp.int32)


def steps_of(own_key, extent, cuts, least, high):
    def one(dim, blocks):
        steps = jax.random.uniform(jax.random.fold_in(jax.random.fold_in(own_key, 6), dim), (blocks,), jnp.float32, least / len(cuts), high / len(cuts))
        return jnp.repeat(jnp.exp(steps), extent[dim] // blocks).reshape((-1,) + (1,) * (len(extent) - dim - 1))

    level = one(*cuts[0])
    for cut in cuts[1:]:
        level = level * one(*cut)
    return level


def normal_values(stream_key, shape, width, limit, shards=(), held_as=jnp.bfloat16):
    gain = steps_of(stream_key, shape, shards, -0.22, 0.18) if shards else 1.0
    entries = jax.random.normal(stream_key, shape, jnp.float32) * width * gain
    return jnp.minimum(jnp.maximum(entries, -limit), limit).astype(held_as)


def setup_inputs(seed: int = 0) -> dict:
    arg_keys = jax.random.split(jax.random.key(seed), 11)
    return {
        "nodes": normal_values(arg_keys[0], (NODES, D), 1.0, 6.0, ((0, 128),)),
        "tiles": normal_values(arg_keys[1], (NB, N_COL, KS, BS, BS), 0.022, 0.12988281, ((0, 16), (1, 8))),
        "tile_col": draw_tile_col(jax.random.fold_in(arg_keys[10], 71), 0),
        "tile_count": draw_tile_count(jax.random.fold_in(arg_keys[10], 71), 0),
        "w_in": normal_values(arg_keys[4], (2 * D, D), (2 * D) ** -0.5, 0.25),
        "bias_in": normal_values(arg_keys[5], (D,), 0.5, 3.0, (), jnp.float32),
        "w_out": normal_values(arg_keys[6], (D, D), D ** -0.5, 0.375),
        "ln_gain": jnp.clip(1.0 + 0.18 * jax.random.normal(arg_keys[7], (D,), jnp.float32), 0.1, 1.9),
        "ln_shift": normal_values(arg_keys[8], (D,), 0.5, 3.0, (), jnp.float32),
        "cotangent": normal_values(arg_keys[9], (NODES, D), 1.0, 6.0, ((0, 128),)),
    }


def source_blocks(tile_col):
    column = lax.broadcasted_iota(jnp.int32, tile_col.shape, 1)
    return ((tile_col // BPD * N_COL + column) * BPD + tile_col % BPD).astype(jnp.int32)

def live_mask(tile_count):
    slot = lax.broadcasted_iota(jnp.int32, (NB, N_COL, KS), 2)
    return slot < tile_count[:, :, None]

def reference(nodes, tiles, tile_col, tile_count, w_in, bias_in, w_out, ln_gain, ln_shift, cotangent):
    live = live_mask(tile_count)
    live_tiles = jnp.where(live[:, :, :, None, None], tiles, jnp.zeros((), tiles.dtype))
    source = source_blocks(tile_col)
    node_blocks = nodes.reshape(NB, BS, D)
    group_tiles = live_tiles.reshape(N_ROW, RB, N_COL, KS, BS, BS)
    group_source = source.reshape(N_ROW, RB, N_COL, KS)

    def forward_group(args):
        tile_group, src_group = args
        picked = node_blocks[src_group].astype(jnp.float32)
        parts = jnp.einsum('rckij,rckjd->rcid', tile_group.astype(jnp.float32), picked)
        rounded = parts.astype(jnp.bfloat16).astype(jnp.float32)
        return lax.optimization_barrier(jnp.sum(rounded, axis=1))
    message = lax.map(forward_group, (group_tiles, group_source)).reshape(NODES, D).astype(jnp.bfloat16)
    pre = jnp.dot(nodes, w_in[:D], preferred_element_type=jnp.float32) + jnp.dot(message, w_in[D:], preferred_element_type=jnp.float32) + bias_in
    act = (pre * jax.nn.sigmoid(pre)).astype(jnp.bfloat16)
    proj = jnp.dot(act, w_out, preferred_element_type=jnp.float32)
    mean = lax.optimization_barrier(jnp.mean(proj, axis=-1, keepdims=True))
    var = lax.optimization_barrier(jnp.mean((proj - mean) ** 2, axis=-1, keepdims=True))
    rstd = 1.0 / jnp.sqrt(var + 1e-05)
    normed = (proj - mean) * rstd
    updated = (nodes.astype(jnp.float32) + normed * ln_gain + ln_shift).astype(jnp.bfloat16)
    grad_out = cotangent.astype(jnp.float32)
    gscaled = grad_out * ln_gain
    gproj = ((gscaled - lax.optimization_barrier(jnp.mean(gscaled, axis=-1, keepdims=True)) - normed * lax.optimization_barrier(jnp.mean(gscaled * normed, axis=-1, keepdims=True))) * rstd).astype(jnp.bfloat16)
    gact = jnp.dot(gproj, w_out.T, preferred_element_type=jnp.float32)
    sig = jax.nn.sigmoid(pre)
    gpre = gact * sig * (1.0 + pre * (1.0 - sig))
    gpre_b = gpre.astype(jnp.bfloat16)
    gmsg = jnp.dot(gpre_b, w_in[D:].T, preferred_element_type=jnp.float32).astype(jnp.bfloat16)
    direct = grad_out + jnp.dot(gpre_b, w_in[:D].T, preferred_element_type=jnp.float32)
    gmsg_groups = gmsg.reshape(N_ROW, RB, BS, D)

    def backward_group(total, args):
        tile_group, src_group, grad_group = args
        back = jnp.einsum('rckij,rid->rckjd', tile_group.astype(jnp.float32), grad_group.astype(jnp.float32))
        seg = (lax.broadcasted_iota(jnp.int32, (RB, N_COL, KS), 1) * NB + src_group).reshape(-1)
        summed = jax.ops.segment_sum(back.reshape(RB * N_COL * KS, BS, D), seg, num_segments=N_COL * NB)
        rounded = summed.astype(jnp.bfloat16).astype(jnp.float32)
        return (total + lax.optimization_barrier(jnp.sum(rounded.reshape(N_COL, NB, BS, D), axis=0)), None)
    agg, _ = lax.scan(backward_group, jnp.zeros((NB, BS, D), jnp.float32), (group_tiles, group_source, gmsg_groups))
    grad_nodes = (direct + agg.reshape(NODES, D)).astype(jnp.bfloat16)

    def tile_group_grad(args):
        src_group, grad_group = args
        picked = node_blocks[src_group].astype(jnp.float32)
        return jnp.einsum('rid,rckjd->rckij', grad_group.astype(jnp.float32), picked)
    tile_grads = lax.map(tile_group_grad, (group_source, gmsg_groups)).reshape(NB, N_COL, KS, BS, BS)
    tile_grads = jnp.where(live[:, :, :, None, None], tile_grads * jnp.float32(D) ** (-0.5), jnp.float32(0.0)).astype(jnp.bfloat16)
    factor = jnp.float32(NODES) ** (-0.5)
    grad_w_in = jnp.concatenate([jnp.dot(nodes.T, gpre_b, preferred_element_type=jnp.float32), jnp.dot(message.T, gpre_b, preferred_element_type=jnp.float32)], axis=0) * factor
    grad_w_out = jnp.dot(act.T, gproj, preferred_element_type=jnp.float32) * factor
    grad_vectors = jnp.stack([lax.optimization_barrier(jnp.sum(gpre, axis=0)), lax.optimization_barrier(jnp.sum(grad_out * normed, axis=0)), lax.optimization_barrier(jnp.sum(grad_out, axis=0))]) * factor
    return (updated, grad_nodes, tile_grads, grad_w_in, grad_w_out, grad_vectors)
```

```python
import functools

import jax
import jax.numpy as jnp
from jax import lax
from jax.experimental import pallas as pl
from jax.experimental.pallas import tpu as pltpu
from jax.sharding import PartitionSpec as P

F32, BF16 = jnp.float32, jnp.bfloat16
MIB = 1024 * 1024
VMEM_LIMIT = 56 * MIB
EPS = 1e-05


class Place:
    def __init__(self):
        self.row = lax.axis_index("row")
        self.col = lax.axis_index("col")
        self.x = lax.div(self.row, 4)
        self.zh = lax.rem(lax.div(self.row, 2), 2)
        self.core = lax.rem(self.row, 2)
        self.y = lax.div(self.col, 2)
        self.zl = lax.rem(self.col, 2)


class RowGroup:
    def __init__(self, place):
        self.place = place
        col = place.col
        self.peers = {
            "p": (self.slot(1, 0), col),
            "m": (self.slot(3, 0), col),
            "pair": (self.slot(0, 1), col),
            "sib": (self.slot(0, 0, 1), col),
        }

    def slot(self, ring, pair, sib=0):
        at = self.place
        return (
            lax.rem(at.x + ring, 4) * 4
            + lax.rem(at.zh + pair, 2) * 2
            + lax.rem(at.core + sib, 2)
        )


class ColGroup:
    def __init__(self, place):
        self.place = place
        row = place.row
        self.peers = {
            "p": (row, self.slot(1, 0)),
            "m": (row, self.slot(3, 0)),
            "pair": (row, self.slot(0, 1)),
        }

    def slot(self, ring, pair):
        at = self.place
        return lax.rem(at.y + ring, 4) * 2 + lax.rem(at.zl + pair, 2)


class Wire:
    def __init__(self, send, recv):
        self.send, self.recv = send, recv
        self.names = {}
        self.open = []

    def index(self, name):
        return self.names.setdefault(name, len(self.names))

    def push(self, name, src, dst, to):
        at = self.index(name)
        copy = pltpu.make_async_remote_copy(
            src_ref=src,
            dst_ref=dst,
            send_sem=self.send.at[at],
            recv_sem=self.recv.at[at],
            device_id=to,
            device_id_type=pl.DeviceIdType.MESH,
        )
        copy.start()
        self.open.append(copy)

    def take(self, name, dst, to):
        at = self.index(name)
        pltpu.make_async_remote_copy(
            src_ref=dst,
            dst_ref=dst,
            send_sem=self.send.at[at],
            recv_sem=self.recv.at[at],
            device_id=to,
            device_id_type=pl.DeviceIdType.MESH,
        ).wait_recv()

    def drain(self):
        for copy in self.open:
            copy.wait_send()
        self.open = []


def greet(devices):
    barrier = pltpu.get_barrier_semaphore()
    for device in devices:
        pl.semaphore_signal(barrier, inc=1, device_id=device, device_id_type=pl.DeviceIdType.MESH)
    pl.semaphore_wait(barrier, len(devices))


MOVES = {"p": (3, 0, 0), "m": (1, 0, 0), "pair": (0, 1, 0), "sib": (0, 0, 1)}


def gather(wire, group, buf, tag, src=None):
    rows = buf.shape[1]
    half_rows = rows // 2
    cut = (pl.ds(0, half_rows), pl.ds(half_rows, half_rows))
    has_sib = "sib" in group.peers

    def send(ring, pair, half, way, origin=None):
        ref = buf.at[group.slot(ring, pair), cut[half]]
        dr, dp, dk = MOVES[way]
        name = (tag, (ring + dr) % 4, (pair + dp) % 2, dk, half)
        wire.push(name, ref if origin is None else origin.at[cut[half]], ref, group.peers[way])

    def take(ring, pair, half, sib=0):
        slot = group.slot(ring, pair, 1) if sib else group.slot(ring, pair)
        wire.take((tag, ring, pair, sib, half), buf.at[slot, cut[half]], group.peers["p"])

    def share(ring, pair, half, origin=None):
        if has_sib:
            send(ring, pair, half, "sib", origin)

    send(0, 0, 0, "p", src)
    send(0, 0, 1, "m", src)
    send(0, 0, 0, "pair", src)
    send(0, 0, 1, "p", src)
    send(0, 0, 0, "m", src)
    send(0, 0, 1, "pair", src)
    for half in (0, 1):
        share(0, 0, half, src)
    yield
    take(3, 0, 0)
    send(3, 0, 0, "p")
    take(1, 0, 1)
    send(1, 0, 1, "m")
    share(3, 0, 0)
    share(1, 0, 1)
    yield
    for half in (0, 1):
        take(0, 1, half)
        send(0, 1, half, "p")
        send(0, 1, half, "m")
        share(0, 1, half)
    yield
    take(3, 0, 1)
    take(1, 0, 0)
    share(3, 0, 1)
    share(1, 0, 0)
    yield
    take(3, 1, 0)
    send(3, 1, 0, "p")
    take(1, 1, 1)
    send(1, 1, 1, "m")
    share(3, 1, 0)
    share(1, 1, 1)
    yield
    for half in (0, 1):
        take(2, 0, half)
        share(2, 0, half)
    yield
    take(3, 1, 1)
    take(1, 1, 0)
    share(3, 1, 1)
    share(1, 1, 0)
    for half in (0, 1):
        take(2, 1, half)
        share(2, 1, half)
    yield
    if has_sib:
        for ring in (0, 1, 3, 2):
            for pair in (0, 1):
                for half in (0, 1):
                    take(ring, pair, half, 1)


def add_rows(rows, step, body):
    def one(i, carry):
        body(pl.ds(pl.multiple_of(i * step, step), step))
        return carry

    lax.fori_loop(0, rows // step, one, 0)


def scatter_shapes(rows, width):
    return [
        pltpu.VMEM((2, rows // 2, width), BF16),
        pltpu.VMEM((2, rows // 2, width), BF16),
        pltpu.VMEM((2, rows, width), BF16),
        pltpu.VMEM((2, rows, width), BF16),
        pltpu.VMEM((rows, width), BF16),
    ]


def scatter(wire, group, terms, bufs, tag, prepare):
    relay_m, relay_p, from_m, from_p, from_pair = bufs
    rows = terms.shape[1]
    half_rows = rows // 2
    cut = (pl.ds(0, half_rows), pl.ds(half_rows, half_rows))
    step = 128

    def part(ring, pair, half):
        return terms.at[group.slot(ring, pair), cut[half]]

    def add(target, *others):
        def body(at):
            total = target[at].astype(F32)
            for other in others:
                total = total + other[at].astype(F32)
            target[at] = total.astype(BF16)

        add_rows(half_rows, step, body)

    for q in (1, 0):
        prepare(2, q)
        wire.push((tag, "rm", q), part(2, q, 0), relay_m.at[q], group.peers["p"])
        wire.push((tag, "rp", q), part(2, q, 1), relay_p.at[q], group.peers["m"])
    yield
    for q in (1, 0):
        prepare(1, q)
        prepare(3, q)
        wire.push((tag, "m", q, 1), part(1, q, 1), from_m.at[q, cut[1]], group.peers["p"])
        wire.push((tag, "p", q, 0), part(3, q, 0), from_p.at[q, cut[0]], group.peers["m"])
        yield
        wire.take((tag, "rm", q), relay_m.at[q], group.peers["p"])
        add(part(1, q, 0), relay_m.at[q])
        wire.push((tag, "m", q, 0), part(1, q, 0), from_m.at[q, cut[0]], group.peers["p"])
        wire.take((tag, "rp", q), relay_p.at[q], group.peers["p"])
        add(part(3, q, 1), relay_p.at[q])
        wire.push((tag, "p", q, 1), part(3, q, 1), from_p.at[q, cut[1]], group.peers["m"])
    yield
    prepare(0, 1)
    for half in (0, 1):
        wire.take((tag, "m", 1, half), from_m.at[1, cut[half]], group.peers["p"])
        wire.take((tag, "p", 1, half), from_p.at[1, cut[half]], group.peers["p"])
        add(part(0, 1, half), from_m.at[1, cut[half]], from_p.at[1, cut[half]])
        wire.push((tag, "z", half), part(0, 1, half), from_pair.at[cut[half]], group.peers["pair"])
    yield
    prepare(0, 0)
    for half in (0, 1):
        wire.take((tag, "m", 0, half), from_m.at[0, cut[half]], group.peers["p"])
        wire.take((tag, "p", 0, half), from_p.at[0, cut[half]], group.peers["p"])
    for half in (0, 1):
        wire.take((tag, "z", half), from_pair.at[cut[half]], group.peers["p"])


def run(steps):
    for _ in steps:
        pass


def dot(a, b, dims=((1,), (0,))):
    return lax.dot_general(a, b, (dims, ((), ())), preferred_element_type=F32)


ANY = pl.BlockSpec(memory_space=pl.ANY)
VM = pl.BlockSpec(memory_space=pltpu.VMEM)


def remote_params(collective_id):
    return pltpu.CompilerParams(
        collective_id=collective_id, has_side_effects=True, vmem_limit_bytes=VMEM_LIMIT
    )


def node_gather_kernel(nodes, out, send, recv, own_sem):
    group = RowGroup(Place())
    greet(list(group.peers.values()))
    own = pltpu.make_async_copy(nodes, out.at[group.slot(0, 0)], own_sem)
    own.start()
    wire = Wire(send, recv)
    run(gather(wire, group, out, "n", nodes))
    wire.drain()
    own.wait()


def node_gather(nodes):
    rows, width = nodes.shape
    return pl.pallas_call(
        node_gather_kernel,
        out_shape=jax.ShapeDtypeStruct((16, rows, width), BF16),
        in_specs=[ANY],
        out_specs=ANY,
        scratch_shapes=[
            pltpu.SemaphoreType.DMA((30,)),
            pltpu.SemaphoreType.DMA((30,)),
            pltpu.SemaphoreType.DMA,
        ],
        compiler_params=remote_params(1),
        name="node_gather",
    )(nodes)


def forward_kernel(cols, count, tiles, nodes, out):
    step = pl.program_id(0)
    per = tiles.shape[0]
    for i in range(per):
        at = step * per + i
        live = count[at]
        base = pl.ds(i * 128, 128)

        @pl.when(live <= 2)
        def _():
            pair = jnp.concatenate(
                [jnp.where(k < live, tiles[i, k], jnp.zeros((), BF16)) for k in (0, 1)], axis=1
            )
            picked = jnp.concatenate([nodes[cols[at, k]] for k in (0, 1)], axis=0)
            out[base] = dot(pair, picked).astype(BF16)

        @pl.when(live > 2)
        def _():
            four = jnp.concatenate(
                [jnp.where(k < live, tiles[i, k], jnp.zeros((), BF16)) for k in range(4)], axis=1
            )
            picked = jnp.concatenate([nodes[cols[at, k]] for k in range(4)], axis=0)
            out[base] = dot(four, picked).astype(BF16)


def forward(cols, count, tiles, nodes):
    row_blocks = tiles.shape[0]
    width = nodes.shape[-1]
    per = 8
    return pl.pallas_call(
        forward_kernel,
        out_shape=jax.ShapeDtypeStruct((row_blocks * 128, width), BF16),
        grid_spec=pltpu.PrefetchScalarGridSpec(
            num_scalar_prefetch=2,
            grid=(row_blocks // per,),
            in_specs=[
                pl.BlockSpec((per, 4, 128, 128), lambda s, *_: (s, 0, 0, 0)),
                pl.BlockSpec(nodes.shape, lambda s, *_: (0, 0, 0)),
            ],
            out_specs=pl.BlockSpec((per * 128, width), lambda s, *_: (s, 0)),
        ),
        compiler_params=pltpu.CompilerParams(vmem_limit_bytes=VMEM_LIMIT),
        name="forward",
    )(cols, count, tiles, nodes)


def middle_kernel(
    partial, nodes, cot, w_in, bias, w_out, gain, shift,
    grads, updated, direct, gw_in, gw_out, gvec,
    terms, relay_m, relay_p, from_m, from_p, from_pair,
    msg_s, act_s, gproj_s, gpre_s, send, recv, load,
):
    group = ColGroup(Place())
    width = nodes.shape[1]
    rows = nodes.shape[0]

    def loader(ring, pair):
        slot = group.slot(ring, pair)
        return pltpu.make_async_copy(partial.at[slot], terms.at[slot], load.at[ring * 2 + pair])

    for ring in (2, 1, 3, 0):
        for pair in (1, 0):
            loader(ring, pair).start()
    greet(list(group.peers.values()))
    wire = Wire(send, recv)
    bufs = (relay_m, relay_p, from_m, from_p, from_pair)
    run(scatter(wire, group, terms, bufs, "s", lambda ring, pair: loader(ring, pair).wait()))
    own = group.slot(0, 0)
    gvec[...] = jnp.zeros_like(gvec)

    def chunk(i, carry):
        at = pl.ds(pl.multiple_of(i * 256, 256), 256)
        msg = (
            terms[own, at].astype(F32)
            + from_m[0, at].astype(F32)
            + from_p[0, at].astype(F32)
            + from_pair[at].astype(F32)
        ).astype(BF16)
        msg_s[at] = msg
        mine = nodes[at]
        pre = dot(mine, w_in[:width]) + dot(msg, w_in[width:]) + bias[...]
        sig = jax.nn.sigmoid(pre)
        act = (pre * sig).astype(BF16)
        act_s[at] = act
        proj = dot(act, w_out[...])
        mean = jnp.mean(proj, axis=-1, keepdims=True)
        off = proj - mean
        var = jnp.mean(off * off, axis=-1, keepdims=True)
        rstd = 1.0 / jnp.sqrt(var + EPS)
        normed = off * rstd
        updated[at] = (mine.astype(F32) + normed * gain[...] + shift[...]).astype(BF16)
        grad_out = cot[at].astype(F32)
        gscaled = grad_out * gain[...]
        gproj = (
            (
                gscaled
                - jnp.mean(gscaled, axis=-1, keepdims=True)
                - normed * jnp.mean(gscaled * normed, axis=-1, keepdims=True)
            )
            * rstd
        ).astype(BF16)
        gproj_s[at] = gproj
        gact = dot(gproj, w_out[...], ((1,), (1,)))
        gpre = gact * sig * (1.0 + pre * (1.0 - sig))
        gpre_b = gpre.astype(BF16)
        gpre_s[at] = gpre_b
        grads[own, at] = dot(gpre_b, w_in[width:], ((1,), (1,))).astype(BF16)
        direct[at] = grad_out + dot(gpre_b, w_in[:width], ((1,), (1,)))
        gvec[0:1] += jnp.sum(gpre, axis=0, keepdims=True)
        gvec[1:2] += jnp.sum(grad_out * normed, axis=0, keepdims=True)
        gvec[2:3] += jnp.sum(grad_out, axis=0, keepdims=True)
        return carry

    lax.fori_loop(0, rows // 256, chunk, 0)
    steps = gather(wire, group, grads, "g")
    next(steps)
    gw_in[:width] = dot(nodes[...], gpre_s[...], ((0,), (0,)))
    gw_in[width:] = dot(msg_s[...], gpre_s[...], ((0,), (0,)))
    gw_out[...] = dot(act_s[...], gproj_s[...], ((0,), (0,)))
    run(steps)
    wire.drain()


def middle(partial, nodes, cot, w_in, bias, w_out, gain, shift):
    rows, width = nodes.shape
    one = functools.partial(pltpu.VMEM, (rows, width))
    return pl.pallas_call(
        middle_kernel,
        out_shape=[
            jax.ShapeDtypeStruct((8, rows, width), BF16),
            jax.ShapeDtypeStruct((rows, width), BF16),
            jax.ShapeDtypeStruct((rows, width), F32),
            jax.ShapeDtypeStruct((2 * width, width), F32),
            jax.ShapeDtypeStruct((width, width), F32),
            jax.ShapeDtypeStruct((3, width), F32),
        ],
        in_specs=[ANY] + [VM] * 7,
        out_specs=[VM] * 6,
        scratch_shapes=[pltpu.VMEM((8, rows, width), BF16)]
        + scatter_shapes(rows, width)
        + [one(BF16)] * 4
        + [
            pltpu.SemaphoreType.DMA((40,)),
            pltpu.SemaphoreType.DMA((40,)),
            pltpu.SemaphoreType.DMA((8,)),
        ],
        compiler_params=remote_params(2),
        name="middle",
    )(partial.reshape(8, rows, width), nodes, cot, w_in, bias, w_out, gain, shift)


def backward_kernel(cols, count, tiles, nodes, grads, tile_grads, back, acc):
    step = pl.program_id(0)
    per = tiles.shape[0]

    @pl.when(step == 0)
    def _():
        def clear(i, carry):
            acc[i] = jnp.zeros(acc.shape[1:], F32)
            return carry

        lax.fori_loop(0, acc.shape[0], clear, 0)

    scale = F32(256.0) ** F32(-0.5)
    for i in range(per):
        at = step * per + i
        live = count[at]
        base = pl.ds(i * 128, 128)
        for k in range(4):
            @pl.when(k < live)
            def _():
                col = cols[at, k]
                grad = grads[base]
                tile_grads[i, k] = (dot(grad, nodes[col], ((1,), (1,))) * scale).astype(BF16)
                acc[col] += dot(tiles[i, k], grad, ((0,), (0,)))

            @pl.when(k >= live)
            def _():
                tile_grads[i, k] = jnp.zeros((128, 128), BF16)

    @pl.when(step == pl.num_programs(0) - 1)
    def _():
        def put(i, carry):
            back[i] = acc[i].astype(BF16)
            return carry

        lax.fori_loop(0, acc.shape[0], put, 0)


def backward(cols, count, tiles, nodes, grads):
    row_blocks = tiles.shape[0]
    blocks, _, width = nodes.shape
    per = 8
    return pl.pallas_call(
        backward_kernel,
        out_shape=[
            jax.ShapeDtypeStruct(tiles.shape, BF16),
            jax.ShapeDtypeStruct(nodes.shape, BF16),
        ],
        grid_spec=pltpu.PrefetchScalarGridSpec(
            num_scalar_prefetch=2,
            grid=(row_blocks // per,),
            in_specs=[
                pl.BlockSpec((per, 4, 128, 128), lambda s, *_: (s, 0, 0, 0)),
                pl.BlockSpec(nodes.shape, lambda s, *_: (0, 0, 0), pipeline_mode=pl.Buffered(1)),
                pl.BlockSpec((per * 128, width), lambda s, *_: (s, 0)),
            ],
            out_specs=[
                pl.BlockSpec((per, 4, 128, 128), lambda s, *_: (s, 0, 0, 0)),
                pl.BlockSpec(nodes.shape, lambda s, *_: (0, 0, 0), pipeline_mode=pl.Buffered(1)),
            ],
            scratch_shapes=[pltpu.VMEM(nodes.shape, F32)],
        ),
        compiler_params=pltpu.CompilerParams(vmem_limit_bytes=VMEM_LIMIT),
        name="backward",
    )(cols, count, tiles, nodes, grads)


def finish_kernel(
    back, direct, out,
    terms, others, relay_m, relay_p, from_m, from_p, from_pair, send, recv, load,
):
    group = RowGroup(Place())
    rows = terms.shape[1]
    order = [(2, 1), (2, 0), (1, 1), (3, 1), (1, 0), (3, 0), (0, 1), (0, 0)]

    def loader(ring, pair):
        slot = group.slot(ring, pair)
        return pltpu.make_async_copy(back.at[slot], terms.at[slot], load.at[ring * 2 + pair])

    for at in order:
        loader(*at).start()
    greet(list(group.peers.values()))
    wire = Wire(send, recv)
    for ring, pair in order:
        wire.push(
            ("f", ring, pair),
            back.at[group.slot(ring, pair, 1)],
            others.at[ring * 2 + pair],
            group.peers["sib"],
        )

    def prepare(ring, pair):
        loader(ring, pair).wait()
        other = others.at[ring * 2 + pair]
        wire.take(("f", ring, pair), other, group.peers["sib"])
        slot = group.slot(ring, pair)

        def body(at):
            terms[slot, at] = (terms[slot, at].astype(F32) + other[at].astype(F32)).astype(BF16)

        add_rows(rows, 128, body)

    bufs = (relay_m, relay_p, from_m, from_p, from_pair)
    run(scatter(wire, group, terms, bufs, "b", prepare))
    own = group.slot(0, 0)

    def last(at):
        out[at] = (
            direct[at]
            + terms[own, at].astype(F32)
            + from_m[0, at].astype(F32)
            + from_p[0, at].astype(F32)
            + from_pair[at].astype(F32)
        ).astype(BF16)

    add_rows(rows, 128, last)
    wire.drain()


def finish(back, direct):
    rows, width = direct.shape
    return pl.pallas_call(
        finish_kernel,
        out_shape=jax.ShapeDtypeStruct((rows, width), BF16),
        in_specs=[ANY, VM],
        out_specs=VM,
        scratch_shapes=[
            pltpu.VMEM((16, rows, width), BF16),
            pltpu.VMEM((8, rows, width), BF16),
        ]
        + scatter_shapes(rows, width)
        + [
            pltpu.SemaphoreType.DMA((40,)),
            pltpu.SemaphoreType.DMA((40,)),
            pltpu.SemaphoreType.DMA((8,)),
        ],
        compiler_params=remote_params(3),
        name="finish",
    )(back.reshape(16, rows, width), direct)


def body(nodes, tiles, tile_col, tile_count, w_in, bias_in, w_out, ln_gain, ln_shift, cotangent):
    rows, width = nodes.shape
    cols, count = tile_col[:, 0], tile_count[:, 0]
    slots = tiles[:, 0]
    cols = jnp.clip(cols, 0, 127)
    gathered = node_gather(nodes).reshape(128, 128, width)
    partial = forward(cols, count, slots, gathered)
    grads, updated, direct, gw_in, gw_out, gvec = middle(
        partial, nodes, cotangent, w_in, bias_in[None], w_out, ln_gain[None], ln_shift[None]
    )
    gw_in, gw_out, gvec = lax.psum((gw_in, gw_out, gvec), ("row", "col"))
    grad_tiles, back = backward(cols, count, slots, gathered, grads.reshape(8 * rows, width))
    grad_nodes = finish(back, direct)
    total_nodes = rows * lax.axis_size("row") * lax.axis_size("col")
    factor = jnp.float32(total_nodes) ** (-0.5)
    return (
        updated,
        grad_nodes,
        grad_tiles[:, None],
        gw_in * factor,
        gw_out * factor,
        gvec * factor,
    )


def solution(mesh):
    placed = (
        P(("row", "col"), None),
        P("row", "col", None, None, None),
        P("row", "col", None),
        P("row", "col"),
        P(),
        P(),
        P(),
        P(),
        P(),
        P(("row", "col"), None),
    )
    return jax.shard_map(
        body,
        mesh=mesh,
        in_specs=placed,
        out_specs=(
            P(("row", "col"), None),
            P(("row", "col"), None),
            P("row", "col", None, None, None),
            P(),
            P(),
            P(),
        ),
        check_vma=False,
    )
```

```python
import functools

import jax
import jax.numpy as jnp
from jax import lax
from jax.experimental import pallas as pl
from jax.experimental.pallas import tpu as pltpu
from jax.sharding import PartitionSpec as P

F32, BF16 = jnp.float32, jnp.bfloat16
MIB = 1024 * 1024
VMEM_LIMIT = 56 * MIB
EPS = 1e-05
TOTAL_ROWS = 1024


class Place:
    def __init__(self):
        self.row = lax.axis_index("row")
        self.col = lax.axis_index("col")
        self.x = lax.div(self.row, 4)
        self.zh = lax.rem(lax.div(self.row, 2), 2)
        self.core = lax.rem(self.row, 2)
        self.y = lax.div(self.col, 2)
        self.zl = lax.rem(self.col, 2)


    def peer(self, x=0, y=0, z=0, core=0):
        z_at = lax.rem(self.zh * 2 + self.zl + z, 4)
        row = lax.rem(self.x + x, 4) * 4 + lax.div(z_at, 2) * 2 + lax.rem(self.core + core, 2)
        return (row, lax.rem(self.y + y, 4) * 2 + lax.rem(z_at, 2))

    def all_peers(self):
        steps = [dict(core=1)] + [{axis: d} for axis in "xyz" for d in (1, 2, 3)]
        return [self.peer(**step) for step in steps]


class RowGroup:
    def __init__(self, place):
        self.place = place
        col = place.col
        self.peers = {
            "p": (self.slot(1, 0), col),
            "m": (self.slot(3, 0), col),
            "pair": (self.slot(0, 1), col),
            "sib": (self.slot(0, 0, 1), col),
        }

    def slot(self, ring, pair, sib=0):
        at = self.place
        return (
            lax.rem(at.x + ring, 4) * 4
            + lax.rem(at.zh + pair, 2) * 2
            + lax.rem(at.core + sib, 2)
        )


class ColGroup:
    def __init__(self, place):
        self.place = place
        row = place.row
        self.peers = {
            "p": (row, self.slot(1, 0)),
            "m": (row, self.slot(3, 0)),
            "pair": (row, self.slot(0, 1)),
        }

    def slot(self, ring, pair):
        at = self.place
        return lax.rem(at.y + ring, 4) * 2 + lax.rem(at.zl + pair, 2)


class Wire:
    def __init__(self, send, recv):
        self.send, self.recv = send, recv
        self.names = {}
        self.open = []

    def index(self, name):
        return self.names.setdefault(name, len(self.names))

    def push(self, name, src, dst, to):
        at = self.index(name)
        copy = pltpu.make_async_remote_copy(
            src_ref=src,
            dst_ref=dst,
            send_sem=self.send.at[at],
            recv_sem=self.recv.at[at],
            device_id=to,
            device_id_type=pl.DeviceIdType.MESH,
        )
        copy.start()
        self.open.append(copy)

    def take(self, name, dst, to):
        at = self.index(name)
        pltpu.make_async_remote_copy(
            src_ref=dst,
            dst_ref=dst,
            send_sem=self.send.at[at],
            recv_sem=self.recv.at[at],
            device_id=to,
            device_id_type=pl.DeviceIdType.MESH,
        ).wait_recv()

    def drain(self):
        for copy in self.open:
            copy.wait_send()
        self.open = []


def greet(devices):
    barrier = pltpu.get_barrier_semaphore()
    for device in devices:
        pl.semaphore_signal(barrier, inc=1, device_id=device, device_id_type=pl.DeviceIdType.MESH)
    pl.semaphore_wait(barrier, len(devices))


MOVES = {"p": (3, 0, 0), "m": (1, 0, 0), "pair": (0, 1, 0), "sib": (0, 0, 1)}


def gather(wire, group, buf, tag, src=None):
    rows = buf.shape[1]
    half_rows = rows // 2
    cut = (pl.ds(0, half_rows), pl.ds(half_rows, half_rows))
    has_sib = "sib" in group.peers

    def send(ring, pair, half, way, origin=None):
        ref = buf.at[group.slot(ring, pair), cut[half]]
        dr, dp, dk = MOVES[way]
        name = (tag, (ring + dr) % 4, (pair + dp) % 2, dk, half)
        wire.push(name, ref if origin is None else origin.at[cut[half]], ref, group.peers[way])

    def take(ring, pair, half, sib=0):
        slot = group.slot(ring, pair, 1) if sib else group.slot(ring, pair)
        wire.take((tag, ring, pair, sib, half), buf.at[slot, cut[half]], group.peers["p"])

    def share(ring, pair, half, origin=None):
        if has_sib:
            send(ring, pair, half, "sib", origin)

    send(0, 0, 0, "p", src)
    send(0, 0, 1, "m", src)
    send(0, 0, 0, "pair", src)
    send(0, 0, 1, "p", src)
    send(0, 0, 0, "m", src)
    send(0, 0, 1, "pair", src)
    for half in (0, 1):
        share(0, 0, half, src)
    yield
    take(3, 0, 0)
    send(3, 0, 0, "p")
    take(1, 0, 1)
    send(1, 0, 1, "m")
    share(3, 0, 0)
    share(1, 0, 1)
    yield
    for half in (0, 1):
        take(0, 1, half)
        send(0, 1, half, "p")
        send(0, 1, half, "m")
        share(0, 1, half)
    yield
    take(3, 0, 1)
    take(1, 0, 0)
    share(3, 0, 1)
    share(1, 0, 0)
    yield
    take(3, 1, 0)
    send(3, 1, 0, "p")
    take(1, 1, 1)
    send(1, 1, 1, "m")
    share(3, 1, 0)
    share(1, 1, 1)
    yield
    for half in (0, 1):
        take(2, 0, half)
        share(2, 0, half)
    yield
    take(3, 1, 1)
    take(1, 1, 0)
    share(3, 1, 1)
    share(1, 1, 0)
    for half in (0, 1):
        take(2, 1, half)
        share(2, 1, half)
    yield
    if has_sib:
        for ring in (0, 1, 3, 2):
            for pair in (0, 1):
                for half in (0, 1):
                    take(ring, pair, half, 1)


def add_rows(rows, step, body):
    def one(i, carry):
        body(pl.ds(pl.multiple_of(i * step, step), step))
        return carry

    lax.fori_loop(0, rows // step, one, 0)


def scatter_shapes(rows, width):
    return [
        pltpu.VMEM((2, rows // 2, width), BF16),
        pltpu.VMEM((2, rows // 2, width), BF16),
        pltpu.VMEM((2, rows, width), BF16),
        pltpu.VMEM((2, rows, width), BF16),
        pltpu.VMEM((rows, width), BF16),
    ]


def scatter(wire, group, terms, bufs, tag, prepare):
    relay_m, relay_p, from_m, from_p, from_pair = bufs
    rows = terms.shape[1]
    half_rows = rows // 2
    cut = (pl.ds(0, half_rows), pl.ds(half_rows, half_rows))
    step = 128

    def part(ring, pair, half):
        return terms.at[group.slot(ring, pair), cut[half]]

    def add(target, *others):
        def body(at):
            total = target[at].astype(F32)
            for other in others:
                total = total + other[at].astype(F32)
            target[at] = total.astype(BF16)

        add_rows(half_rows, step, body)

    for q in (1, 0):
        prepare(2, q)
        wire.push((tag, "rm", q), part(2, q, 0), relay_m.at[q], group.peers["p"])
        wire.push((tag, "rp", q), part(2, q, 1), relay_p.at[q], group.peers["m"])
    yield
    for q in (1, 0):
        prepare(1, q)
        prepare(3, q)
        wire.push((tag, "m", q, 1), part(1, q, 1), from_m.at[q, cut[1]], group.peers["p"])
        wire.push((tag, "p", q, 0), part(3, q, 0), from_p.at[q, cut[0]], group.peers["m"])
        yield
        wire.take((tag, "rm", q), relay_m.at[q], group.peers["p"])
        add(part(1, q, 0), relay_m.at[q])
        wire.push((tag, "m", q, 0), part(1, q, 0), from_m.at[q, cut[0]], group.peers["p"])
        wire.take((tag, "rp", q), relay_p.at[q], group.peers["p"])
        add(part(3, q, 1), relay_p.at[q])
        wire.push((tag, "p", q, 1), part(3, q, 1), from_p.at[q, cut[1]], group.peers["m"])
    yield
    prepare(0, 1)
    for half in (0, 1):
        wire.take((tag, "m", 1, half), from_m.at[1, cut[half]], group.peers["p"])
        wire.take((tag, "p", 1, half), from_p.at[1, cut[half]], group.peers["p"])
        add(part(0, 1, half), from_m.at[1, cut[half]], from_p.at[1, cut[half]])
        wire.push((tag, "z", half), part(0, 1, half), from_pair.at[cut[half]], group.peers["pair"])
    yield
    prepare(0, 0)
    for half in (0, 1):
        wire.take((tag, "m", 0, half), from_m.at[0, cut[half]], group.peers["p"])
        wire.take((tag, "p", 0, half), from_p.at[0, cut[half]], group.peers["p"])
    for half in (0, 1):
        wire.take((tag, "z", half), from_pair.at[cut[half]], group.peers["p"])


def total_shapes(width):
    return [
        pltpu.VMEM((TOTAL_ROWS, width), F32),
        pltpu.VMEM((TOTAL_ROWS // 2, width), F32),
        pltpu.VMEM((3, TOTAL_ROWS // 8, width), F32),
        pltpu.VMEM((3, TOTAL_ROWS // 32, width), F32),
        pltpu.VMEM((4, TOTAL_ROWS // 32, width), F32),
    ]


def total(wire, place, mine, bufs, tag):
    result, in_core, in_x, in_y, in_z = bufs
    half, quarter, piece = TOTAL_ROWS // 2, TOTAL_ROWS // 8, TOTAL_ROWS // 32

    def span(core, x=None, y=None):
        start, size = core * half, half
        if x is not None:
            start, size = start + x * quarter, quarter
        if y is not None:
            start, size = start + y * piece, piece
        return pl.ds(pl.multiple_of(start, piece), size)

    core, x, y = place.core, place.x, place.y
    z = place.zh * 2 + place.zl
    other = 1 - core
    sib = place.peer(core=1)
    wire.push((tag, "core"), mine.at[span(other)], in_core, sib)
    yield
    wire.take((tag, "core"), in_core, sib)

    def fold(i, carry):
        at = pl.ds(pl.multiple_of(core * half + i * 64, 64), 64)
        mine[at] += in_core[pl.ds(pl.multiple_of(i * 64, 64), 64)]
        return carry

    lax.fori_loop(0, half // 64, fold, 0)
    for d in (1, 2, 3):
        to = place.peer(x=d)
        wire.push((tag, "x", d), mine.at[span(core, lax.rem(x + d, 4))], in_x.at[d - 1], to)
    yield
    for d in (1, 2, 3):
        wire.take((tag, "x", d), in_x.at[d - 1], sib)
    mine[span(core, x)] += in_x[0] + in_x[1] + in_x[2]
    for d in (1, 2, 3):
        to = place.peer(y=d)
        wire.push((tag, "y", d), mine.at[span(core, x, lax.rem(y + d, 4))], in_y.at[d - 1], to)
    yield
    for d in (1, 2, 3):
        wire.take((tag, "y", d), in_y.at[d - 1], sib)
    in_z[z] = mine[span(core, x, y)] + in_y[0] + in_y[1] + in_y[2]
    for d in (1, 2, 3):
        wire.push((tag, "z", d), in_z.at[z], in_z.at[z], place.peer(z=d))
    yield
    for d in (1, 2, 3):
        wire.take((tag, "z", d), in_z.at[lax.rem(z + 4 - d, 4)], sib)
    at = span(core, x, y)
    result[at] = in_z[0] + in_z[1] + in_z[2] + in_z[3]
    for d in (1, 2, 3):
        wire.push((tag, "back y", d), result.at[at], result.at[at], place.peer(y=d))
    yield
    for d in (1, 2, 3):
        wire.take((tag, "back y", d), result.at[span(core, x, lax.rem(y + 4 - d, 4))], sib)
    at = span(core, x)
    for d in (1, 2, 3):
        wire.push((tag, "back x", d), result.at[at], result.at[at], place.peer(x=d))
    yield
    for d in (1, 2, 3):
        wire.take((tag, "back x", d), result.at[span(core, lax.rem(x + 4 - d, 4))], sib)
    wire.push((tag, "back core"), result.at[span(core)], result.at[span(core)], sib)
    yield
    wire.take((tag, "back core"), result.at[span(other)], sib)


def run(steps):
    for _ in steps:
        pass


def dot(a, b, dims=((1,), (0,))):
    return lax.dot_general(a, b, (dims, ((), ())), preferred_element_type=F32)


ANY = pl.BlockSpec(memory_space=pl.ANY)
VM = pl.BlockSpec(memory_space=pltpu.VMEM)


def remote_params(collective_id):
    return pltpu.CompilerParams(
        collective_id=collective_id, has_side_effects=True, vmem_limit_bytes=VMEM_LIMIT
    )


def node_gather_kernel(nodes, out, send, recv, own_sem):
    group = RowGroup(Place())
    greet(list(group.peers.values()))
    own = pltpu.make_async_copy(nodes, out.at[group.slot(0, 0)], own_sem)
    own.start()
    wire = Wire(send, recv)
    run(gather(wire, group, out, "n", nodes))
    wire.drain()
    own.wait()


def node_gather(nodes):
    rows, width = nodes.shape
    return pl.pallas_call(
        node_gather_kernel,
        out_shape=jax.ShapeDtypeStruct((16, rows, width), BF16),
        in_specs=[ANY],
        out_specs=ANY,
        scratch_shapes=[
            pltpu.SemaphoreType.DMA((30,)),
            pltpu.SemaphoreType.DMA((30,)),
            pltpu.SemaphoreType.DMA,
        ],
        compiler_params=remote_params(1),
        name="node_gather",
    )(nodes)


def forward_kernel(cols, count, tiles, nodes, out):
    step = pl.program_id(0)
    per = tiles.shape[0]
    for i in range(per):
        at = step * per + i
        live = count[at]
        base = pl.ds(i * 128, 128)

        @pl.when(live <= 2)
        def _():
            pair = jnp.concatenate(
                [jnp.where(k < live, tiles[i, k], jnp.zeros((), BF16)) for k in (0, 1)], axis=1
            )
            picked = jnp.concatenate([nodes[cols[at, k]] for k in (0, 1)], axis=0)
            out[base] = dot(pair, picked).astype(BF16)

        @pl.when(live > 2)
        def _():
            four = jnp.concatenate(
                [jnp.where(k < live, tiles[i, k], jnp.zeros((), BF16)) for k in range(4)], axis=1
            )
            picked = jnp.concatenate([nodes[cols[at, k]] for k in range(4)], axis=0)
            out[base] = dot(four, picked).astype(BF16)


def forward(cols, count, tiles, nodes):
    row_blocks = tiles.shape[0]
    width = nodes.shape[-1]
    per = 8
    return pl.pallas_call(
        forward_kernel,
        out_shape=jax.ShapeDtypeStruct((row_blocks * 128, width), BF16),
        grid_spec=pltpu.PrefetchScalarGridSpec(
            num_scalar_prefetch=2,
            grid=(row_blocks // per,),
            in_specs=[
                pl.BlockSpec((per, 4, 128, 128), lambda s, *_: (s, 0, 0, 0)),
                pl.BlockSpec(nodes.shape, lambda s, *_: (0, 0, 0)),
            ],
            out_specs=pl.BlockSpec((per * 128, width), lambda s, *_: (s, 0)),
        ),
        compiler_params=pltpu.CompilerParams(vmem_limit_bytes=VMEM_LIMIT),
        name="forward",
    )(cols, count, tiles, nodes)


def middle_kernel(
    partial, nodes, cot, w_in, bias, w_out, gain, shift,
    grads, updated, direct, weights,
    terms, relay_m, relay_p, from_m, from_p, from_pair,
    msg_s, act_s, gproj_s, gpre_s, send, recv, load,
):
    group = ColGroup(Place())
    width = nodes.shape[1]
    rows = nodes.shape[0]

    def loader(ring, pair):
        slot = group.slot(ring, pair)
        return pltpu.make_async_copy(partial.at[slot], terms.at[slot], load.at[ring * 2 + pair])

    for ring in (2, 1, 3, 0):
        for pair in (1, 0):
            loader(ring, pair).start()
    greet(list(group.peers.values()))
    wire = Wire(send, recv)
    bufs = (relay_m, relay_p, from_m, from_p, from_pair)
    run(scatter(wire, group, terms, bufs, "s", lambda ring, pair: loader(ring, pair).wait()))
    own = group.slot(0, 0)
    gvec = weights.at[pl.ds(3 * width, 8)]
    weights[3 * width :] = jnp.zeros((weights.shape[0] - 3 * width, width), F32)

    def chunk(i, carry):
        at = pl.ds(pl.multiple_of(i * 256, 256), 256)
        msg = (
            terms[own, at].astype(F32)
            + from_m[0, at].astype(F32)
            + from_p[0, at].astype(F32)
            + from_pair[at].astype(F32)
        ).astype(BF16)
        msg_s[at] = msg
        mine = nodes[at]
        pre = dot(mine, w_in[:width]) + dot(msg, w_in[width:]) + bias[...]
        sig = jax.nn.sigmoid(pre)
        act = (pre * sig).astype(BF16)
        act_s[at] = act
        proj = dot(act, w_out[...])
        mean = jnp.mean(proj, axis=-1, keepdims=True)
        off = proj - mean
        var = jnp.mean(off * off, axis=-1, keepdims=True)
        rstd = 1.0 / jnp.sqrt(var + EPS)
        normed = off * rstd
        updated[at] = (mine.astype(F32) + normed * gain[...] + shift[...]).astype(BF16)
        grad_out = cot[at].astype(F32)
        gscaled = grad_out * gain[...]
        gproj = (
            (
                gscaled
                - jnp.mean(gscaled, axis=-1, keepdims=True)
                - normed * jnp.mean(gscaled * normed, axis=-1, keepdims=True)
            )
            * rstd
        ).astype(BF16)
        gproj_s[at] = gproj
        gact = dot(gproj, w_out[...], ((1,), (1,)))
        gpre = gact * sig * (1.0 + pre * (1.0 - sig))
        gpre_b = gpre.astype(BF16)
        gpre_s[at] = gpre_b
        grads[own, at] = dot(gpre_b, w_in[width:], ((1,), (1,))).astype(BF16)
        direct[at] = grad_out + dot(gpre_b, w_in[:width], ((1,), (1,)))
        gvec[0:1] += jnp.sum(gpre, axis=0, keepdims=True)
        gvec[1:2] += jnp.sum(grad_out * normed, axis=0, keepdims=True)
        gvec[2:3] += jnp.sum(grad_out, axis=0, keepdims=True)
        return carry

    lax.fori_loop(0, rows // 256, chunk, 0)
    steps = gather(wire, group, grads, "g")
    next(steps)
    weights[:width] = dot(nodes[...], gpre_s[...], ((0,), (0,)))
    weights[width : 2 * width] = dot(msg_s[...], gpre_s[...], ((0,), (0,)))
    weights[2 * width : 3 * width] = dot(act_s[...], gproj_s[...], ((0,), (0,)))
    run(steps)
    wire.drain()


def middle(partial, nodes, cot, w_in, bias, w_out, gain, shift):
    rows, width = nodes.shape
    one = functools.partial(pltpu.VMEM, (rows, width))
    return pl.pallas_call(
        middle_kernel,
        out_shape=[
            jax.ShapeDtypeStruct((8, rows, width), BF16),
            jax.ShapeDtypeStruct((rows, width), BF16),
            jax.ShapeDtypeStruct((rows, width), F32),
            jax.ShapeDtypeStruct((TOTAL_ROWS, width), F32),
        ],
        in_specs=[ANY] + [VM] * 7,
        out_specs=[VM] * 4,
        scratch_shapes=[pltpu.VMEM((8, rows, width), BF16)]
        + scatter_shapes(rows, width)
        + [one(BF16)] * 4
        + [
            pltpu.SemaphoreType.DMA((40,)),
            pltpu.SemaphoreType.DMA((40,)),
            pltpu.SemaphoreType.DMA((8,)),
        ],
        compiler_params=remote_params(2),
        name="middle",
    )(partial.reshape(8, rows, width), nodes, cot, w_in, bias, w_out, gain, shift)


def backward_kernel(cols, count, tiles, nodes, grads, tile_grads, back, acc):
    step = pl.program_id(0)
    per = tiles.shape[0]

    @pl.when(step == 0)
    def _():
        def clear(i, carry):
            acc[i] = jnp.zeros(acc.shape[1:], F32)
            return carry

        lax.fori_loop(0, acc.shape[0], clear, 0)

    scale = F32(256.0) ** F32(-0.5)
    for i in range(per):
        at = step * per + i
        live = count[at]
        base = pl.ds(i * 128, 128)
        for k in range(4):
            @pl.when(k < live)
            def _():
                col = cols[at, k]
                grad = grads[base]
                tile_grads[i, k] = (dot(grad, nodes[col], ((1,), (1,))) * scale).astype(BF16)
                acc[col] += dot(tiles[i, k], grad, ((0,), (0,)))

            @pl.when(k >= live)
            def _():
                tile_grads[i, k] = jnp.zeros((128, 128), BF16)

    @pl.when(step == pl.num_programs(0) - 1)
    def _():
        def put(i, carry):
            back[i] = acc[i].astype(BF16)
            return carry

        lax.fori_loop(0, acc.shape[0], put, 0)


def backward(cols, count, tiles, nodes, grads):
    row_blocks = tiles.shape[0]
    blocks, _, width = nodes.shape
    per = 8
    return pl.pallas_call(
        backward_kernel,
        out_shape=[
            jax.ShapeDtypeStruct(tiles.shape, BF16),
            jax.ShapeDtypeStruct(nodes.shape, BF16),
        ],
        grid_spec=pltpu.PrefetchScalarGridSpec(
            num_scalar_prefetch=2,
            grid=(row_blocks // per,),
            in_specs=[
                pl.BlockSpec((per, 4, 128, 128), lambda s, *_: (s, 0, 0, 0)),
                pl.BlockSpec(nodes.shape, lambda s, *_: (0, 0, 0), pipeline_mode=pl.Buffered(1)),
                pl.BlockSpec((per * 128, width), lambda s, *_: (s, 0)),
            ],
            out_specs=[
                pl.BlockSpec((per, 4, 128, 128), lambda s, *_: (s, 0, 0, 0)),
                pl.BlockSpec(nodes.shape, lambda s, *_: (0, 0, 0), pipeline_mode=pl.Buffered(1)),
            ],
            scratch_shapes=[pltpu.VMEM(nodes.shape, F32)],
        ),
        compiler_params=pltpu.CompilerParams(vmem_limit_bytes=VMEM_LIMIT),
        name="backward",
    )(cols, count, tiles, nodes, grads)


def finish_kernel(
    back, direct, weights, out, gw_in, gw_out, gvec,
    terms, others, relay_m, relay_p, from_m, from_p, from_pair,
    mine, result, in_core, in_x, in_y, in_z, send, recv, load,
):
    place = Place()
    group = RowGroup(place)
    rows = terms.shape[1]
    order = [(2, 1), (2, 0), (1, 1), (3, 1), (1, 0), (3, 0), (0, 1), (0, 0)]

    def loader(ring, pair):
        slot = group.slot(ring, pair)
        return pltpu.make_async_copy(back.at[slot], terms.at[slot], load.at[ring * 2 + pair])

    whole = pltpu.make_async_copy(weights, mine, load.at[8])
    whole.start()
    for at in order:
        loader(*at).start()
    greet(place.all_peers())
    wire = Wire(send, recv)
    whole.wait()
    sums = total(wire, place, mine, (result, in_core, in_x, in_y, in_z), "w")
    next(sums)
    for ring, pair in order:
        wire.push(
            ("f", ring, pair),
            back.at[group.slot(ring, pair, 1)],
            others.at[ring * 2 + pair],
            group.peers["sib"],
        )

    def prepare(ring, pair):
        loader(ring, pair).wait()
        other = others.at[ring * 2 + pair]
        wire.take(("f", ring, pair), other, group.peers["sib"])
        slot = group.slot(ring, pair)

        def body(at):
            terms[slot, at] = (terms[slot, at].astype(F32) + other[at].astype(F32)).astype(BF16)

        add_rows(rows, 128, body)

    bufs = (relay_m, relay_p, from_m, from_p, from_pair)
    for _ in scatter(wire, group, terms, bufs, "b", prepare):
        next(sums, None)
    own = group.slot(0, 0)

    def last(at):
        out[at] = (
            direct[at]
            + terms[own, at].astype(F32)
            + from_m[0, at].astype(F32)
            + from_p[0, at].astype(F32)
            + from_pair[at].astype(F32)
        ).astype(BF16)

    add_rows(rows, 128, last)
    run(sums)
    width = out.shape[1]
    factor = F32(131072.0) ** F32(-0.5)
    gw_in[...] = result[: 2 * width] * factor
    gw_out[...] = result[2 * width : 3 * width] * factor
    gvec[...] = result[3 * width : 3 * width + 3] * factor
    wire.drain()


def finish(back, direct, weights):
    rows, width = direct.shape
    return pl.pallas_call(
        finish_kernel,
        out_shape=[
            jax.ShapeDtypeStruct((rows, width), BF16),
            jax.ShapeDtypeStruct((2 * width, width), F32),
            jax.ShapeDtypeStruct((width, width), F32),
            jax.ShapeDtypeStruct((3, width), F32),
        ],
        in_specs=[ANY, VM, ANY],
        out_specs=[VM] * 4,
        scratch_shapes=[
            pltpu.VMEM((16, rows, width), BF16),
            pltpu.VMEM((8, rows, width), BF16),
        ]
        + scatter_shapes(rows, width)
        + [pltpu.VMEM((TOTAL_ROWS, width), F32)]
        + total_shapes(width)
        + [
            pltpu.SemaphoreType.DMA((60,)),
            pltpu.SemaphoreType.DMA((60,)),
            pltpu.SemaphoreType.DMA((9,)),
        ],
        compiler_params=remote_params(3),
        name="finish",
    )(back.reshape(16, rows, width), direct, weights)


def body(nodes, tiles, tile_col, tile_count, w_in, bias_in, w_out, ln_gain, ln_shift, cotangent):
    rows, width = nodes.shape
    cols, count = tile_col[:, 0], tile_count[:, 0]
    slots = tiles[:, 0]
    cols = jnp.clip(cols, 0, 127)
    gathered = node_gather(nodes).reshape(128, 128, width)
    partial = forward(cols, count, slots, gathered)
    grads, updated, direct, weights = middle(
        partial, nodes, cotangent, w_in, bias_in[None], w_out, ln_gain[None], ln_shift[None]
    )
    grad_tiles, back = backward(cols, count, slots, gathered, grads.reshape(8 * rows, width))
    grad_nodes, gw_in, gw_out, gvec = finish(back, direct, weights)
    return updated, grad_nodes, grad_tiles[:, None], gw_in, gw_out, gvec


def solution(mesh):
    placed = (
        P(("row", "col"), None),
        P("row", "col", None, None, None),
        P("row", "col", None),
        P("row", "col"),
        P(),
        P(),
        P(),
        P(),
        P(),
        P(("row", "col"), None),
    )
    return jax.shard_map(
        body,
        mesh=mesh,
        in_specs=placed,
        out_specs=(
            P(("row", "col"), None),
            P(("row", "col"), None),
            P("row", "col", None, None, None),
            P(),
            P(),
            P(),
        ),
        check_vma=False,
    )
```

```python
import functools

import jax
import jax.numpy as jnp
from jax import lax
from jax.experimental import pallas as pl
from jax.experimental.pallas import tpu as pltpu
from jax.sharding import PartitionSpec as P

F32, BF16 = jnp.float32, jnp.bfloat16
MIB = 1024 * 1024
VMEM_LIMIT = 56 * MIB
EPS = 1e-05
TOTAL_ROWS = 1024


class Place:
    def __init__(self):
        self.row = lax.axis_index("row")
        self.col = lax.axis_index("col")
        self.x = lax.div(self.row, 4)
        self.zh = lax.rem(lax.div(self.row, 2), 2)
        self.core = lax.rem(self.row, 2)
        self.y = lax.div(self.col, 2)
        self.zl = lax.rem(self.col, 2)


    def peer(self, x=0, y=0, z=0, core=0):
        z_at = lax.rem(self.zh * 2 + self.zl + z, 4)
        row = lax.rem(self.x + x, 4) * 4 + lax.div(z_at, 2) * 2 + lax.rem(self.core + core, 2)
        return (row, lax.rem(self.y + y, 4) * 2 + lax.rem(z_at, 2))

    def all_peers(self):
        steps = [dict(core=1)] + [{axis: d} for axis in "xyz" for d in (1, 2, 3)]
        return [self.peer(**step) for step in steps]


class RowGroup:
    def __init__(self, place):
        self.place = place
        col = place.col
        self.peers = {
            "p": (self.slot(1, 0), col),
            "m": (self.slot(3, 0), col),
            "pair": (self.slot(0, 1), col),
            "sib": (self.slot(0, 0, 1), col),
        }

    def slot(self, ring, pair, sib=0):
        at = self.place
        return (
            lax.rem(at.x + ring, 4) * 4
            + lax.rem(at.zh + pair, 2) * 2
            + lax.rem(at.core + sib, 2)
        )


class ColGroup:
    def __init__(self, place):
        self.place = place
        row = place.row
        self.peers = {
            "p": (row, self.slot(1, 0)),
            "m": (row, self.slot(3, 0)),
            "pair": (row, self.slot(0, 1)),
        }

    def slot(self, ring, pair):
        at = self.place
        return lax.rem(at.y + ring, 4) * 2 + lax.rem(at.zl + pair, 2)


class Wire:
    def __init__(self, send, recv):
        self.send, self.recv = send, recv
        self.names = {}
        self.open = []

    def index(self, name):
        return self.names.setdefault(name, len(self.names))

    def push(self, name, src, dst, to):
        at = self.index(name)
        copy = pltpu.make_async_remote_copy(
            src_ref=src,
            dst_ref=dst,
            send_sem=self.send.at[at],
            recv_sem=self.recv.at[at],
            device_id=to,
            device_id_type=pl.DeviceIdType.MESH,
        )
        copy.start()
        self.open.append(copy)

    def take(self, name, dst, to):
        at = self.index(name)
        pltpu.make_async_remote_copy(
            src_ref=dst,
            dst_ref=dst,
            send_sem=self.send.at[at],
            recv_sem=self.recv.at[at],
            device_id=to,
            device_id_type=pl.DeviceIdType.MESH,
        ).wait_recv()

    def drain(self):
        for copy in self.open:
            copy.wait_send()
        self.open = []


def greet(devices):
    barrier = pltpu.get_barrier_semaphore()
    for device in devices:
        pl.semaphore_signal(barrier, inc=1, device_id=device, device_id_type=pl.DeviceIdType.MESH)
    pl.semaphore_wait(barrier, len(devices))


MOVES = {"p": (3, 0, 0), "m": (1, 0, 0), "pair": (0, 1, 0), "sib": (0, 0, 1)}


def gather(wire, group, buf, tag, per=1):
    half_rows = buf.shape[1] // 2

    def view(slot, half):
        if per == 1:
            return buf.at[slot, pl.ds(half * half_rows, half_rows)]
        return buf.at[pl.ds(slot * per + half * (per // 2), per // 2)]

    has_sib = "sib" in group.peers

    def send(ring, pair, half, way):
        ref = view(group.slot(ring, pair), half)
        dr, dp, dk = MOVES[way]
        name = (tag, (ring + dr) % 4, (pair + dp) % 2, dk, half)
        wire.push(name, ref, ref, group.peers[way])

    def take(ring, pair, half, sib=0):
        slot = group.slot(ring, pair, 1) if sib else group.slot(ring, pair)
        wire.take((tag, ring, pair, sib, half), view(slot, half), group.peers["p"])

    def share(ring, pair, half):
        if has_sib:
            send(ring, pair, half, "sib")

    send(0, 0, 0, "p")
    send(0, 0, 1, "m")
    send(0, 0, 0, "pair")
    send(0, 0, 1, "p")
    send(0, 0, 0, "m")
    send(0, 0, 1, "pair")
    for half in (0, 1):
        share(0, 0, half)
    yield
    take(3, 0, 0)
    send(3, 0, 0, "p")
    take(1, 0, 1)
    send(1, 0, 1, "m")
    share(3, 0, 0)
    share(1, 0, 1)
    yield
    for half in (0, 1):
        take(0, 1, half)
        send(0, 1, half, "p")
        send(0, 1, half, "m")
        share(0, 1, half)
    yield
    take(3, 0, 1)
    take(1, 0, 0)
    share(3, 0, 1)
    share(1, 0, 0)
    yield
    take(3, 1, 0)
    send(3, 1, 0, "p")
    take(1, 1, 1)
    send(1, 1, 1, "m")
    share(3, 1, 0)
    share(1, 1, 1)
    yield
    for half in (0, 1):
        take(2, 0, half)
        share(2, 0, half)
    yield
    take(3, 1, 1)
    take(1, 1, 0)
    share(3, 1, 1)
    share(1, 1, 0)
    for half in (0, 1):
        take(2, 1, half)
        share(2, 1, half)
    yield
    if has_sib:
        for ring in (0, 1, 3, 2):
            for pair in (0, 1):
                for half in (0, 1):
                    take(ring, pair, half, 1)


def add_rows(rows, step, body):
    def one(i, carry):
        body(pl.ds(pl.multiple_of(i * step, step), step))
        return carry

    lax.fori_loop(0, rows // step, one, 0)


def scatter_shapes(rows, width):
    return [
        pltpu.VMEM((2, rows // 2, width), BF16),
        pltpu.VMEM((2, rows // 2, width), BF16),
        pltpu.VMEM((2, rows, width), BF16),
        pltpu.VMEM((2, rows, width), BF16),
        pltpu.VMEM((rows, width), BF16),
    ]


def scatter(wire, group, terms, bufs, tag, prepare):
    relay_m, relay_p, from_m, from_p, from_pair = bufs
    rows = terms.shape[1]
    half_rows = rows // 2
    cut = (pl.ds(0, half_rows), pl.ds(half_rows, half_rows))
    step = 128

    def part(ring, pair, half):
        return terms.at[group.slot(ring, pair), cut[half]]

    def add(target, *others):
        def body(at):
            total = target[at].astype(F32)
            for other in others:
                total = total + other[at].astype(F32)
            target[at] = total.astype(BF16)

        add_rows(half_rows, step, body)

    for q in (1, 0):
        prepare(2, q)
        wire.push((tag, "rm", q), part(2, q, 0), relay_m.at[q], group.peers["p"])
        wire.push((tag, "rp", q), part(2, q, 1), relay_p.at[q], group.peers["m"])
    yield
    for q in (1, 0):
        prepare(1, q)
        prepare(3, q)
        wire.push((tag, "m", q, 1), part(1, q, 1), from_m.at[q, cut[1]], group.peers["p"])
        wire.push((tag, "p", q, 0), part(3, q, 0), from_p.at[q, cut[0]], group.peers["m"])
        yield
        wire.take((tag, "rm", q), relay_m.at[q], group.peers["p"])
        add(part(1, q, 0), relay_m.at[q])
        wire.push((tag, "m", q, 0), part(1, q, 0), from_m.at[q, cut[0]], group.peers["p"])
        wire.take((tag, "rp", q), relay_p.at[q], group.peers["p"])
        add(part(3, q, 1), relay_p.at[q])
        wire.push((tag, "p", q, 1), part(3, q, 1), from_p.at[q, cut[1]], group.peers["m"])
    yield
    prepare(0, 1)
    for half in (0, 1):
        wire.take((tag, "m", 1, half), from_m.at[1, cut[half]], group.peers["p"])
        wire.take((tag, "p", 1, half), from_p.at[1, cut[half]], group.peers["p"])
        add(part(0, 1, half), from_m.at[1, cut[half]], from_p.at[1, cut[half]])
        wire.push((tag, "z", half), part(0, 1, half), from_pair.at[cut[half]], group.peers["pair"])
    yield
    prepare(0, 0)
    for half in (0, 1):
        wire.take((tag, "m", 0, half), from_m.at[0, cut[half]], group.peers["p"])
        wire.take((tag, "p", 0, half), from_p.at[0, cut[half]], group.peers["p"])
    for half in (0, 1):
        wire.take((tag, "z", half), from_pair.at[cut[half]], group.peers["p"])


def total_shapes(width):
    return [
        pltpu.VMEM((TOTAL_ROWS, width), F32),
        pltpu.VMEM((TOTAL_ROWS // 2, width), F32),
        pltpu.VMEM((3, TOTAL_ROWS // 8, width), F32),
        pltpu.VMEM((3, TOTAL_ROWS // 32, width), F32),
        pltpu.VMEM((4, TOTAL_ROWS // 32, width), F32),
    ]


def total(wire, place, mine, bufs, tag):
    result, in_core, in_x, in_y, in_z = bufs
    half, quarter, piece = TOTAL_ROWS // 2, TOTAL_ROWS // 8, TOTAL_ROWS // 32

    def span(core, x=None, y=None):
        start, size = core * half, half
        if x is not None:
            start, size = start + x * quarter, quarter
        if y is not None:
            start, size = start + y * piece, piece
        return pl.ds(pl.multiple_of(start, piece), size)

    core, x, y = place.core, place.x, place.y
    z = place.zh * 2 + place.zl
    other = 1 - core
    sib = place.peer(core=1)
    wire.push((tag, "core"), mine.at[span(other)], in_core, sib)
    yield
    wire.take((tag, "core"), in_core, sib)

    def fold(i, carry):
        at = pl.ds(pl.multiple_of(core * half + i * 64, 64), 64)
        mine[at] += in_core[pl.ds(pl.multiple_of(i * 64, 64), 64)]
        return carry

    lax.fori_loop(0, half // 64, fold, 0)
    for d in (1, 2, 3):
        to = place.peer(x=d)
        wire.push((tag, "x", d), mine.at[span(core, lax.rem(x + d, 4))], in_x.at[d - 1], to)
    yield
    for d in (1, 2, 3):
        wire.take((tag, "x", d), in_x.at[d - 1], sib)
    mine[span(core, x)] += in_x[0] + in_x[1] + in_x[2]
    for d in (1, 2, 3):
        to = place.peer(y=d)
        wire.push((tag, "y", d), mine.at[span(core, x, lax.rem(y + d, 4))], in_y.at[d - 1], to)
    yield
    for d in (1, 2, 3):
        wire.take((tag, "y", d), in_y.at[d - 1], sib)
    in_z[z] = mine[span(core, x, y)] + in_y[0] + in_y[1] + in_y[2]
    for d in (1, 2, 3):
        wire.push((tag, "z", d), in_z.at[z], in_z.at[z], place.peer(z=d))
    yield
    for d in (1, 2, 3):
        wire.take((tag, "z", d), in_z.at[lax.rem(z + 4 - d, 4)], sib)
    at = span(core, x, y)
    result[at] = in_z[0] + in_z[1] + in_z[2] + in_z[3]
    for d in (1, 2, 3):
        wire.push((tag, "back y", d), result.at[at], result.at[at], place.peer(y=d))
    yield
    for d in (1, 2, 3):
        wire.take((tag, "back y", d), result.at[span(core, x, lax.rem(y + 4 - d, 4))], sib)
    at = span(core, x)
    for d in (1, 2, 3):
        wire.push((tag, "back x", d), result.at[at], result.at[at], place.peer(x=d))
    yield
    for d in (1, 2, 3):
        wire.take((tag, "back x", d), result.at[span(core, lax.rem(x + 4 - d, 4))], sib)
    wire.push((tag, "back core"), result.at[span(core)], result.at[span(core)], sib)
    yield
    wire.take((tag, "back core"), result.at[span(other)], sib)


def run(steps):
    for _ in steps:
        pass


def dot(a, b, dims=((1,), (0,))):
    return lax.dot_general(a, b, (dims, ((), ())), preferred_element_type=F32)


ANY = pl.BlockSpec(memory_space=pl.ANY)
VM = pl.BlockSpec(memory_space=pltpu.VMEM)


def remote_params(collective_id):
    return pltpu.CompilerParams(
        collective_id=collective_id, has_side_effects=True, vmem_limit_bytes=VMEM_LIMIT
    )


ORDER = [(2, 1), (2, 0), (1, 1), (3, 1), (1, 0), (3, 0), (0, 1), (0, 0)]


def middle_kernel(
    cols, live, tiles, nodes_any, nodes, cot, w_in, bias, w_out, gain, shift,
    near0, near1, grads, updated, direct, gw_in, gw_out, gvec,
    slots, terms0, terms1, *rest,
):
    bufs0, bufs1, rest = rest[:5], rest[5:10], rest[10:]
    msg_s, act_s, gproj_s, gpre_s, weights = rest[:5]
    sum_bufs, (send, recv, load) = rest[5:10], rest[10:]
    place = Place()
    across, along = RowGroup(place), ColGroup(place)
    width = nodes.shape[1]
    rows = nodes.shape[0]
    near, terms = (near0, near1), (terms0, terms1)

    mine = [
        pltpu.make_async_copy(
            nodes_any.at[:, :, pl.ds(h * 128, 128)],
            near[h].at[pl.ds(across.slot(0, 0) * 8, 8)],
            load.at[8 + h],
        )
        for h in (0, 1)
    ]
    for copy in mine:
        copy.start()

    def loader(ring, pair):
        at = pl.ds(along.slot(ring, pair) * 8, 8)
        return pltpu.make_async_copy(tiles.at[at], slots.at[at], load.at[ring * 2 + pair])

    for at in ORDER:
        loader(*at).start()
    greet(place.all_peers())
    wire = Wire(send, recv)
    for copy in mine:
        copy.wait()

    def mask(ring, pair):
        loader(ring, pair).wait()
        base = along.slot(ring, pair) * 8

        def one(i, carry):
            for k in range(4):
                keep = live[base + i, pl.ds(k, 1)].astype(BF16)
                slots[base + i, k] = slots[base + i, k] * keep
            return carry

        lax.fori_loop(0, 8, one, 0)

    def product(h, ring, pair):
        slot = along.slot(ring, pair)

        def one(j, carry):
            for u in range(2):
                i = slot * 8 + j * 2 + u
                left = jnp.concatenate([slots[i, k] for k in range(4)], axis=1)
                right = []
                for k in range(4):
                    right.append(near[h][cols[i, k]])
                at = pl.ds(pl.multiple_of((j * 2 + u) * 128, 128), 128)
                terms[h][slot, at] = dot(left, jnp.concatenate(right, axis=0)).astype(BF16)
            return carry

        lax.fori_loop(0, 4, one, 0)

    gather0 = gather(wire, across, near0, "n0", 8)
    gather1 = gather(wire, across, near1, "n1", 8)
    for step in range(5):
        next(gather0)
        for at in ORDER[2 * step : 2 * step + 2]:
            mask(*at)
    next(gather1)
    run(gather0)

    def prepare0(ring, pair):
        product(0, ring, pair)
        next(gather1, None)

    scatter0 = scatter(wire, along, terms0, bufs0, "s0", prepare0)
    for _ in range(4):
        next(scatter0)
    run(gather1)
    scatter1 = scatter(wire, along, terms1, bufs1, "s1", lambda *at: product(1, *at))
    for _ in scatter1:
        next(scatter0, None)
    run(scatter0)
    own = along.slot(0, 0)
    gsum = weights.at[pl.ds(3 * width, 8)]
    weights[3 * width :] = jnp.zeros((weights.shape[0] - 3 * width, width), F32)

    def chunk(i, carry):
        at = pl.ds(pl.multiple_of(i * 256, 256), 256)
        msg = jnp.concatenate(
            [
                (
                    terms[h][own, at].astype(F32)
                    + bufs[2][0, at].astype(F32)
                    + bufs[3][0, at].astype(F32)
                    + bufs[4][at].astype(F32)
                ).astype(BF16)
                for h, bufs in ((0, bufs0), (1, bufs1))
            ],
            axis=1,
        )
        msg_s[at] = msg
        mine = nodes[at]
        pre = dot(mine, w_in[:width]) + dot(msg, w_in[width:]) + bias[...]
        sig = jax.nn.sigmoid(pre)
        act = (pre * sig).astype(BF16)
        act_s[at] = act
        proj = dot(act, w_out[...])
        mean = jnp.mean(proj, axis=-1, keepdims=True)
        off = proj - mean
        var = jnp.mean(off * off, axis=-1, keepdims=True)
        rstd = 1.0 / jnp.sqrt(var + EPS)
        normed = off * rstd
        updated[at] = (mine.astype(F32) + normed * gain[...] + shift[...]).astype(BF16)
        grad_out = cot[at].astype(F32)
        gscaled = grad_out * gain[...]
        gproj = (
            (
                gscaled
                - jnp.mean(gscaled, axis=-1, keepdims=True)
                - normed * jnp.mean(gscaled * normed, axis=-1, keepdims=True)
            )
            * rstd
        ).astype(BF16)
        gproj_s[at] = gproj
        gact = dot(gproj, w_out[...], ((1,), (1,)))
        gpre = gact * sig * (1.0 + pre * (1.0 - sig))
        gpre_b = gpre.astype(BF16)
        gpre_s[at] = gpre_b
        grads[own, at] = dot(gpre_b, w_in[width:], ((1,), (1,))).astype(BF16)
        direct[at] = grad_out + dot(gpre_b, w_in[:width], ((1,), (1,)))
        gsum[0:1] += jnp.sum(gpre, axis=0, keepdims=True)
        gsum[1:2] += jnp.sum(grad_out * normed, axis=0, keepdims=True)
        gsum[2:3] += jnp.sum(grad_out, axis=0, keepdims=True)
        return carry

    lax.fori_loop(0, rows // 256, chunk, 0)
    steps = gather(wire, along, grads, "g")
    next(steps)
    weights[:width] = dot(nodes[...], gpre_s[...], ((0,), (0,)))
    weights[width : 2 * width] = dot(msg_s[...], gpre_s[...], ((0,), (0,)))
    weights[2 * width : 3 * width] = dot(act_s[...], gproj_s[...], ((0,), (0,)))
    sums = total(wire, place, weights, sum_bufs, "w")
    next(sums)
    for _ in steps:
        next(sums, None)
    run(sums)
    result = sum_bufs[0]
    factor = F32(131072.0) ** F32(-0.5)
    gw_in[...] = result[: 2 * width] * factor
    gw_out[...] = result[2 * width : 3 * width] * factor
    gvec[...] = result[3 * width : 3 * width + 3] * factor
    wire.drain()


def middle(cols, live, tiles, nodes, cot, w_in, bias, w_out, gain, shift):
    rows, width = nodes.shape
    one = functools.partial(pltpu.VMEM, (rows, width))
    smem = pl.BlockSpec(memory_space=pltpu.SMEM)
    near = jax.ShapeDtypeStruct((128, 128, 128), BF16)
    return pl.pallas_call(
        middle_kernel,
        out_shape=[
            near,
            near,
            jax.ShapeDtypeStruct((8, rows, width), BF16),
            jax.ShapeDtypeStruct((rows, width), BF16),
            jax.ShapeDtypeStruct((rows, width), F32),
            jax.ShapeDtypeStruct((2 * width, width), F32),
            jax.ShapeDtypeStruct((width, width), F32),
            jax.ShapeDtypeStruct((3, width), F32),
        ],
        in_specs=[smem, VM, ANY, ANY] + [VM] * 7,
        out_specs=[VM] * 8,
        scratch_shapes=[pltpu.VMEM(tiles.shape, BF16)]
        + [pltpu.VMEM((8, rows, 128), BF16)] * 2
        + scatter_shapes(rows, 128) * 2
        + [one(BF16)] * 4
        + [pltpu.VMEM((TOTAL_ROWS, width), F32)]
        + total_shapes(width)
        + [
            pltpu.SemaphoreType.DMA((140,)),
            pltpu.SemaphoreType.DMA((140,)),
            pltpu.SemaphoreType.DMA((10,)),
        ],
        compiler_params=remote_params(2),
        name="middle",
    )(cols, live, tiles, nodes.reshape(8, 128, width), nodes, cot, w_in, bias, w_out, gain, shift)


def backward_kernel(cols, count, tiles, near0, near1, grads, tile_grads, back, acc):
    step = pl.program_id(0)
    per = tiles.shape[0]

    @pl.when(step == 0)
    def _():
        def clear(i, carry):
            acc[i] = jnp.zeros(acc.shape[1:], F32)
            return carry

        lax.fori_loop(0, acc.shape[0], clear, 0)

    scale = F32(256.0) ** F32(-0.5)
    for i in range(per):
        at = step * per + i
        live = count[at]
        base = pl.ds(i * 128, 128)
        for k in range(4):
            @pl.when(k < live)
            def _():
                col = cols[at, k]
                grad = grads[base]
                picked = jnp.concatenate([near0[col], near1[col]], axis=1)
                tile_grads[i, k] = (dot(grad, picked, ((1,), (1,))) * scale).astype(BF16)
                acc[col] += dot(tiles[i, k], grad, ((0,), (0,)))

            @pl.when(k >= live)
            def _():
                tile_grads[i, k] = jnp.zeros((128, 128), BF16)

    @pl.when(step == pl.num_programs(0) - 1)
    def _():
        def put(i, carry):
            back[i] = acc[i].astype(BF16)
            return carry

        lax.fori_loop(0, acc.shape[0], put, 0)


def backward(cols, count, tiles, near0, near1, grads):
    row_blocks = tiles.shape[0]
    width = grads.shape[1]
    columns = (128, 128, width)
    near = pl.BlockSpec(near0.shape, lambda s, *_: (0, 0, 0), pipeline_mode=pl.Buffered(1))
    per = 8
    return pl.pallas_call(
        backward_kernel,
        out_shape=[
            jax.ShapeDtypeStruct(tiles.shape, BF16),
            jax.ShapeDtypeStruct(columns, BF16),
        ],
        grid_spec=pltpu.PrefetchScalarGridSpec(
            num_scalar_prefetch=2,
            grid=(row_blocks // per,),
            in_specs=[
                pl.BlockSpec((per, 4, 128, 128), lambda s, *_: (s, 0, 0, 0)),
                near,
                near,
                pl.BlockSpec((per * 128, width), lambda s, *_: (s, 0)),
            ],
            out_specs=[
                pl.BlockSpec((per, 4, 128, 128), lambda s, *_: (s, 0, 0, 0)),
                pl.BlockSpec(columns, lambda s, *_: (0, 0, 0), pipeline_mode=pl.Buffered(1)),
            ],
            scratch_shapes=[pltpu.VMEM(columns, F32)],
        ),
        compiler_params=pltpu.CompilerParams(vmem_limit_bytes=VMEM_LIMIT),
        name="backward",
    )(cols, count, tiles, near0, near1, grads)


def finish_kernel(
    back, direct, out,
    terms, others, relay_m, relay_p, from_m, from_p, from_pair, send, recv, load,
):
    group = RowGroup(Place())
    rows = terms.shape[1]

    def loader(ring, pair):
        slot = group.slot(ring, pair)
        return pltpu.make_async_copy(back.at[slot], terms.at[slot], load.at[ring * 2 + pair])

    for at in ORDER:
        loader(*at).start()
    greet(list(group.peers.values()))
    wire = Wire(send, recv)
    for ring, pair in ORDER:
        wire.push(
            ("f", ring, pair),
            back.at[group.slot(ring, pair, 1)],
            others.at[ring * 2 + pair],
            group.peers["sib"],
        )

    def prepare(ring, pair):
        loader(ring, pair).wait()
        other = others.at[ring * 2 + pair]
        wire.take(("f", ring, pair), other, group.peers["sib"])
        slot = group.slot(ring, pair)

        def body(at):
            terms[slot, at] = (terms[slot, at].astype(F32) + other[at].astype(F32)).astype(BF16)

        add_rows(rows, 128, body)

    bufs = (relay_m, relay_p, from_m, from_p, from_pair)
    run(scatter(wire, group, terms, bufs, "b", prepare))
    own = group.slot(0, 0)

    def last(at):
        out[at] = (
            direct[at]
            + terms[own, at].astype(F32)
            + from_m[0, at].astype(F32)
            + from_p[0, at].astype(F32)
            + from_pair[at].astype(F32)
        ).astype(BF16)

    add_rows(rows, 128, last)
    wire.drain()


def finish(back, direct):
    rows, width = direct.shape
    return pl.pallas_call(
        finish_kernel,
        out_shape=jax.ShapeDtypeStruct((rows, width), BF16),
        in_specs=[ANY, VM],
        out_specs=VM,
        scratch_shapes=[
            pltpu.VMEM((16, rows, width), BF16),
            pltpu.VMEM((8, rows, width), BF16),
        ]
        + scatter_shapes(rows, width)
        + [
            pltpu.SemaphoreType.DMA((60,)),
            pltpu.SemaphoreType.DMA((60,)),
            pltpu.SemaphoreType.DMA((9,)),
        ],
        compiler_params=remote_params(3),
        name="finish",
    )(back.reshape(16, rows, width), direct)


def body(nodes, tiles, tile_col, tile_count, w_in, bias_in, w_out, ln_gain, ln_shift, cotangent):
    rows, width = nodes.shape
    cols, count = tile_col[:, 0], tile_count[:, 0]
    slots = tiles[:, 0]
    cols = jnp.clip(cols, 0, 127)
    live = lax.broadcasted_iota(jnp.int32, (64, 4, 128), 1) < count[:, None, None]
    live = live.astype(F32)
    near0, near1, grads, updated, direct, gw_in, gw_out, gvec = middle(
        cols, live, slots, nodes, cotangent, w_in, bias_in[None], w_out, ln_gain[None], ln_shift[None]
    )
    grad_tiles, back = backward(cols, count, slots, near0, near1, grads.reshape(8 * rows, width))
    grad_nodes = finish(back, direct)
    return updated, grad_nodes, grad_tiles[:, None], gw_in, gw_out, gvec


def solution(mesh):
    placed = (
        P(("row", "col"), None),
        P("row", "col", None, None, None),
        P("row", "col", None),
        P("row", "col"),
        P(),
        P(),
        P(),
        P(),
        P(),
        P(("row", "col"), None),
    )
    return jax.shard_map(
        body,
        mesh=mesh,
        in_specs=placed,
        out_specs=(
            P(("row", "col"), None),
            P(("row", "col"), None),
            P("row", "col", None, None, None),
            P(),
            P(),
            P(),
        ),
        check_vma=False,
    )
```

```python
import functools

import jax
import jax.numpy as jnp
from jax import lax
from jax.experimental import pallas as pl
from jax.experimental.pallas import tpu as pltpu
from jax.sharding import PartitionSpec as P

F32, BF16 = jnp.float32, jnp.bfloat16
MIB = 1024 * 1024
VMEM_LIMIT = 56 * MIB
EPS = 1e-05
TOTAL_ROWS = 1024


class Place:
    def __init__(self):
        self.row = lax.axis_index("row")
        self.col = lax.axis_index("col")
        self.x = lax.div(self.row, 4)
        self.zh = lax.rem(lax.div(self.row, 2), 2)
        self.core = lax.rem(self.row, 2)
        self.y = lax.div(self.col, 2)
        self.zl = lax.rem(self.col, 2)


    def peer(self, x=0, y=0, z=0, core=0):
        z_at = lax.rem(self.zh * 2 + self.zl + z, 4)
        row = lax.rem(self.x + x, 4) * 4 + lax.div(z_at, 2) * 2 + lax.rem(self.core + core, 2)
        return (row, lax.rem(self.y + y, 4) * 2 + lax.rem(z_at, 2))

    def all_peers(self):
        steps = [dict(core=1)] + [{axis: d} for axis in "xyz" for d in (1, 2, 3)]
        return [self.peer(**step) for step in steps]


class RowGroup:
    def __init__(self, place):
        self.place = place
        col = place.col
        self.peers = {
            "p": (self.slot(1, 0), col),
            "m": (self.slot(3, 0), col),
            "pair": (self.slot(0, 1), col),
            "sib": (self.slot(0, 0, 1), col),
        }

    def slot(self, ring, pair, sib=0):
        at = self.place
        return (
            lax.rem(at.x + ring, 4) * 4
            + lax.rem(at.zh + pair, 2) * 2
            + lax.rem(at.core + sib, 2)
        )


class ColGroup:
    def __init__(self, place):
        self.place = place
        row = place.row
        self.peers = {
            "p": (row, self.slot(1, 0)),
            "m": (row, self.slot(3, 0)),
            "pair": (row, self.slot(0, 1)),
        }

    def slot(self, ring, pair):
        at = self.place
        return lax.rem(at.y + ring, 4) * 2 + lax.rem(at.zl + pair, 2)


class Wire:
    def __init__(self, send, recv):
        self.send, self.recv = send, recv
        self.names = {}
        self.open = []

    def index(self, name):
        return self.names.setdefault(name, len(self.names))

    def push(self, name, src, dst, to):
        at = self.index(name)
        copy = pltpu.make_async_remote_copy(
            src_ref=src,
            dst_ref=dst,
            send_sem=self.send.at[at],
            recv_sem=self.recv.at[at],
            device_id=to,
            device_id_type=pl.DeviceIdType.MESH,
        )
        copy.start()
        self.open.append(copy)

    def take(self, name, dst, to):
        at = self.index(name)
        pltpu.make_async_remote_copy(
            src_ref=dst,
            dst_ref=dst,
            send_sem=self.send.at[at],
            recv_sem=self.recv.at[at],
            device_id=to,
            device_id_type=pl.DeviceIdType.MESH,
        ).wait_recv()

    def drain(self):
        for copy in self.open:
            copy.wait_send()
        self.open = []


def greet(devices):
    barrier = pltpu.get_barrier_semaphore()
    for device in devices:
        pl.semaphore_signal(barrier, inc=1, device_id=device, device_id_type=pl.DeviceIdType.MESH)
    pl.semaphore_wait(barrier, len(devices))


MOVES = {"p": (3, 0, 0), "m": (1, 0, 0), "pair": (0, 1, 0), "sib": (0, 0, 1)}


def gather(wire, group, buf, tag, per=1):
    half_rows = buf.shape[1] // 2

    def view(slot, half):
        if per == 1:
            return buf.at[slot, pl.ds(half * half_rows, half_rows)]
        return buf.at[pl.ds(slot * per + half * (per // 2), per // 2)]

    has_sib = "sib" in group.peers

    def send(ring, pair, half, way):
        ref = view(group.slot(ring, pair), half)
        dr, dp, dk = MOVES[way]
        name = (tag, (ring + dr) % 4, (pair + dp) % 2, dk, half)
        wire.push(name, ref, ref, group.peers[way])

    def take(ring, pair, half, sib=0):
        slot = group.slot(ring, pair, 1) if sib else group.slot(ring, pair)
        wire.take((tag, ring, pair, sib, half), view(slot, half), group.peers["p"])

    def share(ring, pair, half):
        if has_sib:
            send(ring, pair, half, "sib")

    send(0, 0, 0, "p")
    send(0, 0, 1, "m")
    send(0, 0, 0, "pair")
    send(0, 0, 1, "p")
    send(0, 0, 0, "m")
    send(0, 0, 1, "pair")
    for half in (0, 1):
        share(0, 0, half)
    yield
    take(3, 0, 0)
    send(3, 0, 0, "p")
    take(1, 0, 1)
    send(1, 0, 1, "m")
    share(3, 0, 0)
    share(1, 0, 1)
    yield
    for half in (0, 1):
        take(0, 1, half)
        send(0, 1, half, "p")
        send(0, 1, half, "m")
        share(0, 1, half)
    yield
    take(3, 0, 1)
    take(1, 0, 0)
    share(3, 0, 1)
    share(1, 0, 0)
    yield
    take(3, 1, 0)
    send(3, 1, 0, "p")
    take(1, 1, 1)
    send(1, 1, 1, "m")
    share(3, 1, 0)
    share(1, 1, 1)
    yield
    for half in (0, 1):
        take(2, 0, half)
        share(2, 0, half)
    yield
    take(3, 1, 1)
    take(1, 1, 0)
    share(3, 1, 1)
    share(1, 1, 0)
    for half in (0, 1):
        take(2, 1, half)
        share(2, 1, half)
    yield
    if has_sib:
        for ring in (0, 1, 3, 2):
            for pair in (0, 1):
                for half in (0, 1):
                    take(ring, pair, half, 1)


def add_rows(rows, step, body):
    def one(i, carry):
        body(pl.ds(pl.multiple_of(i * step, step), step))
        return carry

    lax.fori_loop(0, rows // step, one, 0)


def scatter_shapes(rows, width):
    return [
        pltpu.VMEM((2, rows // 2, width), BF16),
        pltpu.VMEM((2, rows // 2, width), BF16),
        pltpu.VMEM((2, rows, width), BF16),
        pltpu.VMEM((2, rows, width), BF16),
        pltpu.VMEM((rows, width), BF16),
    ]


def scatter(wire, group, terms, bufs, tag, prepare):
    relay_m, relay_p, from_m, from_p, from_pair = bufs
    rows = terms.shape[1]
    half_rows = rows // 2
    cut = (pl.ds(0, half_rows), pl.ds(half_rows, half_rows))
    step = 128

    def part(ring, pair, half):
        return terms.at[group.slot(ring, pair), cut[half]]

    def add(target, *others):
        def body(at):
            total = target[at].astype(F32)
            for other in others:
                total = total + other[at].astype(F32)
            target[at] = total.astype(BF16)

        add_rows(half_rows, step, body)

    for q in (1, 0):
        prepare(2, q)
        wire.push((tag, "rm", q), part(2, q, 0), relay_m.at[q], group.peers["p"])
        wire.push((tag, "rp", q), part(2, q, 1), relay_p.at[q], group.peers["m"])
    yield
    for q in (1, 0):
        prepare(1, q)
        prepare(3, q)
        wire.push((tag, "m", q, 1), part(1, q, 1), from_m.at[q, cut[1]], group.peers["p"])
        wire.push((tag, "p", q, 0), part(3, q, 0), from_p.at[q, cut[0]], group.peers["m"])
        yield
        wire.take((tag, "rm", q), relay_m.at[q], group.peers["p"])
        add(part(1, q, 0), relay_m.at[q])
        wire.push((tag, "m", q, 0), part(1, q, 0), from_m.at[q, cut[0]], group.peers["p"])
        wire.take((tag, "rp", q), relay_p.at[q], group.peers["p"])
        add(part(3, q, 1), relay_p.at[q])
        wire.push((tag, "p", q, 1), part(3, q, 1), from_p.at[q, cut[1]], group.peers["m"])
    yield
    prepare(0, 1)
    for half in (0, 1):
        wire.take((tag, "m", 1, half), from_m.at[1, cut[half]], group.peers["p"])
        wire.take((tag, "p", 1, half), from_p.at[1, cut[half]], group.peers["p"])
        add(part(0, 1, half), from_m.at[1, cut[half]], from_p.at[1, cut[half]])
        wire.push((tag, "z", half), part(0, 1, half), from_pair.at[cut[half]], group.peers["pair"])
    yield
    prepare(0, 0)
    for half in (0, 1):
        wire.take((tag, "m", 0, half), from_m.at[0, cut[half]], group.peers["p"])
        wire.take((tag, "p", 0, half), from_p.at[0, cut[half]], group.peers["p"])
    for half in (0, 1):
        wire.take((tag, "z", half), from_pair.at[cut[half]], group.peers["p"])


def total_shapes(width):
    return [
        pltpu.VMEM((TOTAL_ROWS, width), F32),
        pltpu.VMEM((TOTAL_ROWS // 2, width), F32),
        pltpu.VMEM((3, TOTAL_ROWS // 8, width), F32),
        pltpu.VMEM((3, TOTAL_ROWS // 32, width), F32),
        pltpu.VMEM((4, TOTAL_ROWS // 32, width), F32),
    ]


def total(wire, place, mine, bufs, tag):
    result, in_core, in_x, in_y, in_z = bufs
    half, quarter, piece = TOTAL_ROWS // 2, TOTAL_ROWS // 8, TOTAL_ROWS // 32

    def span(core, x=None, y=None):
        start, size = core * half, half
        if x is not None:
            start, size = start + x * quarter, quarter
        if y is not None:
            start, size = start + y * piece, piece
        return pl.ds(pl.multiple_of(start, piece), size)

    core, x, y = place.core, place.x, place.y
    z = place.zh * 2 + place.zl
    other = 1 - core
    sib = place.peer(core=1)
    wire.push((tag, "core"), mine.at[span(other)], in_core, sib)
    yield
    wire.take((tag, "core"), in_core, sib)

    def fold(i, carry):
        at = pl.ds(pl.multiple_of(core * half + i * 64, 64), 64)
        mine[at] += in_core[pl.ds(pl.multiple_of(i * 64, 64), 64)]
        return carry

    lax.fori_loop(0, half // 64, fold, 0)
    for d in (1, 2, 3):
        to = place.peer(x=d)
        wire.push((tag, "x", d), mine.at[span(core, lax.rem(x + d, 4))], in_x.at[d - 1], to)
    yield
    for d in (1, 2, 3):
        wire.take((tag, "x", d), in_x.at[d - 1], sib)
    mine[span(core, x)] += in_x[0] + in_x[1] + in_x[2]
    for d in (1, 2, 3):
        to = place.peer(y=d)
        wire.push((tag, "y", d), mine.at[span(core, x, lax.rem(y + d, 4))], in_y.at[d - 1], to)
    yield
    for d in (1, 2, 3):
        wire.take((tag, "y", d), in_y.at[d - 1], sib)
    in_z[z] = mine[span(core, x, y)] + in_y[0] + in_y[1] + in_y[2]
    for d in (1, 2, 3):
        wire.push((tag, "z", d), in_z.at[z], in_z.at[z], place.peer(z=d))
    yield
    for d in (1, 2, 3):
        wire.take((tag, "z", d), in_z.at[lax.rem(z + 4 - d, 4)], sib)
    at = span(core, x, y)
    result[at] = in_z[0] + in_z[1] + in_z[2] + in_z[3]
    for d in (1, 2, 3):
        wire.push((tag, "back y", d), result.at[at], result.at[at], place.peer(y=d))
    yield
    for d in (1, 2, 3):
        wire.take((tag, "back y", d), result.at[span(core, x, lax.rem(y + 4 - d, 4))], sib)
    at = span(core, x)
    for d in (1, 2, 3):
        wire.push((tag, "back x", d), result.at[at], result.at[at], place.peer(x=d))
    yield
    for d in (1, 2, 3):
        wire.take((tag, "back x", d), result.at[span(core, lax.rem(x + 4 - d, 4))], sib)
    wire.push((tag, "back core"), result.at[span(core)], result.at[span(core)], sib)
    yield
    wire.take((tag, "back core"), result.at[span(other)], sib)


def run(steps):
    for _ in steps:
        pass


def dot(a, b, dims=((1,), (0,))):
    return lax.dot_general(a, b, (dims, ((), ())), preferred_element_type=F32)


ANY = pl.BlockSpec(memory_space=pl.ANY)
VM = pl.BlockSpec(memory_space=pltpu.VMEM)


def remote_params(collective_id):
    return pltpu.CompilerParams(
        collective_id=collective_id, has_side_effects=True, vmem_limit_bytes=VMEM_LIMIT
    )


ORDER = [(2, 1), (2, 0), (1, 1), (3, 1), (1, 0), (3, 0), (0, 1), (0, 0)]


def middle_kernel(
    cols, live, tiles, nodes_any, nodes, cot, w_in, bias, w_out, gain, shift,
    near0_out, near1_out, grads, updated, direct, gw_in, gw_out, gvec,
    near0, near1, slots, terms0, terms1, *rest,
):
    bufs0, bufs1, rest = rest[:5], rest[5:10], rest[10:]
    msg_s, act_s, gproj_s, gpre_s, weights = rest[:5]
    sum_bufs, (send, recv, load) = rest[5:10], rest[10:]
    place = Place()
    across, along = RowGroup(place), ColGroup(place)
    width = nodes.shape[1]
    rows = nodes.shape[0]
    near, terms = (near0, near1), (terms0, terms1)

    mine = [
        pltpu.make_async_copy(
            nodes_any.at[:, :, pl.ds(h * 128, 128)],
            near[h].at[pl.ds(across.slot(0, 0) * 8, 8)],
            load.at[8 + h],
        )
        for h in (0, 1)
    ]
    for copy in mine:
        copy.start()

    def loader(ring, pair):
        at = pl.ds(along.slot(ring, pair) * 8, 8)
        return pltpu.make_async_copy(tiles.at[at], slots.at[at], load.at[ring * 2 + pair])

    for at in ORDER:
        loader(*at).start()
    greet(place.all_peers())
    wire = Wire(send, recv)
    for copy in mine:
        copy.wait()

    def mask(ring, pair):
        loader(ring, pair).wait()
        base = along.slot(ring, pair) * 8

        def one(i, carry):
            for k in range(4):
                keep = live[base + i, pl.ds(k, 1)].astype(BF16)
                slots[base + i, k] = slots[base + i, k] * keep
            return carry

        lax.fori_loop(0, 8, one, 0)

    def product(h, ring, pair):
        slot = along.slot(ring, pair)

        def one(j, carry):
            for u in range(2):
                i = slot * 8 + j * 2 + u
                left = jnp.concatenate([slots[i, k] for k in range(4)], axis=1)
                right = []
                for k in range(4):
                    right.append(near[h][cols[i, k]])
                at = pl.ds(pl.multiple_of((j * 2 + u) * 128, 128), 128)
                terms[h][slot, at] = dot(left, jnp.concatenate(right, axis=0)).astype(BF16)
            return carry

        lax.fori_loop(0, 4, one, 0)

    gather0 = gather(wire, across, near0, "n0", 8)
    gather1 = gather(wire, across, near1, "n1", 8)
    for step in range(5):
        next(gather0)
        for at in ORDER[2 * step : 2 * step + 2]:
            mask(*at)
    next(gather1)
    run(gather0)

    def prepare0(ring, pair):
        product(0, ring, pair)
        next(gather1, None)

    scatter0 = scatter(wire, along, terms0, bufs0, "s0", prepare0)
    for _ in range(4):
        next(scatter0)
    run(gather1)
    leaving = [
        pltpu.make_async_copy(near[h], out, load.at[10 + h])
        for h, out in ((0, near0_out), (1, near1_out))
    ]
    for copy in leaving:
        copy.start()
    scatter1 = scatter(wire, along, terms1, bufs1, "s1", lambda *at: product(1, *at))
    for _ in scatter1:
        next(scatter0, None)
    run(scatter0)
    own = along.slot(0, 0)
    gsum = weights.at[pl.ds(3 * width, 8)]
    weights[3 * width :] = jnp.zeros((weights.shape[0] - 3 * width, width), F32)

    def chunk(i, carry):
        at = pl.ds(pl.multiple_of(i * 256, 256), 256)
        msg = jnp.concatenate(
            [
                (
                    terms[h][own, at].astype(F32)
                    + bufs[2][0, at].astype(F32)
                    + bufs[3][0, at].astype(F32)
                    + bufs[4][at].astype(F32)
                ).astype(BF16)
                for h, bufs in ((0, bufs0), (1, bufs1))
            ],
            axis=1,
        )
        msg_s[at] = msg
        mine = nodes[at]
        pre = dot(mine, w_in[:width]) + dot(msg, w_in[width:]) + bias[...]
        sig = jax.nn.sigmoid(pre)
        act = (pre * sig).astype(BF16)
        act_s[at] = act
        proj = dot(act, w_out[...])
        mean = jnp.mean(proj, axis=-1, keepdims=True)
        off = proj - mean
        var = jnp.mean(off * off, axis=-1, keepdims=True)
        rstd = 1.0 / jnp.sqrt(var + EPS)
        normed = off * rstd
        updated[at] = (mine.astype(F32) + normed * gain[...] + shift[...]).astype(BF16)
        grad_out = cot[at].astype(F32)
        gscaled = grad_out * gain[...]
        gproj = (
            (
                gscaled
                - jnp.mean(gscaled, axis=-1, keepdims=True)
                - normed * jnp.mean(gscaled * normed, axis=-1, keepdims=True)
            )
            * rstd
        ).astype(BF16)
        gproj_s[at] = gproj
        gact = dot(gproj, w_out[...], ((1,), (1,)))
        gpre = gact * sig * (1.0 + pre * (1.0 - sig))
        gpre_b = gpre.astype(BF16)
        gpre_s[at] = gpre_b
        grads[own, at] = dot(gpre_b, w_in[width:], ((1,), (1,))).astype(BF16)
        direct[at] = grad_out + dot(gpre_b, w_in[:width], ((1,), (1,)))
        gsum[0:1] += jnp.sum(gpre, axis=0, keepdims=True)
        gsum[1:2] += jnp.sum(grad_out * normed, axis=0, keepdims=True)
        gsum[2:3] += jnp.sum(grad_out, axis=0, keepdims=True)
        return carry

    lax.fori_loop(0, rows // 256, chunk, 0)
    steps = gather(wire, along, grads, "g")
    next(steps)
    weights[:width] = dot(nodes[...], gpre_s[...], ((0,), (0,)))
    weights[width : 2 * width] = dot(msg_s[...], gpre_s[...], ((0,), (0,)))
    weights[2 * width : 3 * width] = dot(act_s[...], gproj_s[...], ((0,), (0,)))
    sums = total(wire, place, weights, sum_bufs, "w")
    next(sums)
    for _ in steps:
        next(sums, None)
    run(sums)
    result = sum_bufs[0]
    factor = F32(131072.0) ** F32(-0.5)
    gw_in[...] = result[: 2 * width] * factor
    gw_out[...] = result[2 * width : 3 * width] * factor
    gvec[...] = result[3 * width : 3 * width + 3] * factor
    for copy in leaving:
        copy.wait()
    wire.drain()


def middle(cols, live, tiles, nodes, cot, w_in, bias, w_out, gain, shift):
    rows, width = nodes.shape
    one = functools.partial(pltpu.VMEM, (rows, width))
    smem = pl.BlockSpec(memory_space=pltpu.SMEM)
    near = jax.ShapeDtypeStruct((128, 128, 128), BF16)
    return pl.pallas_call(
        middle_kernel,
        out_shape=[
            near,
            near,
            jax.ShapeDtypeStruct((8, rows, width), BF16),
            jax.ShapeDtypeStruct((rows, width), BF16),
            jax.ShapeDtypeStruct((rows, width), F32),
            jax.ShapeDtypeStruct((2 * width, width), F32),
            jax.ShapeDtypeStruct((width, width), F32),
            jax.ShapeDtypeStruct((3, width), F32),
        ],
        in_specs=[smem, VM, ANY, ANY] + [VM] * 7,
        out_specs=[ANY] * 2 + [VM] * 6,
        scratch_shapes=[pltpu.VMEM((128, 128, 128), BF16)] * 2
        + [pltpu.VMEM(tiles.shape, BF16)]
        + [pltpu.VMEM((8, rows, 128), BF16)] * 2
        + scatter_shapes(rows, 128) * 2
        + [one(BF16)] * 4
        + [pltpu.VMEM((TOTAL_ROWS, width), F32)]
        + total_shapes(width)
        + [
            pltpu.SemaphoreType.DMA((140,)),
            pltpu.SemaphoreType.DMA((140,)),
            pltpu.SemaphoreType.DMA((12,)),
        ],
        compiler_params=remote_params(2),
        name="middle",
    )(cols, live, tiles, nodes.reshape(8, 128, width), nodes, cot, w_in, bias, w_out, gain, shift)


def backward_kernel(
    cols, count, tiles, near0, near1, grads, updated_in, gw_in_in, gw_out_in, gvec_in,
    tile_grads, back, updated, gw_in, gw_out, gvec, acc,
):
    step = pl.program_id(0)
    per = tiles.shape[0]
    updated[...] = updated_in[...]
    gw_in[...] = gw_in_in[...]
    gw_out[...] = gw_out_in[...]
    gvec[...] = gvec_in[...]

    @pl.when(step == 0)
    def _():
        def clear(i, carry):
            acc[i] = jnp.zeros(acc.shape[1:], F32)
            return carry

        lax.fori_loop(0, acc.shape[0], clear, 0)

    scale = F32(256.0) ** F32(-0.5)

    def work(i, at, slots):
        live = count[at]
        grad = grads[pl.ds(i * 128, 128)]
        which = [cols[at, k] for k in range(slots)]
        picked = jnp.concatenate(
            [jnp.concatenate([near0[c], near1[c]], axis=1) for c in which], axis=0
        )
        made = (dot(grad, picked, ((1,), (1,))) * scale).astype(BF16)
        zero = jnp.zeros((128, 128), BF16)
        for k in range(slots):
            tile_grads[i, k] = jnp.where(k < live, made[:, k * 128 : k * 128 + 128], zero)
        kept = jnp.concatenate([jnp.where(k < live, tiles[i, k], zero) for k in range(slots)], axis=1)
        return which, dot(kept, grad, ((0,), (0,)))

    def both(i, slots):
        found = [work(i + u, step * per + i + u, slots) for u in (0, 1)]
        for which, terms in found:
            for k in range(slots):
                acc[which[k]] += terms[k * 128 : k * 128 + 128]

    for i in range(0, per, 2):
        most = jnp.maximum(count[step * per + i], count[step * per + i + 1])

        @pl.when(most <= 2)
        def _():
            for u in (0, 1):
                tile_grads[i + u, 2:4] = jnp.zeros((2, 128, 128), BF16)

        @pl.when(most <= 0)
        def _():
            for u in (0, 1):
                tile_grads[i + u, 0:2] = jnp.zeros((2, 128, 128), BF16)

        @pl.when((most > 0) & (most <= 2))
        def _():
            both(i, 2)

        @pl.when(most > 2)
        def _():
            both(i, 4)

    @pl.when(step == pl.num_programs(0) - 1)
    def _():
        def put(i, carry):
            back[i] = acc[i].astype(BF16)
            return carry

        lax.fori_loop(0, acc.shape[0], put, 0)


def backward(cols, count, tiles, near0, near1, grads, updated, gw_in, gw_out, gvec):
    row_blocks = tiles.shape[0]
    width = grads.shape[1]
    columns = (128, 128, width)
    near = pl.BlockSpec(near0.shape, lambda s, *_: (0, 0, 0), pipeline_mode=pl.Buffered(1))
    per = 8
    steps = row_blocks // per

    def cut(array):
        return pl.BlockSpec((array.shape[0] // steps, width), lambda s, *_: (s, 0))

    passed = [cut(updated), cut(gw_in), cut(gw_out), pl.BlockSpec((3, width), lambda s, *_: (0, 0))]
    return pl.pallas_call(
        backward_kernel,
        out_shape=[
            jax.ShapeDtypeStruct(tiles.shape, BF16),
            jax.ShapeDtypeStruct(columns, BF16),
        ]
        + [jax.ShapeDtypeStruct(a.shape, a.dtype) for a in (updated, gw_in, gw_out, gvec)],
        grid_spec=pltpu.PrefetchScalarGridSpec(
            num_scalar_prefetch=2,
            grid=(steps,),
            in_specs=[
                pl.BlockSpec((per, 4, 128, 128), lambda s, *_: (s, 0, 0, 0)),
                near,
                near,
                pl.BlockSpec((per * 128, width), lambda s, *_: (s, 0)),
            ]
            + passed,
            out_specs=[
                pl.BlockSpec((per, 4, 128, 128), lambda s, *_: (s, 0, 0, 0)),
                pl.BlockSpec(columns, lambda s, *_: (0, 0, 0), pipeline_mode=pl.Buffered(1)),
            ]
            + passed,
            scratch_shapes=[pltpu.VMEM(columns, F32)],
        ),
        compiler_params=pltpu.CompilerParams(vmem_limit_bytes=VMEM_LIMIT),
        name="backward",
    )(cols, count, tiles, near0, near1, grads, updated, gw_in, gw_out, gvec)


def finish_kernel(
    back, direct, out,
    terms, others, relay_m, relay_p, from_m, from_p, from_pair, send, recv, load,
):
    group = RowGroup(Place())
    rows = terms.shape[1]

    def loader(ring, pair):
        slot = group.slot(ring, pair)
        return pltpu.make_async_copy(back.at[slot], terms.at[slot], load.at[ring * 2 + pair])

    for at in ORDER:
        loader(*at).start()
    greet(list(group.peers.values()))
    wire = Wire(send, recv)
    for ring, pair in ORDER:
        wire.push(
            ("f", ring, pair),
            back.at[group.slot(ring, pair, 1)],
            others.at[ring * 2 + pair],
            group.peers["sib"],
        )

    def prepare(ring, pair):
        loader(ring, pair).wait()
        other = others.at[ring * 2 + pair]
        wire.take(("f", ring, pair), other, group.peers["sib"])
        slot = group.slot(ring, pair)

        def body(at):
            terms[slot, at] = (terms[slot, at].astype(F32) + other[at].astype(F32)).astype(BF16)

        add_rows(rows, 128, body)

    bufs = (relay_m, relay_p, from_m, from_p, from_pair)
    run(scatter(wire, group, terms, bufs, "b", prepare))
    own = group.slot(0, 0)

    def last(at):
        out[at] = (
            direct[at]
            + terms[own, at].astype(F32)
            + from_m[0, at].astype(F32)
            + from_p[0, at].astype(F32)
            + from_pair[at].astype(F32)
        ).astype(BF16)

    add_rows(rows, 128, last)
    wire.drain()


def finish(back, direct):
    rows, width = direct.shape
    return pl.pallas_call(
        finish_kernel,
        out_shape=jax.ShapeDtypeStruct((rows, width), BF16),
        in_specs=[ANY, VM],
        out_specs=VM,
        scratch_shapes=[
            pltpu.VMEM((16, rows, width), BF16),
            pltpu.VMEM((8, rows, width), BF16),
        ]
        + scatter_shapes(rows, width)
        + [
            pltpu.SemaphoreType.DMA((60,)),
            pltpu.SemaphoreType.DMA((60,)),
            pltpu.SemaphoreType.DMA((9,)),
        ],
        compiler_params=remote_params(3),
        name="finish",
    )(back.reshape(16, rows, width), direct)


def body(nodes, tiles, tile_col, tile_count, w_in, bias_in, w_out, ln_gain, ln_shift, cotangent):
    rows, width = nodes.shape
    cols, count = tile_col[:, 0], tile_count[:, 0]
    slots = tiles[:, 0]
    cols = jnp.clip(cols, 0, 127)
    live = lax.broadcasted_iota(jnp.int32, (64, 4, 128), 1) < count[:, None, None]
    live = live.astype(F32)
    near0, near1, grads, updated, direct, gw_in, gw_out, gvec = middle(
        cols, live, slots, nodes, cotangent, w_in, bias_in[None], w_out, ln_gain[None], ln_shift[None]
    )
    grad_tiles, back, updated, gw_in, gw_out, gvec = backward(
        cols, count, slots, near0, near1, grads.reshape(8 * rows, width), updated, gw_in, gw_out, gvec
    )
    grad_nodes = finish(back, direct)
    return updated, grad_nodes, grad_tiles[:, None], gw_in, gw_out, gvec


def solution(mesh):
    placed = (
        P(("row", "col"), None),
        P("row", "col", None, None, None),
        P("row", "col", None),
        P("row", "col"),
        P(),
        P(),
        P(),
        P(),
        P(),
        P(("row", "col"), None),
    )
    return jax.shard_map(
        body,
        mesh=mesh,
        in_specs=placed,
        out_specs=(
            P(("row", "col"), None),
            P(("row", "col"), None),
            P("row", "col", None, None, None),
            P(),
            P(),
            P(),
        ),
        check_vma=False,
    )
```

```python
import functools

import jax
import jax.numpy as jnp
from jax import lax
from jax.experimental import pallas as pl
from jax.experimental.pallas import tpu as pltpu
from jax.sharding import PartitionSpec as P

F32, BF16 = jnp.float32, jnp.bfloat16
MIB = 1024 * 1024
VMEM_LIMIT = 58 * MIB
EPS = 1e-05
TOTAL_ROWS = 1024


class Place:
    def __init__(self):
        self.row = lax.axis_index("row")
        self.col = lax.axis_index("col")
        self.x = lax.div(self.row, 4)
        self.zh = lax.rem(lax.div(self.row, 2), 2)
        self.core = lax.rem(self.row, 2)
        self.y = lax.div(self.col, 2)
        self.zl = lax.rem(self.col, 2)


    def peer(self, x=0, y=0, z=0, core=0):
        z_at = lax.rem(self.zh * 2 + self.zl + z, 4)
        row = lax.rem(self.x + x, 4) * 4 + lax.div(z_at, 2) * 2 + lax.rem(self.core + core, 2)
        return (row, lax.rem(self.y + y, 4) * 2 + lax.rem(z_at, 2))

    def all_peers(self):
        steps = [dict(core=1)] + [{axis: d} for axis in "xyz" for d in (1, 2, 3)]
        return [self.peer(**step) for step in steps]


class RowGroup:
    def __init__(self, place):
        self.place = place
        col = place.col
        self.peers = {
            "p": (self.slot(1, 0), col),
            "m": (self.slot(3, 0), col),
            "pair": (self.slot(0, 1), col),
            "sib": (self.slot(0, 0, 1), col),
        }

    def slot(self, ring, pair, sib=0):
        at = self.place
        return (
            lax.rem(at.x + ring, 4) * 4
            + lax.rem(at.zh + pair, 2) * 2
            + lax.rem(at.core + sib, 2)
        )


class ColGroup:
    def __init__(self, place):
        self.place = place
        row = place.row
        self.peers = {
            "p": (row, self.slot(1, 0)),
            "m": (row, self.slot(3, 0)),
            "pair": (row, self.slot(0, 1)),
        }

    def slot(self, ring, pair):
        at = self.place
        return lax.rem(at.y + ring, 4) * 2 + lax.rem(at.zl + pair, 2)


class Wire:
    def __init__(self, send, recv):
        self.send, self.recv = send, recv
        self.names = {}
        self.open = []

    def index(self, name):
        return self.names.setdefault(name, len(self.names))

    def push(self, name, src, dst, to):
        at = self.index(name)
        copy = pltpu.make_async_remote_copy(
            src_ref=src,
            dst_ref=dst,
            send_sem=self.send.at[at],
            recv_sem=self.recv.at[at],
            device_id=to,
            device_id_type=pl.DeviceIdType.MESH,
        )
        copy.start()
        self.open.append(copy)

    def take(self, name, dst, to):
        at = self.index(name)
        pltpu.make_async_remote_copy(
            src_ref=dst,
            dst_ref=dst,
            send_sem=self.send.at[at],
            recv_sem=self.recv.at[at],
            device_id=to,
            device_id_type=pl.DeviceIdType.MESH,
        ).wait_recv()

    def drain(self):
        for copy in self.open:
            copy.wait_send()
        self.open = []


def greet(devices):
    barrier = pltpu.get_barrier_semaphore()
    for device in devices:
        pl.semaphore_signal(barrier, inc=1, device_id=device, device_id_type=pl.DeviceIdType.MESH)
    pl.semaphore_wait(barrier, len(devices))


MOVES = {"p": (3, 0, 0), "m": (1, 0, 0), "pair": (0, 1, 0), "sib": (0, 0, 1)}


QUARTER = ((0, 3, False), (3, 3, False), (6, 1, True), (7, 1, True))
MORE = ((0, 3, False), (3, 2, False), (5, 1, True), (6, 2, True))


def gather(wire, group, buf, tag, parts, per=1):
    unit = buf.shape[1] // 8

    def view(slot, part):
        start, size, _ = parts[part]
        if per == 1:
            return buf.at[slot, pl.ds(start * unit, size * unit)]
        return buf.at[pl.ds(slot * per + start, size)]

    has_sib = "sib" in group.peers
    late = [c for c in range(4) if parts[c][2]]
    early = [c for c in range(4) if not parts[c][2]]

    def send(ring, pair, part, way):
        ref = view(group.slot(ring, pair), part)
        dr, dp, dk = MOVES[way]
        name = (tag, (ring + dr) % 4, (pair + dp) % 2, dk, part)
        wire.push(name, ref, ref, group.peers[way])

    def take(ring, pair, part, sib=0):
        slot = group.slot(ring, pair, 1) if sib else group.slot(ring, pair)
        wire.take((tag, ring, pair, sib, part), view(slot, part), group.peers["p"])

    def share(ring, pair, part):
        if has_sib:
            send(ring, pair, part, "sib")

    def relay(pair, which):
        for c in which:
            ring, way = ((3, "p"), (1, "m"))[c % 2]
            take(ring, pair, c)
            send(ring, pair, c, way)
            if c in late and pair == 0:
                send(ring, pair, c, "pair")
            share(ring, pair, c)

    def rest(pair, which):
        for c in which:
            ring = (1, 3)[c % 2]
            take(ring, pair, c)
            if c in late and pair == 0:
                send(ring, pair, c, "pair")
            share(ring, pair, c)

    for c in early:
        send(0, 0, c, "pair")
    for c in early + late:
        send(0, 0, c, ("p", "m")[c % 2])
    for c in early + late:
        send(0, 0, c, ("m", "p")[c % 2])
    for c in late:
        send(0, 0, c, "pair")
    for c in early + late:
        share(0, 0, c)
    yield
    relay(0, early + late)
    yield
    for c in early:
        take(0, 1, c)
        send(0, 1, c, "p")
        send(0, 1, c, "m")
        share(0, 1, c)
    yield
    rest(0, late + early)
    yield
    for c in late:
        take(2, 0, c)
        send(2, 0, c, "pair")
        share(2, 0, c)
    relay(1, early)
    yield
    for c in early:
        take(2, 0, c)
        share(2, 0, c)
    for c in late:
        take(0, 1, c)
        share(0, 1, c)
    yield
    rest(1, early)
    for c in late:
        for ring in (1, 3, 2):
            take(ring, 1, c)
            share(ring, 1, c)
    for c in early:
        take(2, 1, c)
        share(2, 1, c)
    yield
    if has_sib:
        for ring in (0, 1, 3, 2):
            for pair in (0, 1):
                for c in range(4):
                    take(ring, pair, c, 1)


def add_rows(rows, step, body):
    def one(i, carry):
        body(pl.ds(pl.multiple_of(i * step, step), step))
        return carry

    lax.fori_loop(0, rows // step, one, 0)


def scatter_shapes(rows, width):
    return [
        pltpu.VMEM((2, rows, width), BF16),
        pltpu.VMEM((2, rows, width), BF16),
        pltpu.VMEM((2, rows, width), BF16),
        pltpu.VMEM((2, rows, width), BF16),
        pltpu.VMEM((4, rows, width), BF16),
    ]


def scatter(wire, group, terms, bufs, tag, prepare, parts):
    relay_m, relay_p, from_m, from_p, from_pair = bufs
    unit = terms.shape[1] // 8
    cut = [pl.ds(start * unit, size * unit) for start, size, _ in parts]
    late = [c for c in range(4) if parts[c][2]]
    early = [c for c in range(4) if not parts[c][2]]
    start = parts[late[0]][0]
    first = pl.ds(start * unit, sum(parts[c][1] for c in late) * unit)
    to_p, to_m, to_pair = group.peers["p"], group.peers["m"], group.peers["pair"]

    def at(ring, pair, rows):
        return terms.at[group.slot(ring, pair), rows]

    def add(target, *others):
        def body(rows):
            total = target[rows].astype(F32)
            for other in others:
                total = total + other[rows].astype(F32)
            target[rows] = total.astype(BF16)

        add_rows(target.shape[0], unit, body)

    def cross(ring):
        dst = from_pair.at[ring, first]
        wire.push((tag, "first", ring), at(ring, 1, first), dst, to_pair)

    def crossed(ring):
        src = from_pair.at[ring, first]
        wire.take((tag, "first", ring), src, to_pair)
        add(at(ring, 0, first), src)

    def far(q, which):
        for c in which:
            dst, to = ((relay_m, to_p), (relay_p, to_m))[c % 2]
            wire.push((tag, "far", q, c), at(2, q, cut[c]), dst.at[q, cut[c]], to)

    def single(q, which):
        for c in which:
            ring, dst, to = ((3, from_p, to_m), (1, from_m, to_p))[c % 2]
            wire.push((tag, "one", q, c), at(ring, q, cut[c]), dst.at[q, cut[c]], to)

    def double(q, which):
        for c in which:
            ring, via, dst, to = ((1, relay_m, from_m, to_p), (3, relay_p, from_p, to_m))[c % 2]
            wire.take((tag, "far", q, c), via.at[q, cut[c]], to)
            add(at(ring, q, cut[c]), via.at[q, cut[c]])
            wire.push((tag, "two", q, c), at(ring, q, cut[c]), dst.at[q, cut[c]], to)

    def arrive(q, which):
        for c in which:
            one, two = ((from_p, from_m), (from_m, from_p))[c % 2]
            wire.take((tag, "one", q, c), one.at[q, cut[c]], to_p)
            wire.take((tag, "two", q, c), two.at[q, cut[c]], to_p)

    prepare(2, 1)
    cross(2)
    far(1, early)
    prepare(2, 0)
    far(0, early)
    yield
    prepare(1, 1)
    cross(1)
    prepare(3, 1)
    cross(3)
    single(1, early)
    crossed(2)
    far(0, late)
    yield
    double(1, early)
    prepare(1, 0)
    prepare(3, 0)
    single(0, early)
    yield
    crossed(1)
    crossed(3)
    single(0, late)
    double(0, early + late)
    yield
    prepare(0, 1)
    cross(0)
    for c in early:
        arrive(1, [c])
        add(at(0, 1, cut[c]), from_m.at[1, cut[c]], from_p.at[1, cut[c]])
        wire.push((tag, "last", c), at(0, 1, cut[c]), from_pair.at[0, cut[c]], to_pair)
    yield
    prepare(0, 0)
    arrive(0, early + late)
    wire.take((tag, "first", 0), from_pair.at[0, first], to_pair)
    for c in early:
        wire.take((tag, "last", c), from_pair.at[0, cut[c]], to_pair)


def total_shapes(width):
    return [
        pltpu.VMEM((TOTAL_ROWS, width), F32),
        pltpu.VMEM((TOTAL_ROWS // 2, width), F32),
        pltpu.VMEM((3, TOTAL_ROWS // 8, width), F32),
        pltpu.VMEM((3, TOTAL_ROWS // 32, width), F32),
        pltpu.VMEM((4, TOTAL_ROWS // 32, width), F32),
    ]


def total(wire, place, mine, bufs, tag):
    result, in_core, in_x, in_y, in_z = bufs
    half, quarter, piece = TOTAL_ROWS // 2, TOTAL_ROWS // 8, TOTAL_ROWS // 32

    def span(core, x=None, y=None):
        start, size = core * half, half
        if x is not None:
            start, size = start + x * quarter, quarter
        if y is not None:
            start, size = start + y * piece, piece
        return pl.ds(pl.multiple_of(start, piece), size)

    core, x, y = place.core, place.x, place.y
    z = place.zh * 2 + place.zl
    other = 1 - core
    sib = place.peer(core=1)
    wire.push((tag, "core"), mine.at[span(other)], in_core, sib)
    yield
    wire.take((tag, "core"), in_core, sib)

    def fold(i, carry):
        at = pl.ds(pl.multiple_of(core * half + i * 64, 64), 64)
        mine[at] += in_core[pl.ds(pl.multiple_of(i * 64, 64), 64)]
        return carry

    lax.fori_loop(0, half // 64, fold, 0)
    for d in (1, 2, 3):
        to = place.peer(x=d)
        wire.push((tag, "x", d), mine.at[span(core, lax.rem(x + d, 4))], in_x.at[d - 1], to)
    yield
    for d in (1, 2, 3):
        wire.take((tag, "x", d), in_x.at[d - 1], sib)
    mine[span(core, x)] += in_x[0] + in_x[1] + in_x[2]
    for d in (1, 2, 3):
        to = place.peer(y=d)
        wire.push((tag, "y", d), mine.at[span(core, x, lax.rem(y + d, 4))], in_y.at[d - 1], to)
    yield
    for d in (1, 2, 3):
        wire.take((tag, "y", d), in_y.at[d - 1], sib)
    in_z[z] = mine[span(core, x, y)] + in_y[0] + in_y[1] + in_y[2]
    for d in (1, 2, 3):
        wire.push((tag, "z", d), in_z.at[z], in_z.at[z], place.peer(z=d))
    yield
    for d in (1, 2, 3):
        wire.take((tag, "z", d), in_z.at[lax.rem(z + 4 - d, 4)], sib)
    at = span(core, x, y)
    result[at] = in_z[0] + in_z[1] + in_z[2] + in_z[3]
    for d in (1, 2, 3):
        wire.push((tag, "back y", d), result.at[at], result.at[at], place.peer(y=d))
    yield
    for d in (1, 2, 3):
        wire.take((tag, "back y", d), result.at[span(core, x, lax.rem(y + 4 - d, 4))], sib)
    at = span(core, x)
    for d in (1, 2, 3):
        wire.push((tag, "back x", d), result.at[at], result.at[at], place.peer(x=d))
    yield
    for d in (1, 2, 3):
        wire.take((tag, "back x", d), result.at[span(core, lax.rem(x + 4 - d, 4))], sib)
    wire.push((tag, "back core"), result.at[span(core)], result.at[span(core)], sib)
    yield
    wire.take((tag, "back core"), result.at[span(other)], sib)


def run(steps):
    for _ in steps:
        pass


def dot(a, b, dims=((1,), (0,))):
    return lax.dot_general(a, b, (dims, ((), ())), preferred_element_type=F32)


ANY = pl.BlockSpec(memory_space=pl.ANY)
VM = pl.BlockSpec(memory_space=pltpu.VMEM)


def remote_params(collective_id):
    return pltpu.CompilerParams(
        collective_id=collective_id, has_side_effects=True, vmem_limit_bytes=VMEM_LIMIT
    )


ORDER = [(2, 1), (2, 0), (1, 1), (3, 1), (1, 0), (3, 0), (0, 1), (0, 0)]


def middle_kernel(
    cols, live, tiles, nodes_any, nodes, cot, w_in, bias, w_out, gain, shift,
    near0_out, near1_out, grads, updated, direct, gw_in, gw_out, gvec,
    near0, near1, slots, terms0, terms1, *rest,
):
    bufs0, bufs1, rest = rest[:5], rest[5:10], rest[10:]
    msg_s, act_s, gproj_s, gpre_s, weights = rest[:5]
    sum_bufs, (send, recv, load) = rest[5:10], rest[10:]
    place = Place()
    across, along = RowGroup(place), ColGroup(place)
    width = nodes.shape[1]
    rows = nodes.shape[0]
    near, terms = (near0, near1), (terms0, terms1)

    mine = [
        pltpu.make_async_copy(
            nodes_any.at[:, :, pl.ds(h * 128, 128)],
            near[h].at[pl.ds(across.slot(0, 0) * 8, 8)],
            load.at[8 + h],
        )
        for h in (0, 1)
    ]
    for copy in mine:
        copy.start()

    def loader(ring, pair):
        at = pl.ds(along.slot(ring, pair) * 8, 8)
        return pltpu.make_async_copy(tiles.at[at], slots.at[at], load.at[ring * 2 + pair])

    for at in ORDER:
        loader(*at).start()
    greet(place.all_peers())
    wire = Wire(send, recv)
    for copy in mine:
        copy.wait()

    def mask(ring, pair):
        loader(ring, pair).wait()
        base = along.slot(ring, pair) * 8

        def one(i, carry):
            for k in range(4):
                keep = live[base + i, pl.ds(k, 1)].astype(BF16)
                slots[base + i, k] = slots[base + i, k] * keep
            return carry

        lax.fori_loop(0, 8, one, 0)

    def product(h, ring, pair):
        slot = along.slot(ring, pair)

        def one(j, carry):
            for u in range(2):
                i = slot * 8 + j * 2 + u
                left = jnp.concatenate([slots[i, k] for k in range(4)], axis=1)
                right = []
                for k in range(4):
                    right.append(near[h][cols[i, k]])
                at = pl.ds(pl.multiple_of((j * 2 + u) * 128, 128), 128)
                terms[h][slot, at] = dot(left, jnp.concatenate(right, axis=0)).astype(BF16)
            return carry

        lax.fori_loop(0, 4, one, 0)

    gather0 = gather(wire, across, near0, "n0", QUARTER, 8)
    gather1 = gather(wire, across, near1, "n1", QUARTER, 8)
    for step in range(5):
        next(gather0)
        for at in ORDER[2 * step : 2 * step + 2]:
            mask(*at)
    next(gather1)
    run(gather0)

    def prepare0(ring, pair):
        product(0, ring, pair)
        next(gather1, None)

    scatter0 = scatter(wire, along, terms0, bufs0, "s0", prepare0, QUARTER)
    for _ in range(4):
        next(scatter0)
    run(gather1)
    leaving = [
        pltpu.make_async_copy(near[h], out, load.at[10 + h])
        for h, out in ((0, near0_out), (1, near1_out))
    ]
    for copy in leaving:
        copy.start()
    scatter1 = scatter(
        wire, along, terms1, bufs1, "s1", lambda *at: product(1, *at), QUARTER
    )
    for _ in scatter1:
        next(scatter0, None)
    run(scatter0)
    own = along.slot(0, 0)
    gsum = weights.at[pl.ds(3 * width, 8)]
    weights[3 * width :] = jnp.zeros((weights.shape[0] - 3 * width, width), F32)

    def chunk(i, carry):
        at = pl.ds(pl.multiple_of(i * 256, 256), 256)
        msg = jnp.concatenate(
            [
                (
                    terms[h][own, at].astype(F32)
                    + bufs[2][0, at].astype(F32)
                    + bufs[3][0, at].astype(F32)
                    + bufs[4][0, at].astype(F32)
                ).astype(BF16)
                for h, bufs in ((0, bufs0), (1, bufs1))
            ],
            axis=1,
        )
        msg_s[at] = msg
        mine = nodes[at]
        pre = dot(mine, w_in[:width]) + dot(msg, w_in[width:]) + bias[...]
        sig = jax.nn.sigmoid(pre)
        act = (pre * sig).astype(BF16)
        act_s[at] = act
        proj = dot(act, w_out[...])
        mean = jnp.mean(proj, axis=-1, keepdims=True)
        off = proj - mean
        var = jnp.mean(off * off, axis=-1, keepdims=True)
        rstd = 1.0 / jnp.sqrt(var + EPS)
        normed = off * rstd
        updated[at] = (mine.astype(F32) + normed * gain[...] + shift[...]).astype(BF16)
        grad_out = cot[at].astype(F32)
        gscaled = grad_out * gain[...]
        gproj = (
            (
                gscaled
                - jnp.mean(gscaled, axis=-1, keepdims=True)
                - normed * jnp.mean(gscaled * normed, axis=-1, keepdims=True)
            )
            * rstd
        ).astype(BF16)
        gproj_s[at] = gproj
        gact = dot(gproj, w_out[...], ((1,), (1,)))
        gpre = gact * sig * (1.0 + pre * (1.0 - sig))
        gpre_b = gpre.astype(BF16)
        gpre_s[at] = gpre_b
        grads[own, at] = dot(gpre_b, w_in[width:], ((1,), (1,))).astype(BF16)
        direct[at] = grad_out + dot(gpre_b, w_in[:width], ((1,), (1,)))
        gsum[0:1] += jnp.sum(gpre, axis=0, keepdims=True)
        gsum[1:2] += jnp.sum(grad_out * normed, axis=0, keepdims=True)
        gsum[2:3] += jnp.sum(grad_out, axis=0, keepdims=True)
        return carry

    lax.fori_loop(0, rows // 256, chunk, 0)
    steps = gather(wire, along, grads, "g", MORE)
    next(steps)
    weights[:width] = dot(nodes[...], gpre_s[...], ((0,), (0,)))
    weights[width : 2 * width] = dot(msg_s[...], gpre_s[...], ((0,), (0,)))
    weights[2 * width : 3 * width] = dot(act_s[...], gproj_s[...], ((0,), (0,)))
    sums = total(wire, place, weights, sum_bufs, "w")
    for following in (sums, steps, sums, steps, sums, steps, steps, steps, sums, sums):
        next(following)
    run(steps)
    run(sums)
    result = sum_bufs[0]
    factor = F32(131072.0) ** F32(-0.5)
    gw_in[...] = result[: 2 * width] * factor
    gw_out[...] = result[2 * width : 3 * width] * factor
    gvec[...] = result[3 * width : 3 * width + 3] * factor
    for copy in leaving:
        copy.wait()
    wire.drain()


def middle(cols, live, tiles, nodes, cot, w_in, bias, w_out, gain, shift):
    rows, width = nodes.shape
    one = functools.partial(pltpu.VMEM, (rows, width))
    smem = pl.BlockSpec(memory_space=pltpu.SMEM)
    near = jax.ShapeDtypeStruct((128, 128, 128), BF16)
    return pl.pallas_call(
        middle_kernel,
        out_shape=[
            near,
            near,
            jax.ShapeDtypeStruct((8, rows, width), BF16),
            jax.ShapeDtypeStruct((rows, width), BF16),
            jax.ShapeDtypeStruct((rows, width), F32),
            jax.ShapeDtypeStruct((2 * width, width), F32),
            jax.ShapeDtypeStruct((width, width), F32),
            jax.ShapeDtypeStruct((3, width), F32),
        ],
        in_specs=[smem, VM, ANY, ANY] + [VM] * 7,
        out_specs=[ANY] * 2 + [VM] * 6,
        scratch_shapes=[pltpu.VMEM((128, 128, 128), BF16)] * 2
        + [pltpu.VMEM(tiles.shape, BF16)]
        + [pltpu.VMEM((8, rows, 128), BF16)] * 2
        + scatter_shapes(rows, 128) * 2
        + [one(BF16)] * 4
        + [pltpu.VMEM((TOTAL_ROWS, width), F32)]
        + total_shapes(width)
        + [
            pltpu.SemaphoreType.DMA((240,)),
            pltpu.SemaphoreType.DMA((240,)),
            pltpu.SemaphoreType.DMA((12,)),
        ],
        compiler_params=remote_params(2),
        name="middle",
    )(cols, live, tiles, nodes.reshape(8, 128, width), nodes, cot, w_in, bias, w_out, gain, shift)


def backward_kernel(
    cols, count, tiles, near0, near1, grads, updated_in, gw_in_in, gw_out_in, gvec_in,
    tile_grads, back, updated, gw_in, gw_out, gvec, acc,
):
    step = pl.program_id(0)
    per = tiles.shape[0]
    updated[...] = updated_in[...]
    gw_in[...] = gw_in_in[...]
    gw_out[...] = gw_out_in[...]
    gvec[...] = gvec_in[...]

    @pl.when(step == 0)
    def _():
        def clear(i, carry):
            acc[i] = jnp.zeros(acc.shape[1:], F32)
            return carry

        lax.fori_loop(0, acc.shape[0], clear, 0)

    scale = F32(256.0) ** F32(-0.5)

    def work(i, at, slots):
        live = count[at]
        grad = grads[pl.ds(i * 128, 128)]
        which = [cols[at, k] for k in range(slots)]
        picked = jnp.concatenate(
            [jnp.concatenate([near0[c], near1[c]], axis=1) for c in which], axis=0
        )
        made = (dot(grad, picked, ((1,), (1,))) * scale).astype(BF16)
        zero = jnp.zeros((128, 128), BF16)
        for k in range(slots):
            tile_grads[i, k] = jnp.where(k < live, made[:, k * 128 : k * 128 + 128], zero)
        kept = jnp.concatenate([jnp.where(k < live, tiles[i, k], zero) for k in range(slots)], axis=1)
        return which, dot(kept, grad, ((0,), (0,)))

    def both(i, slots):
        found = [work(i + u, step * per + i + u, slots) for u in (0, 1)]
        for which, terms in found:
            for k in range(slots):
                acc[which[k]] += terms[k * 128 : k * 128 + 128]

    for i in range(0, per, 2):
        most = jnp.maximum(count[step * per + i], count[step * per + i + 1])

        @pl.when(most <= 2)
        def _():
            for u in (0, 1):
                tile_grads[i + u, 2:4] = jnp.zeros((2, 128, 128), BF16)

        @pl.when(most <= 0)
        def _():
            for u in (0, 1):
                tile_grads[i + u, 0:2] = jnp.zeros((2, 128, 128), BF16)

        @pl.when((most > 0) & (most <= 2))
        def _():
            both(i, 2)

        @pl.when(most > 2)
        def _():
            both(i, 4)

    @pl.when(step == pl.num_programs(0) - 1)
    def _():
        def put(i, carry):
            back[i] = acc[i].astype(BF16)
            return carry

        lax.fori_loop(0, acc.shape[0], put, 0)


def backward(cols, count, tiles, near0, near1, grads, updated, gw_in, gw_out, gvec):
    row_blocks = tiles.shape[0]
    width = grads.shape[1]
    columns = (128, 128, width)
    near = pl.BlockSpec(near0.shape, lambda s, *_: (0, 0, 0), pipeline_mode=pl.Buffered(1))
    per = 8
    steps = row_blocks // per

    def cut(array):
        return pl.BlockSpec((array.shape[0] // steps, width), lambda s, *_: (s, 0))

    passed = [cut(updated), cut(gw_in), cut(gw_out), pl.BlockSpec((3, width), lambda s, *_: (0, 0))]
    return pl.pallas_call(
        backward_kernel,
        out_shape=[
            jax.ShapeDtypeStruct(tiles.shape, BF16),
            jax.ShapeDtypeStruct(columns, BF16),
        ]
        + [jax.ShapeDtypeStruct(a.shape, a.dtype) for a in (updated, gw_in, gw_out, gvec)],
        grid_spec=pltpu.PrefetchScalarGridSpec(
            num_scalar_prefetch=2,
            grid=(steps,),
            in_specs=[
                pl.BlockSpec((per, 4, 128, 128), lambda s, *_: (s, 0, 0, 0)),
                near,
                near,
                pl.BlockSpec((per * 128, width), lambda s, *_: (s, 0)),
            ]
            + passed,
            out_specs=[
                pl.BlockSpec((per, 4, 128, 128), lambda s, *_: (s, 0, 0, 0)),
                pl.BlockSpec(columns, lambda s, *_: (0, 0, 0), pipeline_mode=pl.Buffered(1)),
            ]
            + passed,
            scratch_shapes=[pltpu.VMEM(columns, F32)],
        ),
        compiler_params=pltpu.CompilerParams(vmem_limit_bytes=VMEM_LIMIT),
        name="backward",
    )(cols, count, tiles, near0, near1, grads, updated, gw_in, gw_out, gvec)


def finish_kernel(
    back, direct, out,
    terms, others, relay_m, relay_p, from_m, from_p, from_pair, send, recv, load,
):
    group = RowGroup(Place())
    rows = terms.shape[1]

    def loader(ring, pair):
        slot = group.slot(ring, pair)
        return pltpu.make_async_copy(back.at[slot], terms.at[slot], load.at[ring * 2 + pair])

    for at in ORDER:
        loader(*at).start()
    greet(list(group.peers.values()))
    wire = Wire(send, recv)
    for ring, pair in ORDER:
        wire.push(
            ("f", ring, pair),
            back.at[group.slot(ring, pair, 1)],
            others.at[ring * 2 + pair],
            group.peers["sib"],
        )

    def prepare(ring, pair):
        loader(ring, pair).wait()
        other = others.at[ring * 2 + pair]
        wire.take(("f", ring, pair), other, group.peers["sib"])
        slot = group.slot(ring, pair)

        def body(at):
            terms[slot, at] = (terms[slot, at].astype(F32) + other[at].astype(F32)).astype(BF16)

        add_rows(rows, 128, body)

    bufs = (relay_m, relay_p, from_m, from_p, from_pair)
    run(scatter(wire, group, terms, bufs, "b", prepare, MORE))
    own = group.slot(0, 0)

    def last(at):
        out[at] = (
            direct[at]
            + terms[own, at].astype(F32)
            + from_m[0, at].astype(F32)
            + from_p[0, at].astype(F32)
            + from_pair[0, at].astype(F32)
        ).astype(BF16)

    add_rows(rows, 128, last)
    wire.drain()


def finish(back, direct):
    rows, width = direct.shape
    return pl.pallas_call(
        finish_kernel,
        out_shape=jax.ShapeDtypeStruct((rows, width), BF16),
        in_specs=[ANY, VM],
        out_specs=VM,
        scratch_shapes=[
            pltpu.VMEM((16, rows, width), BF16),
            pltpu.VMEM((8, rows, width), BF16),
        ]
        + scatter_shapes(rows, width)
        + [
            pltpu.SemaphoreType.DMA((60,)),
            pltpu.SemaphoreType.DMA((60,)),
            pltpu.SemaphoreType.DMA((9,)),
        ],
        compiler_params=remote_params(3),
        name="finish",
    )(back.reshape(16, rows, width), direct)


def body(nodes, tiles, tile_col, tile_count, w_in, bias_in, w_out, ln_gain, ln_shift, cotangent):
    rows, width = nodes.shape
    cols, count = tile_col[:, 0], tile_count[:, 0]
    slots = tiles[:, 0]
    cols = jnp.clip(cols, 0, 127)
    live = lax.broadcasted_iota(jnp.int32, (64, 4, 128), 1) < count[:, None, None]
    live = live.astype(F32)
    near0, near1, grads, updated, direct, gw_in, gw_out, gvec = middle(
        cols, live, slots, nodes, cotangent, w_in, bias_in[None], w_out, ln_gain[None], ln_shift[None]
    )
    grad_tiles, back, updated, gw_in, gw_out, gvec = backward(
        cols, count, slots, near0, near1, grads.reshape(8 * rows, width), updated, gw_in, gw_out, gvec
    )
    grad_nodes = finish(back, direct)
    return updated, grad_nodes, grad_tiles[:, None], gw_in, gw_out, gvec


def solution(mesh):
    placed = (
        P(("row", "col"), None),
        P("row", "col", None, None, None),
        P("row", "col", None),
        P("row", "col"),
        P(),
        P(),
        P(),
        P(),
        P(),
        P(("row", "col"), None),
    )
    return jax.shard_map(
        body,
        mesh=mesh,
        in_specs=placed,
        out_specs=(
            P(("row", "col"), None),
            P(("row", "col"), None),
            P("row", "col", None, None, None),
            P(),
            P(),
            P(),
        ),
        check_vma=False,
    )
```

```python
import functools

import jax
import jax.numpy as jnp
from jax import lax
from jax.experimental import pallas as pl
from jax.experimental.pallas import tpu as pltpu
from jax.sharding import PartitionSpec as P

F32, BF16 = jnp.float32, jnp.bfloat16
MIB = 1024 * 1024
VMEM_LIMIT = 58 * MIB
EPS = 1e-05
TOTAL_ROWS = 1024


class Place:
    def __init__(self):
        self.row = lax.axis_index("row")
        self.col = lax.axis_index("col")
        self.x = lax.div(self.row, 4)
        self.zh = lax.rem(lax.div(self.row, 2), 2)
        self.core = lax.rem(self.row, 2)
        self.y = lax.div(self.col, 2)
        self.zl = lax.rem(self.col, 2)


    def peer(self, x=0, y=0, z=0, core=0):
        z_at = lax.rem(self.zh * 2 + self.zl + z, 4)
        row = lax.rem(self.x + x, 4) * 4 + lax.div(z_at, 2) * 2 + lax.rem(self.core + core, 2)
        return (row, lax.rem(self.y + y, 4) * 2 + lax.rem(z_at, 2))

    def all_peers(self):
        steps = [dict(core=1)] + [{axis: d} for axis in "xyz" for d in (1, 2, 3)]
        return [self.peer(**step) for step in steps]


class RowGroup:
    def __init__(self, place):
        self.place = place
        col = place.col
        self.peers = {
            "p": (self.slot(1, 0), col),
            "m": (self.slot(3, 0), col),
            "pair": (self.slot(0, 1), col),
            "sib": (self.slot(0, 0, 1), col),
        }

    def slot(self, ring, pair, sib=0):
        at = self.place
        return (
            lax.rem(at.x + ring, 4) * 4
            + lax.rem(at.zh + pair, 2) * 2
            + lax.rem(at.core + sib, 2)
        )


class ColGroup:
    def __init__(self, place):
        self.place = place
        row = place.row
        self.peers = {
            "p": (row, self.slot(1, 0)),
            "m": (row, self.slot(3, 0)),
            "pair": (row, self.slot(0, 1)),
        }

    def slot(self, ring, pair):
        at = self.place
        return lax.rem(at.y + ring, 4) * 2 + lax.rem(at.zl + pair, 2)


class Wire:
    def __init__(self, send, recv):
        self.send, self.recv = send, recv
        self.names = {}
        self.open = []

    def index(self, name):
        return self.names.setdefault(name, len(self.names))

    def push(self, name, src, dst, to):
        at = self.index(name)
        copy = pltpu.make_async_remote_copy(
            src_ref=src,
            dst_ref=dst,
            send_sem=self.send.at[at],
            recv_sem=self.recv.at[at],
            device_id=to,
            device_id_type=pl.DeviceIdType.MESH,
        )
        copy.start()
        self.open.append(copy)

    def take(self, name, dst, to):
        at = self.index(name)
        pltpu.make_async_remote_copy(
            src_ref=dst,
            dst_ref=dst,
            send_sem=self.send.at[at],
            recv_sem=self.recv.at[at],
            device_id=to,
            device_id_type=pl.DeviceIdType.MESH,
        ).wait_recv()

    def drain(self):
        for copy in self.open:
            copy.wait_send()
        self.open = []


def greet(devices):
    barrier = pltpu.get_barrier_semaphore()
    for device in devices:
        pl.semaphore_signal(barrier, inc=1, device_id=device, device_id_type=pl.DeviceIdType.MESH)
    pl.semaphore_wait(barrier, len(devices))


MOVES = {"p": (3, 0, 0), "m": (1, 0, 0), "pair": (0, 1, 0), "sib": (0, 0, 1)}


QUARTER = ((0, 3, False), (3, 3, False), (6, 1, True), (7, 1, True))
MORE = ((0, 3, False), (3, 2, False), (5, 1, True), (6, 2, True))


def gather(wire, group, buf, tag, parts, per=1):
    unit = buf.shape[1] // 8

    def view(slot, part):
        start, size, _ = parts[part]
        if per == 1:
            return buf.at[slot, pl.ds(start * unit, size * unit)]
        return buf.at[pl.ds(slot * per + start, size)]

    def whole(slot):
        return buf.at[slot] if per == 1 else buf.at[pl.ds(slot * per, per)]

    has_sib = "sib" in group.peers
    late = [c for c in range(4) if parts[c][2]]
    early = [c for c in range(4) if not parts[c][2]]

    def send(ring, pair, part, way):
        ref = view(group.slot(ring, pair), part)
        dr, dp, dk = MOVES[way]
        name = (tag, (ring + dr) % 4, (pair + dp) % 2, dk, part)
        wire.push(name, ref, ref, group.peers[way])

    def take(ring, pair, part):
        slot = group.slot(ring, pair)
        wire.take((tag, ring, pair, 0, part), view(slot, part), group.peers["p"])

    def share(ring, pair):
        if has_sib:
            ref = whole(group.slot(ring, pair))
            wire.push((tag, ring, pair, 1), ref, ref, group.peers["sib"])

    def relay(pair, which):
        for c in which:
            ring, way = ((3, "p"), (1, "m"))[c % 2]
            take(ring, pair, c)
            send(ring, pair, c, way)
            if c in late and pair == 0:
                send(ring, pair, c, "pair")

    def rest(pair, which):
        for c in which:
            ring = (1, 3)[c % 2]
            take(ring, pair, c)
            if c in late and pair == 0:
                send(ring, pair, c, "pair")

    for c in early:
        send(0, 0, c, "pair")
    for c in early + late:
        send(0, 0, c, ("p", "m")[c % 2])
    for c in early + late:
        send(0, 0, c, ("m", "p")[c % 2])
    for c in late:
        send(0, 0, c, "pair")
    share(0, 0)
    yield
    relay(0, early + late)
    yield
    for c in early:
        take(0, 1, c)
        send(0, 1, c, "p")
        send(0, 1, c, "m")
    yield
    rest(0, late + early)
    share(1, 0)
    share(3, 0)
    yield
    for c in late:
        take(2, 0, c)
        send(2, 0, c, "pair")
    relay(1, early)
    yield
    for c in early:
        take(2, 0, c)
    share(2, 0)
    for c in late:
        take(0, 1, c)
    share(0, 1)
    yield
    rest(1, early)
    for ring in (1, 3):
        for c in late:
            take(ring, 1, c)
        share(ring, 1)
    for c in early + late:
        take(2, 1, c)
    share(2, 1)
    yield
    if has_sib:
        for pair in (0, 1):
            for ring in (0, 1, 3, 2):
                slot = group.slot(ring, pair, 1)
                wire.take((tag, ring, pair, 1), whole(slot), group.peers["p"])


def add_rows(rows, step, body):
    def one(i, carry):
        body(pl.ds(pl.multiple_of(i * step, step), step))
        return carry

    lax.fori_loop(0, rows // step, one, 0)


def scatter_shapes(rows, width):
    return [
        pltpu.VMEM((2, rows, width), BF16),
        pltpu.VMEM((2, rows, width), BF16),
        pltpu.VMEM((2, rows, width), BF16),
        pltpu.VMEM((2, rows, width), BF16),
        pltpu.VMEM((4, rows, width), BF16),
    ]


def scatter(wire, group, terms, bufs, tag, prepare, parts):
    relay_m, relay_p, from_m, from_p, from_pair = bufs
    unit = terms.shape[1] // 8
    cut = [pl.ds(start * unit, size * unit) for start, size, _ in parts]
    late = [c for c in range(4) if parts[c][2]]
    early = [c for c in range(4) if not parts[c][2]]
    start = parts[late[0]][0]
    first = pl.ds(start * unit, sum(parts[c][1] for c in late) * unit)
    to_p, to_m, to_pair = group.peers["p"], group.peers["m"], group.peers["pair"]

    def at(ring, pair, rows):
        return terms.at[group.slot(ring, pair), rows]

    def add(target, *others):
        def body(rows):
            total = target[rows].astype(F32)
            for other in others:
                total = total + other[rows].astype(F32)
            target[rows] = total.astype(BF16)

        add_rows(target.shape[0], unit, body)

    def cross(ring):
        dst = from_pair.at[ring, first]
        wire.push((tag, "first", ring), at(ring, 1, first), dst, to_pair)

    def crossed(ring):
        src = from_pair.at[ring, first]
        wire.take((tag, "first", ring), src, to_pair)
        add(at(ring, 0, first), src)

    def far(q, which):
        for c in which:
            dst, to = ((relay_m, to_p), (relay_p, to_m))[c % 2]
            wire.push((tag, "far", q, c), at(2, q, cut[c]), dst.at[q, cut[c]], to)

    def single(q, which):
        for c in which:
            ring, dst, to = ((3, from_p, to_m), (1, from_m, to_p))[c % 2]
            wire.push((tag, "one", q, c), at(ring, q, cut[c]), dst.at[q, cut[c]], to)

    def double(q, which):
        for c in which:
            ring, via, dst, to = ((1, relay_m, from_m, to_p), (3, relay_p, from_p, to_m))[c % 2]
            wire.take((tag, "far", q, c), via.at[q, cut[c]], to)
            add(at(ring, q, cut[c]), via.at[q, cut[c]])
            wire.push((tag, "two", q, c), at(ring, q, cut[c]), dst.at[q, cut[c]], to)

    def arrive(q, which):
        for c in which:
            one, two = ((from_p, from_m), (from_m, from_p))[c % 2]
            wire.take((tag, "one", q, c), one.at[q, cut[c]], to_p)
            wire.take((tag, "two", q, c), two.at[q, cut[c]], to_p)

    prepare(2, 1)
    cross(2)
    far(1, early)
    prepare(2, 0)
    far(0, early)
    yield
    prepare(1, 1)
    cross(1)
    prepare(3, 1)
    cross(3)
    single(1, early)
    crossed(2)
    far(0, late)
    yield
    double(1, early)
    prepare(1, 0)
    prepare(3, 0)
    single(0, early)
    yield
    crossed(1)
    crossed(3)
    single(0, late)
    double(0, early + late)
    yield
    prepare(0, 1)
    cross(0)
    for c in early:
        arrive(1, [c])
        add(at(0, 1, cut[c]), from_m.at[1, cut[c]], from_p.at[1, cut[c]])
        wire.push((tag, "last", c), at(0, 1, cut[c]), from_pair.at[0, cut[c]], to_pair)
    yield
    prepare(0, 0)
    arrive(0, early + late)
    wire.take((tag, "first", 0), from_pair.at[0, first], to_pair)
    for c in early:
        wire.take((tag, "last", c), from_pair.at[0, cut[c]], to_pair)


def exchange(wire, tag, axis, place, part, dst):
    for d in (1, 2, 3):
        wire.push((tag, axis, d), part(d), dst(d), place.peer(**{axis: d}))


def block(index, rows):
    return pl.ds(pl.multiple_of(index * rows, rows), rows)


def total_near(wire, place, mine, result, in_core, in_x, tag):
    half, quarter = TOTAL_ROWS // 2, TOTAL_ROWS // 8
    core, x = place.core, place.x
    sib = place.peer(core=1)
    wire.push((tag, "core"), mine.at[block(1 - core, half)], in_core, sib)
    yield
    wire.take((tag, "core"), in_core, sib)

    def fold(i, carry):
        at = pl.ds(pl.multiple_of(core * half + i * 64, 64), 64)
        mine[at] += in_core[block(i, 64)]
        return carry

    lax.fori_loop(0, half // 64, fold, 0)

    def own(index):
        return mine.at[block(core * 4 + index, quarter)]

    exchange(
        wire, tag, "x", place, lambda d: own(lax.rem(x + d, 4)), lambda d: in_x.at[d - 1]
    )
    yield
    for d in (1, 2, 3):
        wire.take((tag, "x", d), in_x.at[d - 1], sib)
    at = block(x, quarter)
    result[at] = mine[block(core * 4 + x, quarter)] + in_x[0] + in_x[1] + in_x[2]
    exchange(wire, tag + "r", "x", place, lambda d: result.at[at], lambda d: result.at[at])
    yield
    for d in (1, 2, 3):
        wire.take((tag + "r", "x", d), result.at[block(lax.rem(x + 4 - d, 4), quarter)], sib)


def total_far(wire, place, mine, result, in_y, in_z, tag):
    quarter = TOTAL_ROWS // 8
    core, y = place.core, place.y
    z = place.zh * 2 + place.zl
    sib = place.peer(core=1)
    exchange(
        wire,
        tag,
        "y",
        place,
        lambda d: mine.at[block(lax.rem(y + d, 4), quarter)],
        lambda d: in_y.at[d - 1],
    )
    yield
    for d in (1, 2, 3):
        wire.take((tag, "y", d), in_y.at[d - 1], sib)
    in_z[z] = mine[block(y, quarter)] + in_y[0] + in_y[1] + in_y[2]
    exchange(wire, tag, "z", place, lambda d: in_z.at[z], lambda d: in_z.at[z])
    yield
    for d in (1, 2, 3):
        wire.take((tag, "z", d), in_z.at[lax.rem(z + 4 - d, 4)], sib)
    at = block(core * 4 + y, quarter)
    result[at] = in_z[0] + in_z[1] + in_z[2] + in_z[3]
    exchange(wire, tag + "r", "y", place, lambda d: result.at[at], lambda d: result.at[at])
    yield
    for d in (1, 2, 3):
        there = block(core * 4 + lax.rem(y + 4 - d, 4), quarter)
        wire.take((tag + "r", "y", d), result.at[there], sib)
    half = block(core, TOTAL_ROWS // 2)
    wire.push((tag, "join"), result.at[half], result.at[half], sib)
    yield
    wire.take((tag, "join"), result.at[block(1 - core, TOTAL_ROWS // 2)], sib)


def run(steps):
    for _ in steps:
        pass


def dot(a, b, dims=((1,), (0,))):
    return lax.dot_general(a, b, (dims, ((), ())), preferred_element_type=F32)


ANY = pl.BlockSpec(memory_space=pl.ANY)
VM = pl.BlockSpec(memory_space=pltpu.VMEM)


def remote_params(collective_id):
    return pltpu.CompilerParams(
        collective_id=collective_id, has_side_effects=True, vmem_limit_bytes=VMEM_LIMIT
    )


ORDER = [(2, 1), (2, 0), (1, 1), (3, 1), (1, 0), (3, 0), (0, 1), (0, 0)]


def middle_kernel(
    cols, live, tiles, nodes_any, nodes, cot, w_in, bias, w_out, gain, shift,
    near0_out, near1_out, grads, updated, direct, part_sum,
    near0, near1, slots, terms0, terms1, *rest,
):
    bufs0, bufs1, rest = rest[:5], rest[5:10], rest[10:]
    msg_s, act_s, gproj_s, gpre_s, weights, in_core, in_x, send, recv, load = rest
    place = Place()
    across, along = RowGroup(place), ColGroup(place)
    width = nodes.shape[1]
    rows = nodes.shape[0]
    near, terms = (near0, near1), (terms0, terms1)

    mine = [
        pltpu.make_async_copy(
            nodes_any.at[:, :, pl.ds(h * 128, 128)],
            near[h].at[pl.ds(across.slot(0, 0) * 8, 8)],
            load.at[8 + h],
        )
        for h in (0, 1)
    ]
    for copy in mine:
        copy.start()

    def loader(ring, pair):
        at = pl.ds(along.slot(ring, pair) * 8, 8)
        return pltpu.make_async_copy(tiles.at[at], slots.at[at], load.at[ring * 2 + pair])

    for at in ORDER:
        loader(*at).start()
    greet(place.all_peers())
    wire = Wire(send, recv)
    for copy in mine:
        copy.wait()

    def mask(ring, pair):
        loader(ring, pair).wait()
        base = along.slot(ring, pair) * 8

        def one(i, carry):
            for k in range(4):
                keep = live[base + i, pl.ds(k, 1)].astype(BF16)
                slots[base + i, k] = slots[base + i, k] * keep
            return carry

        lax.fori_loop(0, 8, one, 0)

    def product(h, ring, pair):
        slot = along.slot(ring, pair)

        def one(j, carry):
            for u in range(2):
                i = slot * 8 + j * 2 + u
                left = jnp.concatenate([slots[i, k] for k in range(4)], axis=1)
                right = []
                for k in range(4):
                    right.append(near[h][cols[i, k]])
                at = pl.ds(pl.multiple_of((j * 2 + u) * 128, 128), 128)
                terms[h][slot, at] = dot(left, jnp.concatenate(right, axis=0)).astype(BF16)
            return carry

        lax.fori_loop(0, 4, one, 0)

    gather0 = gather(wire, across, near0, "n0", QUARTER, 8)
    gather1 = gather(wire, across, near1, "n1", QUARTER, 8)
    for step in range(5):
        next(gather0)
        for at in ORDER[2 * step : 2 * step + 2]:
            mask(*at)
    next(gather1)
    run(gather0)

    def prepare0(ring, pair):
        product(0, ring, pair)
        next(gather1, None)

    scatter0 = scatter(wire, along, terms0, bufs0, "s0", prepare0, QUARTER)
    for _ in range(4):
        next(scatter0)
    run(gather1)
    leaving = [
        pltpu.make_async_copy(near[h], out, load.at[10 + h])
        for h, out in ((0, near0_out), (1, near1_out))
    ]
    for copy in leaving:
        copy.start()
    scatter1 = scatter(
        wire, along, terms1, bufs1, "s1", lambda *at: product(1, *at), QUARTER
    )
    for _ in scatter1:
        next(scatter0, None)
    run(scatter0)
    own = along.slot(0, 0)
    gsum = weights.at[pl.ds(3 * width, 8)]
    weights[3 * width :] = jnp.zeros((weights.shape[0] - 3 * width, width), F32)

    def chunk(i, carry):
        at = pl.ds(pl.multiple_of(i * 256, 256), 256)
        msg = jnp.concatenate(
            [
                (
                    terms[h][own, at].astype(F32)
                    + bufs[2][0, at].astype(F32)
                    + bufs[3][0, at].astype(F32)
                    + bufs[4][0, at].astype(F32)
                ).astype(BF16)
                for h, bufs in ((0, bufs0), (1, bufs1))
            ],
            axis=1,
        )
        msg_s[at] = msg
        mine = nodes[at]
        pre = dot(mine, w_in[:width]) + dot(msg, w_in[width:]) + bias[...]
        sig = jax.nn.sigmoid(pre)
        act = (pre * sig).astype(BF16)
        act_s[at] = act
        proj = dot(act, w_out[...])
        mean = jnp.mean(proj, axis=-1, keepdims=True)
        off = proj - mean
        var = jnp.mean(off * off, axis=-1, keepdims=True)
        rstd = 1.0 / jnp.sqrt(var + EPS)
        normed = off * rstd
        updated[at] = (mine.astype(F32) + normed * gain[...] + shift[...]).astype(BF16)
        grad_out = cot[at].astype(F32)
        gscaled = grad_out * gain[...]
        gproj = (
            (
                gscaled
                - jnp.mean(gscaled, axis=-1, keepdims=True)
                - normed * jnp.mean(gscaled * normed, axis=-1, keepdims=True)
            )
            * rstd
        ).astype(BF16)
        gproj_s[at] = gproj
        gact = dot(gproj, w_out[...], ((1,), (1,)))
        gpre = gact * sig * (1.0 + pre * (1.0 - sig))
        gpre_b = gpre.astype(BF16)
        gpre_s[at] = gpre_b
        grads[own, at] = dot(gpre_b, w_in[width:], ((1,), (1,))).astype(BF16)
        direct[at] = grad_out + dot(gpre_b, w_in[:width], ((1,), (1,)))
        gsum[0:1] += jnp.sum(gpre, axis=0, keepdims=True)
        gsum[1:2] += jnp.sum(grad_out * normed, axis=0, keepdims=True)
        gsum[2:3] += jnp.sum(grad_out, axis=0, keepdims=True)
        return carry

    lax.fori_loop(0, rows // 256, chunk, 0)
    steps = gather(wire, along, grads, "g", MORE)
    next(steps)
    weights[:width] = dot(nodes[...], gpre_s[...], ((0,), (0,)))
    weights[width : 2 * width] = dot(msg_s[...], gpre_s[...], ((0,), (0,)))
    weights[2 * width : 3 * width] = dot(act_s[...], gproj_s[...], ((0,), (0,)))
    sums = total_near(wire, place, weights, part_sum, in_core, in_x, "w")
    for following in (sums, steps, sums, steps, steps, sums, steps, steps):
        next(following)
    run(steps)
    run(sums)
    for copy in leaving:
        copy.wait()
    wire.drain()


def middle(cols, live, tiles, nodes, cot, w_in, bias, w_out, gain, shift):
    rows, width = nodes.shape
    one = functools.partial(pltpu.VMEM, (rows, width))
    smem = pl.BlockSpec(memory_space=pltpu.SMEM)
    near = jax.ShapeDtypeStruct((128, 128, 128), BF16)
    return pl.pallas_call(
        middle_kernel,
        out_shape=[
            near,
            near,
            jax.ShapeDtypeStruct((8, rows, width), BF16),
            jax.ShapeDtypeStruct((rows, width), BF16),
            jax.ShapeDtypeStruct((rows, width), F32),
            jax.ShapeDtypeStruct((TOTAL_ROWS // 2, width), F32),
        ],
        in_specs=[smem, VM, ANY, ANY] + [VM] * 7,
        out_specs=[ANY] * 2 + [VM] * 4,
        scratch_shapes=[pltpu.VMEM((128, 128, 128), BF16)] * 2
        + [pltpu.VMEM(tiles.shape, BF16)]
        + [pltpu.VMEM((8, rows, 128), BF16)] * 2
        + scatter_shapes(rows, 128) * 2
        + [one(BF16)] * 4
        + [
            pltpu.VMEM((TOTAL_ROWS, width), F32),
            pltpu.VMEM((TOTAL_ROWS // 2, width), F32),
            pltpu.VMEM((3, TOTAL_ROWS // 8, width), F32),
        ]
        + [
            pltpu.SemaphoreType.DMA((240,)),
            pltpu.SemaphoreType.DMA((240,)),
            pltpu.SemaphoreType.DMA((12,)),
        ],
        compiler_params=remote_params(2),
        name="middle",
    )(cols, live, tiles, nodes.reshape(8, 128, width), nodes, cot, w_in, bias, w_out, gain, shift)


def backward_kernel(
    cols, count, tiles, near0, near1, grads, updated_in, tile_grads, back, updated, acc
):
    step = pl.program_id(0)
    per = tiles.shape[0]
    updated[...] = updated_in[...]

    @pl.when(step == 0)
    def _():
        def clear(i, carry):
            acc[i] = jnp.zeros(acc.shape[1:], F32)
            return carry

        lax.fori_loop(0, acc.shape[0], clear, 0)

    scale = F32(256.0) ** F32(-0.5)

    def work(i, at, slots):
        live = count[at]
        grad = grads[pl.ds(i * 128, 128)]
        which = [cols[at, k] for k in range(slots)]
        picked = jnp.concatenate(
            [jnp.concatenate([near0[c], near1[c]], axis=1) for c in which], axis=0
        )
        made = (dot(grad, picked, ((1,), (1,))) * scale).astype(BF16)
        zero = jnp.zeros((128, 128), BF16)
        for k in range(slots):
            tile_grads[i, k] = jnp.where(k < live, made[:, k * 128 : k * 128 + 128], zero)
        kept = jnp.concatenate([jnp.where(k < live, tiles[i, k], zero) for k in range(slots)], axis=1)
        return which, dot(kept, grad, ((0,), (0,)))

    def both(i, slots):
        found = [work(i + u, step * per + i + u, slots) for u in (0, 1)]
        for which, terms in found:
            for k in range(slots):
                acc[which[k]] += terms[k * 128 : k * 128 + 128]

    for i in range(0, per, 2):
        most = jnp.maximum(count[step * per + i], count[step * per + i + 1])

        @pl.when(most <= 2)
        def _():
            for u in (0, 1):
                tile_grads[i + u, 2:4] = jnp.zeros((2, 128, 128), BF16)

        @pl.when(most <= 0)
        def _():
            for u in (0, 1):
                tile_grads[i + u, 0:2] = jnp.zeros((2, 128, 128), BF16)

        @pl.when((most > 0) & (most <= 2))
        def _():
            both(i, 2)

        @pl.when(most > 2)
        def _():
            both(i, 4)

    @pl.when(step == pl.num_programs(0) - 1)
    def _():
        def put(i, carry):
            back[i] = acc[i].astype(BF16)
            return carry

        lax.fori_loop(0, acc.shape[0], put, 0)


def backward(cols, count, tiles, near0, near1, grads, updated):
    row_blocks = tiles.shape[0]
    width = grads.shape[1]
    columns = (128, 128, width)
    near = pl.BlockSpec(near0.shape, lambda s, *_: (0, 0, 0), pipeline_mode=pl.Buffered(1))
    per = 8
    steps = row_blocks // per

    passed = [pl.BlockSpec((updated.shape[0] // steps, width), lambda s, *_: (s, 0))]
    return pl.pallas_call(
        backward_kernel,
        out_shape=[
            jax.ShapeDtypeStruct(tiles.shape, BF16),
            jax.ShapeDtypeStruct(columns, BF16),
            jax.ShapeDtypeStruct(updated.shape, BF16),
        ],
        grid_spec=pltpu.PrefetchScalarGridSpec(
            num_scalar_prefetch=2,
            grid=(steps,),
            in_specs=[
                pl.BlockSpec((per, 4, 128, 128), lambda s, *_: (s, 0, 0, 0)),
                near,
                near,
                pl.BlockSpec((per * 128, width), lambda s, *_: (s, 0)),
            ]
            + passed,
            out_specs=[
                pl.BlockSpec((per, 4, 128, 128), lambda s, *_: (s, 0, 0, 0)),
                pl.BlockSpec(columns, lambda s, *_: (0, 0, 0), pipeline_mode=pl.Buffered(1)),
            ]
            + passed,
            scratch_shapes=[pltpu.VMEM(columns, F32)],
        ),
        compiler_params=pltpu.CompilerParams(vmem_limit_bytes=VMEM_LIMIT),
        name="backward",
    )(cols, count, tiles, near0, near1, grads, updated)


def finish_kernel(
    back, direct, part_sum, out, result,
    terms, others, relay_m, relay_p, from_m, from_p, from_pair, mine, in_y, in_z, send, recv, load,
):
    place = Place()
    group = RowGroup(place)
    rows = terms.shape[1]

    def loader(ring, pair):
        slot = group.slot(ring, pair)
        return pltpu.make_async_copy(back.at[slot], terms.at[slot], load.at[ring * 2 + pair])

    held = pltpu.make_async_copy(part_sum, mine, load.at[8])
    held.start()
    for at in ORDER:
        loader(*at).start()
    greet(place.all_peers())
    wire = Wire(send, recv)
    held.wait()
    sums = total_far(wire, place, mine, result, in_y, in_z, "w")
    next(sums)
    for ring, pair in ORDER:
        wire.push(
            ("f", ring, pair),
            back.at[group.slot(ring, pair, 1)],
            others.at[ring * 2 + pair],
            group.peers["sib"],
        )

    def prepare(ring, pair):
        loader(ring, pair).wait()
        other = others.at[ring * 2 + pair]
        wire.take(("f", ring, pair), other, group.peers["sib"])
        slot = group.slot(ring, pair)

        def body(at):
            terms[slot, at] = (terms[slot, at].astype(F32) + other[at].astype(F32)).astype(BF16)

        add_rows(rows, 128, body)

    bufs = (relay_m, relay_p, from_m, from_p, from_pair)
    for point, _ in enumerate(scatter(wire, group, terms, bufs, "b", prepare, MORE)):
        if point in (0, 3, 4):
            next(sums)
    own = group.slot(0, 0)

    def last(at):
        out[at] = (
            direct[at]
            + terms[own, at].astype(F32)
            + from_m[0, at].astype(F32)
            + from_p[0, at].astype(F32)
            + from_pair[0, at].astype(F32)
        ).astype(BF16)

    add_rows(rows, 128, last)
    run(sums)
    wire.drain()


def finish(back, direct, part_sum):
    rows, width = direct.shape
    return pl.pallas_call(
        finish_kernel,
        out_shape=[
            jax.ShapeDtypeStruct((rows, width), BF16),
            jax.ShapeDtypeStruct((TOTAL_ROWS, width), F32),
        ],
        in_specs=[ANY, VM, ANY],
        out_specs=[VM] * 2,
        scratch_shapes=[
            pltpu.VMEM((16, rows, width), BF16),
            pltpu.VMEM((8, rows, width), BF16),
        ]
        + scatter_shapes(rows, width)
        + [
            pltpu.VMEM((TOTAL_ROWS // 2, width), F32),
            pltpu.VMEM((3, TOTAL_ROWS // 8, width), F32),
            pltpu.VMEM((4, TOTAL_ROWS // 8, width), F32),
            pltpu.SemaphoreType.DMA((60,)),
            pltpu.SemaphoreType.DMA((60,)),
            pltpu.SemaphoreType.DMA((9,)),
        ],
        compiler_params=remote_params(3),
        name="finish",
    )(back.reshape(16, rows, width), direct, part_sum)


def write_kernel(grad, sums, grad_nodes, gw_in, gw_out, gvec):
    width = gw_out.shape[1]
    factor = F32(131072.0) ** F32(-0.5)
    grad_nodes[...] = grad[...]
    gw_in[...] = sums[: 2 * width] * factor
    gw_out[...] = sums[2 * width : 3 * width] * factor
    gvec[...] = sums[3 * width : 3 * width + 3] * factor


def write(grad, sums):
    width = grad.shape[1]
    return pl.pallas_call(
        write_kernel,
        out_shape=[
            jax.ShapeDtypeStruct(grad.shape, BF16),
            jax.ShapeDtypeStruct((2 * width, width), F32),
            jax.ShapeDtypeStruct((width, width), F32),
            jax.ShapeDtypeStruct((3, width), F32),
        ],
        in_specs=[VM] * 2,
        out_specs=[VM] * 4,
        name="write",
    )(grad, sums)


def body(nodes, tiles, tile_col, tile_count, w_in, bias_in, w_out, ln_gain, ln_shift, cotangent):
    rows, width = nodes.shape
    cols, count = tile_col[:, 0], tile_count[:, 0]
    slots = tiles[:, 0]
    cols = jnp.clip(cols, 0, 127)
    live = lax.broadcasted_iota(jnp.int32, (64, 4, 128), 1) < count[:, None, None]
    live = live.astype(F32)
    near0, near1, grads, updated, direct, part_sum = middle(
        cols, live, slots, nodes, cotangent, w_in, bias_in[None], w_out, ln_gain[None], ln_shift[None]
    )
    grads = grads.reshape(8 * rows, width)
    grad_tiles, back, updated = backward(cols, count, slots, near0, near1, grads, updated)
    grad_nodes, gw_in, gw_out, gvec = write(*finish(back, direct, part_sum))
    return updated, grad_nodes, grad_tiles[:, None], gw_in, gw_out, gvec


def solution(mesh):
    placed = (
        P(("row", "col"), None),
        P("row", "col", None, None, None),
        P("row", "col", None),
        P("row", "col"),
        P(),
        P(),
        P(),
        P(),
        P(),
        P(("row", "col"), None),
    )
    return jax.shard_map(
        body,
        mesh=mesh,
        in_specs=placed,
        out_specs=(
            P(("row", "col"), None),
            P(("row", "col"), None),
            P("row", "col", None, None, None),
            P(),
            P(),
            P(),
        ),
        check_vma=False,
    )
```

```python
import functools

import jax
import jax.numpy as jnp
from jax import lax
from jax.experimental import pallas as pl
from jax.experimental.pallas import tpu as pltpu
from jax.sharding import PartitionSpec as P

F32, BF16 = jnp.float32, jnp.bfloat16
MIB = 1024 * 1024
VMEM_LIMIT = 58 * MIB
EPS = 1e-05
TOTAL_ROWS = 1024


class Place:
    def __init__(self):
        self.row = lax.axis_index("row")
        self.col = lax.axis_index("col")
        self.x = lax.div(self.row, 4)
        self.zh = lax.rem(lax.div(self.row, 2), 2)
        self.core = lax.rem(self.row, 2)
        self.y = lax.div(self.col, 2)
        self.zl = lax.rem(self.col, 2)


    def peer(self, x=0, y=0, z=0, core=0):
        z_at = lax.rem(self.zh * 2 + self.zl + z, 4)
        row = lax.rem(self.x + x, 4) * 4 + lax.div(z_at, 2) * 2 + lax.rem(self.core + core, 2)
        return (row, lax.rem(self.y + y, 4) * 2 + lax.rem(z_at, 2))

    def all_peers(self):
        steps = [dict(core=1)] + [{axis: d} for axis in "xyz" for d in (1, 2, 3)]
        return [self.peer(**step) for step in steps]


class RowGroup:
    def __init__(self, place):
        self.place = place
        col = place.col
        self.peers = {
            "p": (self.slot(1, 0), col),
            "m": (self.slot(3, 0), col),
            "pair": (self.slot(0, 1), col),
            "sib": (self.slot(0, 0, 1), col),
        }

    def slot(self, ring, pair, sib=0):
        at = self.place
        return (
            lax.rem(at.x + ring, 4) * 4
            + lax.rem(at.zh + pair, 2) * 2
            + lax.rem(at.core + sib, 2)
        )


class ColGroup:
    def __init__(self, place):
        self.place = place
        row = place.row
        self.peers = {
            "p": (row, self.slot(1, 0)),
            "m": (row, self.slot(3, 0)),
            "pair": (row, self.slot(0, 1)),
        }

    def slot(self, ring, pair):
        at = self.place
        return lax.rem(at.y + ring, 4) * 2 + lax.rem(at.zl + pair, 2)


class Wire:
    def __init__(self, send, recv):
        self.send, self.recv = send, recv
        self.names = {}
        self.open = []

    def index(self, name):
        return self.names.setdefault(name, len(self.names))

    def push(self, name, src, dst, to):
        at = self.index(name)
        copy = pltpu.make_async_remote_copy(
            src_ref=src,
            dst_ref=dst,
            send_sem=self.send.at[at],
            recv_sem=self.recv.at[at],
            device_id=to,
            device_id_type=pl.DeviceIdType.MESH,
        )
        copy.start()
        self.open.append(copy)

    def take(self, name, dst, to):
        at = self.index(name)
        pltpu.make_async_remote_copy(
            src_ref=dst,
            dst_ref=dst,
            send_sem=self.send.at[at],
            recv_sem=self.recv.at[at],
            device_id=to,
            device_id_type=pl.DeviceIdType.MESH,
        ).wait_recv()

    def drain(self):
        for copy in self.open:
            copy.wait_send()
        self.open = []


def greet(devices):
    barrier = pltpu.get_barrier_semaphore()
    for device in devices:
        pl.semaphore_signal(barrier, inc=1, device_id=device, device_id_type=pl.DeviceIdType.MESH)
    pl.semaphore_wait(barrier, len(devices))


MOVES = {"p": (3, 0, 0), "m": (1, 0, 0), "pair": (0, 1, 0), "sib": (0, 0, 1)}


QUARTER = ((0, 3, False), (3, 3, False), (6, 1, True), (7, 1, True))
MORE = ((0, 3, False), (3, 2, False), (5, 1, True), (6, 2, True))


def gather(wire, group, buf, tag, parts, per=1):
    unit = buf.shape[1] // 8

    def view(slot, part):
        start, size, _ = parts[part]
        if per == 1:
            return buf.at[slot, pl.ds(start * unit, size * unit)]
        return buf.at[pl.ds(slot * per + start, size)]

    def whole(slot):
        return buf.at[slot] if per == 1 else buf.at[pl.ds(slot * per, per)]

    has_sib = "sib" in group.peers
    late = [c for c in range(4) if parts[c][2]]
    early = [c for c in range(4) if not parts[c][2]]

    def send(ring, pair, part, way):
        ref = view(group.slot(ring, pair), part)
        dr, dp, dk = MOVES[way]
        name = (tag, (ring + dr) % 4, (pair + dp) % 2, dk, part)
        wire.push(name, ref, ref, group.peers[way])

    def take(ring, pair, part):
        slot = group.slot(ring, pair)
        wire.take((tag, ring, pair, 0, part), view(slot, part), group.peers["p"])

    def share(ring, pair):
        if has_sib:
            ref = whole(group.slot(ring, pair))
            wire.push((tag, ring, pair, 1), ref, ref, group.peers["sib"])

    def relay(pair, which):
        for c in which:
            ring, way = ((3, "p"), (1, "m"))[c % 2]
            take(ring, pair, c)
            send(ring, pair, c, way)
            if c in late and pair == 0:
                send(ring, pair, c, "pair")

    def rest(pair, which):
        for c in which:
            ring = (1, 3)[c % 2]
            take(ring, pair, c)
            if c in late and pair == 0:
                send(ring, pair, c, "pair")

    for c in early:
        send(0, 0, c, "pair")
    for c in early + late:
        send(0, 0, c, ("p", "m")[c % 2])
    for c in early + late:
        send(0, 0, c, ("m", "p")[c % 2])
    for c in late:
        send(0, 0, c, "pair")
    share(0, 0)
    yield
    relay(0, early + late)
    yield
    for c in early:
        take(0, 1, c)
        send(0, 1, c, "p")
        send(0, 1, c, "m")
    yield
    rest(0, late + early)
    share(1, 0)
    share(3, 0)
    yield
    for c in late:
        take(2, 0, c)
        send(2, 0, c, "pair")
    relay(1, early)
    yield
    for c in early:
        take(2, 0, c)
    share(2, 0)
    for c in late:
        take(0, 1, c)
    share(0, 1)
    yield
    rest(1, early)
    for ring in (1, 3):
        for c in late:
            take(ring, 1, c)
        share(ring, 1)
    for c in early + late:
        take(2, 1, c)
    share(2, 1)
    yield
    if has_sib:
        for pair in (0, 1):
            for ring in (0, 1, 3, 2):
                slot = group.slot(ring, pair, 1)
                wire.take((tag, ring, pair, 1), whole(slot), group.peers["p"])


def add_rows(rows, step, body):
    def one(i, carry):
        body(pl.ds(pl.multiple_of(i * step, step), step))
        return carry

    lax.fori_loop(0, rows // step, one, 0)


def scatter_shapes(rows, width):
    return [
        pltpu.VMEM((2, rows, width), BF16),
        pltpu.VMEM((2, rows, width), BF16),
        pltpu.VMEM((2, rows, width), BF16),
        pltpu.VMEM((2, rows, width), BF16),
        pltpu.VMEM((4, rows, width), BF16),
    ]


def scatter(wire, group, terms, bufs, tag, prepare, parts):
    relay_m, relay_p, from_m, from_p, from_pair = bufs
    unit = terms.shape[1] // 8
    cut = [pl.ds(start * unit, size * unit) for start, size, _ in parts]
    late = [c for c in range(4) if parts[c][2]]
    early = [c for c in range(4) if not parts[c][2]]
    start = parts[late[0]][0]
    first = pl.ds(start * unit, sum(parts[c][1] for c in late) * unit)
    to_p, to_m, to_pair = group.peers["p"], group.peers["m"], group.peers["pair"]

    def at(ring, pair, rows):
        return terms.at[group.slot(ring, pair), rows]

    def add(target, *others):
        def body(rows):
            total = target[rows].astype(F32)
            for other in others:
                total = total + other[rows].astype(F32)
            target[rows] = total.astype(BF16)

        add_rows(target.shape[0], unit, body)

    def cross(ring):
        dst = from_pair.at[ring, first]
        wire.push((tag, "first", ring), at(ring, 1, first), dst, to_pair)

    def crossed(ring):
        src = from_pair.at[ring, first]
        wire.take((tag, "first", ring), src, to_pair)
        add(at(ring, 0, first), src)

    def far(q, which):
        for c in which:
            dst, to = ((relay_m, to_p), (relay_p, to_m))[c % 2]
            wire.push((tag, "far", q, c), at(2, q, cut[c]), dst.at[q, cut[c]], to)

    def single(q, which):
        for c in which:
            ring, dst, to = ((3, from_p, to_m), (1, from_m, to_p))[c % 2]
            wire.push((tag, "one", q, c), at(ring, q, cut[c]), dst.at[q, cut[c]], to)

    def double(q, which):
        for c in which:
            ring, via, dst, to = ((1, relay_m, from_m, to_p), (3, relay_p, from_p, to_m))[c % 2]
            wire.take((tag, "far", q, c), via.at[q, cut[c]], to)
            add(at(ring, q, cut[c]), via.at[q, cut[c]])
            wire.push((tag, "two", q, c), at(ring, q, cut[c]), dst.at[q, cut[c]], to)

    def arrive(q, which):
        for c in which:
            one, two = ((from_p, from_m), (from_m, from_p))[c % 2]
            wire.take((tag, "one", q, c), one.at[q, cut[c]], to_p)
            wire.take((tag, "two", q, c), two.at[q, cut[c]], to_p)

    prepare(2, 1)
    cross(2)
    far(1, early)
    prepare(2, 0)
    far(0, early)
    yield
    prepare(1, 1)
    cross(1)
    prepare(3, 1)
    cross(3)
    single(1, early)
    crossed(2)
    far(0, late)
    yield
    double(1, early)
    prepare(1, 0)
    prepare(3, 0)
    single(0, early)
    yield
    crossed(1)
    crossed(3)
    single(0, late)
    double(0, early + late)
    yield
    prepare(0, 1)
    cross(0)
    for c in early:
        arrive(1, [c])
        add(at(0, 1, cut[c]), from_m.at[1, cut[c]], from_p.at[1, cut[c]])
        wire.push((tag, "last", c), at(0, 1, cut[c]), from_pair.at[0, cut[c]], to_pair)
    yield
    prepare(0, 0)
    arrive(0, early + late)
    wire.take((tag, "first", 0), from_pair.at[0, first], to_pair)
    for c in early:
        wire.take((tag, "last", c), from_pair.at[0, cut[c]], to_pair)


def exchange(wire, tag, axis, place, part, dst):
    for d in (1, 2, 3):
        wire.push((tag, axis, d), part(d), dst(d), place.peer(**{axis: d}))


def block(index, rows):
    return pl.ds(pl.multiple_of(index * rows, rows), rows)


def total_near(wire, place, mine, result, in_core, in_x, tag):
    half, quarter = TOTAL_ROWS // 2, TOTAL_ROWS // 8
    core, x = place.core, place.x
    sib = place.peer(core=1)
    wire.push((tag, "core"), mine.at[block(1 - core, half)], in_core, sib)
    yield
    wire.take((tag, "core"), in_core, sib)

    def fold(i, carry):
        at = pl.ds(pl.multiple_of(core * half + i * 64, 64), 64)
        mine[at] += in_core[block(i, 64)]
        return carry

    lax.fori_loop(0, half // 64, fold, 0)

    def own(index):
        return mine.at[block(core * 4 + index, quarter)]

    exchange(
        wire, tag, "x", place, lambda d: own(lax.rem(x + d, 4)), lambda d: in_x.at[d - 1]
    )
    yield
    for d in (1, 2, 3):
        wire.take((tag, "x", d), in_x.at[d - 1], sib)
    at = block(x, quarter)
    result[at] = mine[block(core * 4 + x, quarter)] + in_x[0] + in_x[1] + in_x[2]
    exchange(wire, tag + "r", "x", place, lambda d: result.at[at], lambda d: result.at[at])
    yield
    for d in (1, 2, 3):
        wire.take((tag + "r", "x", d), result.at[block(lax.rem(x + 4 - d, 4), quarter)], sib)


def total_far(wire, place, mine, result, in_y, in_z, tag):
    piece, quarter = TOTAL_ROWS // 32, TOTAL_ROWS // 8
    core, x, y = place.core, place.x, place.y
    z = place.zh * 2 + place.zl
    sib = place.peer(core=1)

    def at(x_at, y_at):
        return block(core * 16 + y_at * 4 + x_at, piece)

    exchange(
        wire,
        tag,
        "y",
        place,
        lambda d: mine.at[block(lax.rem(y + d, 4) * 4 + x, piece)],
        lambda d: in_y.at[d - 1],
    )
    yield
    for d in (1, 2, 3):
        wire.take((tag, "y", d), in_y.at[d - 1], sib)
    in_z[z] = mine[block(y * 4 + x, piece)] + in_y[0] + in_y[1] + in_y[2]
    exchange(wire, tag, "z", place, lambda d: in_z.at[z], lambda d: in_z.at[z])
    yield
    for d in (1, 2, 3):
        wire.take((tag, "z", d), in_z.at[lax.rem(z + 4 - d, 4)], sib)
    result[at(x, y)] = in_z[0] + in_z[1] + in_z[2] + in_z[3]
    own = result.at[at(x, y)]
    exchange(wire, tag + "r", "x", place, lambda d: own, lambda d: own)
    yield
    for d in (1, 2, 3):
        wire.take((tag + "r", "x", d), result.at[at(lax.rem(x + 4 - d, 4), y)], sib)
    four = result.at[block(core * 4 + y, quarter)]
    exchange(wire, tag + "r", "y", place, lambda d: four, lambda d: four)
    yield
    for d in (1, 2, 3):
        there = block(core * 4 + lax.rem(y + 4 - d, 4), quarter)
        wire.take((tag + "r", "y", d), result.at[there], sib)
    half = block(core, TOTAL_ROWS // 2)
    wire.push((tag, "join"), result.at[half], result.at[half], sib)
    yield
    wire.take((tag, "join"), result.at[block(1 - core, TOTAL_ROWS // 2)], sib)


def run(steps):
    for _ in steps:
        pass


def dot(a, b, dims=((1,), (0,))):
    return lax.dot_general(a, b, (dims, ((), ())), preferred_element_type=F32)


ANY = pl.BlockSpec(memory_space=pl.ANY)
VM = pl.BlockSpec(memory_space=pltpu.VMEM)


def remote_params(collective_id):
    return pltpu.CompilerParams(
        collective_id=collective_id, has_side_effects=True, vmem_limit_bytes=VMEM_LIMIT
    )


ORDER = [(2, 1), (2, 0), (1, 1), (3, 1), (1, 0), (3, 0), (0, 1), (0, 0)]


def middle_kernel(
    cols, live, tiles, nodes_any, nodes, cot, w_in, bias, w_out, gain, shift,
    near0_out, near1_out, grads, updated, direct, part_sum,
    near0, near1, slots, terms0, terms1, *rest,
):
    bufs0, bufs1, rest = rest[:5], rest[5:10], rest[10:]
    msg_s, act_s, gproj_s, gpre_s, weights, in_core, in_x, send, recv, load = rest
    place = Place()
    across, along = RowGroup(place), ColGroup(place)
    width = nodes.shape[1]
    rows = nodes.shape[0]
    near, terms = (near0, near1), (terms0, terms1)

    mine = [
        pltpu.make_async_copy(
            nodes_any.at[:, :, pl.ds(h * 128, 128)],
            near[h].at[pl.ds(across.slot(0, 0) * 8, 8)],
            load.at[8 + h],
        )
        for h in (0, 1)
    ]
    for copy in mine:
        copy.start()

    def loader(ring, pair):
        at = pl.ds(along.slot(ring, pair) * 8, 8)
        return pltpu.make_async_copy(tiles.at[at], slots.at[at], load.at[ring * 2 + pair])

    for at in ORDER:
        loader(*at).start()
    greet(place.all_peers())
    wire = Wire(send, recv)
    for copy in mine:
        copy.wait()

    def mask(ring, pair):
        loader(ring, pair).wait()
        base = along.slot(ring, pair) * 8

        def one(i, carry):
            held = jnp.broadcast_to(live[pl.ds(base + i, 1)], (1, 128))
            for k in range(4):
                keep = (held > k).astype(F32).astype(BF16)
                slots[base + i, k] = slots[base + i, k] * keep
            return carry

        lax.fori_loop(0, 8, one, 0)

    def product(h, ring, pair):
        slot = along.slot(ring, pair)

        def one(j, carry):
            for u in range(2):
                i = slot * 8 + j * 2 + u
                left = jnp.concatenate([slots[i, k] for k in range(4)], axis=1)
                right = []
                for k in range(4):
                    right.append(near[h][cols[i, k]])
                at = pl.ds(pl.multiple_of((j * 2 + u) * 128, 128), 128)
                terms[h][slot, at] = dot(left, jnp.concatenate(right, axis=0)).astype(BF16)
            return carry

        lax.fori_loop(0, 4, one, 0)

    gather0 = gather(wire, across, near0, "n0", QUARTER, 8)
    gather1 = gather(wire, across, near1, "n1", QUARTER, 8)
    for step in range(5):
        next(gather0)
        for at in ORDER[2 * step : 2 * step + 2]:
            mask(*at)
    next(gather1)
    run(gather0)

    def prepare0(ring, pair):
        product(0, ring, pair)
        next(gather1, None)

    scatter0 = scatter(wire, along, terms0, bufs0, "s0", prepare0, QUARTER)
    for _ in range(4):
        next(scatter0)
    run(gather1)
    leaving = [
        pltpu.make_async_copy(near[h], out, load.at[10 + h])
        for h, out in ((0, near0_out), (1, near1_out))
    ]
    for copy in leaving:
        copy.start()
    scatter1 = scatter(
        wire, along, terms1, bufs1, "s1", lambda *at: product(1, *at), QUARTER
    )
    for _ in scatter1:
        next(scatter0, None)
    run(scatter0)
    own = along.slot(0, 0)
    gsum = weights.at[pl.ds(3 * width, 8)]
    weights[3 * width :] = jnp.zeros((weights.shape[0] - 3 * width, width), F32)

    def chunk(i, carry):
        at = pl.ds(pl.multiple_of(i * 256, 256), 256)
        msg = jnp.concatenate(
            [
                (
                    terms[h][own, at].astype(F32)
                    + bufs[2][0, at].astype(F32)
                    + bufs[3][0, at].astype(F32)
                    + bufs[4][0, at].astype(F32)
                ).astype(BF16)
                for h, bufs in ((0, bufs0), (1, bufs1))
            ],
            axis=1,
        )
        msg_s[at] = msg
        mine = nodes[at]
        pre = dot(mine, w_in[:width]) + dot(msg, w_in[width:]) + bias[...]
        sig = jax.nn.sigmoid(pre)
        act = (pre * sig).astype(BF16)
        act_s[at] = act
        proj = dot(act, w_out[...])
        mean = jnp.mean(proj, axis=-1, keepdims=True)
        off = proj - mean
        var = jnp.mean(off * off, axis=-1, keepdims=True)
        rstd = 1.0 / jnp.sqrt(var + EPS)
        normed = off * rstd
        updated[at] = (mine.astype(F32) + normed * gain[...] + shift[...]).astype(BF16)
        grad_out = cot[at].astype(F32)
        gscaled = grad_out * gain[...]
        gproj = (
            (
                gscaled
                - jnp.mean(gscaled, axis=-1, keepdims=True)
                - normed * jnp.mean(gscaled * normed, axis=-1, keepdims=True)
            )
            * rstd
        ).astype(BF16)
        gproj_s[at] = gproj
        gact = dot(gproj, w_out[...], ((1,), (1,)))
        gpre = gact * sig * (1.0 + pre * (1.0 - sig))
        gpre_b = gpre.astype(BF16)
        gpre_s[at] = gpre_b
        grads[own, at] = dot(gpre_b, w_in[width:], ((1,), (1,))).astype(BF16)
        direct[at] = grad_out + dot(gpre_b, w_in[:width], ((1,), (1,)))
        gsum[0:1] += jnp.sum(gpre, axis=0, keepdims=True)
        gsum[1:2] += jnp.sum(grad_out * normed, axis=0, keepdims=True)
        gsum[2:3] += jnp.sum(grad_out, axis=0, keepdims=True)
        return carry

    lax.fori_loop(0, rows // 256, chunk, 0)
    steps = gather(wire, along, grads, "g", MORE)
    next(steps)
    weights[:width] = dot(nodes[...], gpre_s[...], ((0,), (0,)))
    weights[width : 2 * width] = dot(msg_s[...], gpre_s[...], ((0,), (0,)))
    weights[2 * width : 3 * width] = dot(act_s[...], gproj_s[...], ((0,), (0,)))
    sums = total_near(wire, place, weights, part_sum, in_core, in_x, "w")
    for following in (sums, steps, sums, steps, steps, sums, steps, steps):
        next(following)
    run(steps)
    run(sums)
    for copy in leaving:
        copy.wait()
    wire.drain()


def middle(cols, live, tiles, nodes, cot, w_in, bias, w_out, gain, shift):
    rows, width = nodes.shape
    one = functools.partial(pltpu.VMEM, (rows, width))
    smem = pl.BlockSpec(memory_space=pltpu.SMEM)
    near = jax.ShapeDtypeStruct((128, 128, 128), BF16)
    return pl.pallas_call(
        middle_kernel,
        out_shape=[
            near,
            near,
            jax.ShapeDtypeStruct((8, rows, width), BF16),
            jax.ShapeDtypeStruct((rows, width), BF16),
            jax.ShapeDtypeStruct((rows, width), F32),
            jax.ShapeDtypeStruct((TOTAL_ROWS // 2, width), F32),
        ],
        in_specs=[smem, VM, ANY, ANY] + [VM] * 7,
        out_specs=[ANY] * 2 + [VM] * 4,
        scratch_shapes=[pltpu.VMEM((128, 128, 128), BF16)] * 2
        + [pltpu.VMEM(tiles.shape, BF16)]
        + [pltpu.VMEM((8, rows, 128), BF16)] * 2
        + scatter_shapes(rows, 128) * 2
        + [one(BF16)] * 4
        + [
            pltpu.VMEM((TOTAL_ROWS, width), F32),
            pltpu.VMEM((TOTAL_ROWS // 2, width), F32),
            pltpu.VMEM((3, TOTAL_ROWS // 8, width), F32),
        ]
        + [
            pltpu.SemaphoreType.DMA((240,)),
            pltpu.SemaphoreType.DMA((240,)),
            pltpu.SemaphoreType.DMA((12,)),
        ],
        compiler_params=remote_params(2),
        name="middle",
    )(cols, live, tiles, nodes.reshape(8, 128, width), nodes, cot, w_in, bias, w_out, gain, shift)


def backward_kernel(
    cols, count, tiles, near0_any, near1_any, grads, updated_in,
    tile_grads, back_any, updated,
    acc, near0, near1, back, load, leave,
):
    step = pl.program_id(0)
    per = tiles.shape[0]
    updated[...] = updated_in[...]

    @pl.when(step == 0)
    def _():
        copies = [
            pltpu.make_async_copy(near0_any, near0, load.at[0]),
            pltpu.make_async_copy(near1_any, near1, load.at[1]),
        ]
        for copy in copies:
            copy.start()

        def clear(i, carry):
            acc[i] = jnp.zeros(acc.shape[1:], F32)
            return carry

        lax.fori_loop(0, acc.shape[0], clear, 0)
        for copy in copies:
            copy.wait()

    scale = F32(256.0) ** F32(-0.5)

    def work(i, at, slots):
        live = count[at]
        grad = grads[pl.ds(i * 128, 128)]
        which = [cols[at, k] for k in range(slots)]
        picked = jnp.concatenate(
            [jnp.concatenate([near0[c], near1[c]], axis=1) for c in which], axis=0
        )
        made = (dot(grad, picked, ((1,), (1,))) * scale).astype(BF16)
        zero = jnp.zeros((128, 128), BF16)
        for k in range(slots):
            tile_grads[i, k] = jnp.where(k < live, made[:, k * 128 : k * 128 + 128], zero)
        kept = jnp.concatenate([jnp.where(k < live, tiles[i, k], zero) for k in range(slots)], axis=1)
        return which, dot(kept, grad, ((0,), (0,)))

    def both(i, slots):
        found = [work(i + u, step * per + i + u, slots) for u in (0, 1)]
        for which, terms in found:
            for k in range(slots):
                acc[which[k]] += terms[k * 128 : k * 128 + 128]

    for i in range(0, per, 2):
        most = jnp.maximum(count[step * per + i], count[step * per + i + 1])

        @pl.when(most <= 2)
        def _():
            for u in (0, 1):
                tile_grads[i + u, 2:4] = jnp.zeros((2, 128, 128), BF16)

        @pl.when(most <= 0)
        def _():
            for u in (0, 1):
                tile_grads[i + u, 0:2] = jnp.zeros((2, 128, 128), BF16)

        @pl.when((most > 0) & (most <= 2))
        def _():
            both(i, 2)

        @pl.when(most > 2)
        def _():
            both(i, 4)

    @pl.when(step == pl.num_programs(0) - 1)
    def _():
        def put(i, carry):
            back[i] = acc[i].astype(BF16)
            return carry

        copies = []
        for part in range(8):
            lax.fori_loop(part * 16, part * 16 + 16, put, 0)
            at = pl.ds(part * 16, 16)
            copies.append(pltpu.make_async_copy(back.at[at], back_any.at[at], leave.at[part]))
            copies[-1].start()
        for copy in copies:
            copy.wait()


def backward(cols, count, tiles, near0, near1, grads, updated):
    row_blocks = tiles.shape[0]
    width = grads.shape[1]
    columns = (128, 128, width)
    per = 8
    steps = row_blocks // per

    passed = [pl.BlockSpec((updated.shape[0] // steps, width), lambda s, *_: (s, 0))]
    return pl.pallas_call(
        backward_kernel,
        out_shape=[
            jax.ShapeDtypeStruct(tiles.shape, BF16),
            jax.ShapeDtypeStruct(columns, BF16),
            jax.ShapeDtypeStruct(updated.shape, BF16),
        ],
        grid_spec=pltpu.PrefetchScalarGridSpec(
            num_scalar_prefetch=2,
            grid=(steps,),
            in_specs=[
                pl.BlockSpec((per, 4, 128, 128), lambda s, *_: (s, 0, 0, 0)),
                ANY,
                ANY,
                pl.BlockSpec((per * 128, width), lambda s, *_: (s, 0)),
            ]
            + passed,
            out_specs=[
                pl.BlockSpec((per, 4, 128, 128), lambda s, *_: (s, 0, 0, 0)),
                ANY,
            ]
            + passed,
            scratch_shapes=[
                pltpu.VMEM(columns, F32),
                pltpu.VMEM(near0.shape, BF16),
                pltpu.VMEM(near1.shape, BF16),
                pltpu.VMEM(columns, BF16),
                pltpu.SemaphoreType.DMA((2,)),
                pltpu.SemaphoreType.DMA((8,)),
            ],
        ),
        compiler_params=pltpu.CompilerParams(vmem_limit_bytes=VMEM_LIMIT),
        name="backward",
    )(cols, count, tiles, near0, near1, grads, updated)


def finish_kernel(
    back, direct, part_sum, out, result,
    terms, others, relay_m, relay_p, from_m, from_p, from_pair, mine, in_y, in_z, send, recv, load,
):
    place = Place()
    group = RowGroup(place)
    rows = terms.shape[1]

    def loader(ring, pair):
        slot = group.slot(ring, pair)
        return pltpu.make_async_copy(back.at[slot], terms.at[slot], load.at[ring * 2 + pair])

    held = pltpu.make_async_copy(part_sum, mine, load.at[8])
    held.start()
    for at in ORDER:
        loader(*at).start()
    greet(place.all_peers())
    wire = Wire(send, recv)
    held.wait()
    sums = total_far(wire, place, mine, result, in_y, in_z, "w")
    next(sums)
    for ring, pair in ORDER:
        wire.push(
            ("f", ring, pair),
            back.at[group.slot(ring, pair, 1)],
            others.at[ring * 2 + pair],
            group.peers["sib"],
        )

    def prepare(ring, pair):
        loader(ring, pair).wait()
        other = others.at[ring * 2 + pair]
        wire.take(("f", ring, pair), other, group.peers["sib"])
        slot = group.slot(ring, pair)

        def body(at):
            terms[slot, at] = (terms[slot, at].astype(F32) + other[at].astype(F32)).astype(BF16)

        add_rows(rows, 128, body)

    bufs = (relay_m, relay_p, from_m, from_p, from_pair)
    for point, _ in enumerate(scatter(wire, group, terms, bufs, "b", prepare, MORE)):
        if point in (0, 1, 3, 4):
            next(sums)
    own = group.slot(0, 0)

    def last(at):
        out[at] = (
            direct[at]
            + terms[own, at].astype(F32)
            + from_m[0, at].astype(F32)
            + from_p[0, at].astype(F32)
            + from_pair[0, at].astype(F32)
        ).astype(BF16)

    add_rows(rows, 128, last)
    run(sums)
    wire.drain()


def finish(back, direct, part_sum):
    rows, width = direct.shape
    return pl.pallas_call(
        finish_kernel,
        out_shape=[
            jax.ShapeDtypeStruct((rows, width), BF16),
            jax.ShapeDtypeStruct((TOTAL_ROWS, width), F32),
        ],
        in_specs=[ANY, VM, ANY],
        out_specs=[VM] * 2,
        scratch_shapes=[
            pltpu.VMEM((16, rows, width), BF16),
            pltpu.VMEM((8, rows, width), BF16),
        ]
        + scatter_shapes(rows, width)
        + [
            pltpu.VMEM((TOTAL_ROWS // 2, width), F32),
            pltpu.VMEM((3, TOTAL_ROWS // 32, width), F32),
            pltpu.VMEM((4, TOTAL_ROWS // 32, width), F32),
            pltpu.SemaphoreType.DMA((60,)),
            pltpu.SemaphoreType.DMA((60,)),
            pltpu.SemaphoreType.DMA((9,)),
        ],
        compiler_params=remote_params(3),
        name="finish",
    )(back.reshape(16, rows, width), direct, part_sum)


def write_kernel(grad, sums, grad_nodes, gw_in, gw_out, gvec):
    width = gw_out.shape[1]
    factor = F32(131072.0) ** F32(-0.5)
    grad_nodes[...] = grad[...]
    gw_in[...] = sums[: 2 * width] * factor
    gw_out[...] = sums[2 * width : 3 * width] * factor
    gvec[...] = sums[3 * width : 3 * width + 3] * factor


def write(grad, sums):
    width = grad.shape[1]
    return pl.pallas_call(
        write_kernel,
        out_shape=[
            jax.ShapeDtypeStruct(grad.shape, BF16),
            jax.ShapeDtypeStruct((2 * width, width), F32),
            jax.ShapeDtypeStruct((width, width), F32),
            jax.ShapeDtypeStruct((3, width), F32),
        ],
        in_specs=[VM] * 2,
        out_specs=[VM] * 4,
        name="write",
    )(grad, sums)


def body(nodes, tiles, tile_col, tile_count, w_in, bias_in, w_out, ln_gain, ln_shift, cotangent):
    rows, width = nodes.shape
    cols, count = tile_col[:, 0], tile_count[:, 0]
    slots = tiles[:, 0]
    cols = jnp.clip(cols, 0, 127)
    near0, near1, grads, updated, direct, part_sum = middle(
        cols, tile_count, slots, nodes, cotangent, w_in, bias_in[None], w_out, ln_gain[None], ln_shift[None]
    )
    grads = grads.reshape(8 * rows, width)
    grad_tiles, back, updated = backward(cols, count, slots, near0, near1, grads, updated)
    grad_nodes, gw_in, gw_out, gvec = write(*finish(back, direct, part_sum))
    return updated, grad_nodes, grad_tiles[:, None], gw_in, gw_out, gvec


def solution(mesh):
    placed = (
        P(("row", "col"), None),
        P("row", "col", None, None, None),
        P("row", "col", None),
        P("row", "col"),
        P(),
        P(),
        P(),
        P(),
        P(),
        P(("row", "col"), None),
    )
    return jax.shard_map(
        body,
        mesh=mesh,
        in_specs=placed,
        out_specs=(
            P(("row", "col"), None),
            P(("row", "col"), None),
            P("row", "col", None, None, None),
            P(),
            P(),
            P(),
        ),
        check_vma=False,
    )
```

```python
import functools

import jax
import jax.numpy as jnp
from jax import lax
from jax.experimental import pallas as pl
from jax.experimental.pallas import tpu as pltpu
from jax.sharding import PartitionSpec as P

F32, BF16 = jnp.float32, jnp.bfloat16
MIB = 1024 * 1024
VMEM_LIMIT = 58 * MIB
EPS = 1e-05
TOTAL_ROWS = 1024


class Place:
    def __init__(self):
        self.row = lax.axis_index("row")
        self.col = lax.axis_index("col")
        self.x = lax.div(self.row, 4)
        self.zh = lax.rem(lax.div(self.row, 2), 2)
        self.core = lax.rem(self.row, 2)
        self.y = lax.div(self.col, 2)
        self.zl = lax.rem(self.col, 2)


    def peer(self, x=0, y=0, z=0, core=0):
        z_at = lax.rem(self.zh * 2 + self.zl + z, 4)
        row = lax.rem(self.x + x, 4) * 4 + lax.div(z_at, 2) * 2 + lax.rem(self.core + core, 2)
        return (row, lax.rem(self.y + y, 4) * 2 + lax.rem(z_at, 2))

    def all_peers(self):
        steps = [dict(core=1)] + [{axis: d} for axis in "xyz" for d in (1, 2, 3)]
        return [self.peer(**step) for step in steps]


class RowGroup:
    def __init__(self, place):
        self.place = place
        col = place.col
        self.peers = {
            "p": (self.slot(1, 0), col),
            "m": (self.slot(3, 0), col),
            "pair": (self.slot(0, 1), col),
            "sib": (self.slot(0, 0, 1), col),
        }

    def slot(self, ring, pair, sib=0):
        at = self.place
        return (
            lax.rem(at.x + ring, 4) * 4
            + lax.rem(at.zh + pair, 2) * 2
            + lax.rem(at.core + sib, 2)
        )


class ColGroup:
    def __init__(self, place):
        self.place = place
        row = place.row
        self.peers = {
            "p": (row, self.slot(1, 0)),
            "m": (row, self.slot(3, 0)),
            "pair": (row, self.slot(0, 1)),
        }

    def slot(self, ring, pair):
        at = self.place
        return lax.rem(at.y + ring, 4) * 2 + lax.rem(at.zl + pair, 2)


class Wire:
    def __init__(self, send, recv):
        self.send, self.recv = send, recv
        self.names = {}
        self.open = []

    def index(self, name):
        return self.names.setdefault(name, len(self.names))

    def push(self, name, src, dst, to):
        at = self.index(name)
        copy = pltpu.make_async_remote_copy(
            src_ref=src,
            dst_ref=dst,
            send_sem=self.send.at[at],
            recv_sem=self.recv.at[at],
            device_id=to,
            device_id_type=pl.DeviceIdType.MESH,
        )
        copy.start()
        self.open.append(copy)

    def take(self, name, dst, to):
        at = self.index(name)
        pltpu.make_async_remote_copy(
            src_ref=dst,
            dst_ref=dst,
            send_sem=self.send.at[at],
            recv_sem=self.recv.at[at],
            device_id=to,
            device_id_type=pl.DeviceIdType.MESH,
        ).wait_recv()

    def drain(self):
        for copy in self.open:
            copy.wait_send()
        self.open = []


def greet(devices):
    barrier = pltpu.get_barrier_semaphore()
    for device in devices:
        pl.semaphore_signal(barrier, inc=1, device_id=device, device_id_type=pl.DeviceIdType.MESH)
    pl.semaphore_wait(barrier, len(devices))


MOVES = {"p": (3, 0, 0), "m": (1, 0, 0), "pair": (0, 1, 0), "sib": (0, 0, 1)}


QUARTER = ((0, 3, False), (3, 3, False), (6, 1, True), (7, 1, True))
MORE = ((0, 3, False), (3, 2, False), (5, 1, True), (6, 2, True))


def gather(wire, group, buf, tag, parts, per=1):
    unit = buf.shape[1] // 8

    def view(slot, part):
        start, size, _ = parts[part]
        if per == 1:
            return buf.at[slot, pl.ds(start * unit, size * unit)]
        return buf.at[pl.ds(slot * per + start, size)]

    def whole(slot):
        return buf.at[slot] if per == 1 else buf.at[pl.ds(slot * per, per)]

    has_sib = "sib" in group.peers
    late = [c for c in range(4) if parts[c][2]]
    early = [c for c in range(4) if not parts[c][2]]

    def send(ring, pair, part, way):
        ref = view(group.slot(ring, pair), part)
        dr, dp, dk = MOVES[way]
        name = (tag, (ring + dr) % 4, (pair + dp) % 2, dk, part)
        wire.push(name, ref, ref, group.peers[way])

    def take(ring, pair, part):
        slot = group.slot(ring, pair)
        wire.take((tag, ring, pair, 0, part), view(slot, part), group.peers["p"])

    def share(ring, pair):
        if has_sib:
            ref = whole(group.slot(ring, pair))
            wire.push((tag, ring, pair, 1), ref, ref, group.peers["sib"])

    def relay(pair, which):
        for c in which:
            ring, way = ((3, "p"), (1, "m"))[c % 2]
            take(ring, pair, c)
            send(ring, pair, c, way)
            if c in late and pair == 0:
                send(ring, pair, c, "pair")

    def rest(pair, which):
        for c in which:
            ring = (1, 3)[c % 2]
            take(ring, pair, c)
            if c in late and pair == 0:
                send(ring, pair, c, "pair")

    for c in early:
        send(0, 0, c, "pair")
    for c in early + late:
        send(0, 0, c, ("p", "m")[c % 2])
    for c in early + late:
        send(0, 0, c, ("m", "p")[c % 2])
    for c in late:
        send(0, 0, c, "pair")
    share(0, 0)
    yield
    relay(0, early + late)
    yield
    for c in early:
        take(0, 1, c)
        send(0, 1, c, "p")
        send(0, 1, c, "m")
    yield
    rest(0, late + early)
    share(1, 0)
    share(3, 0)
    yield
    for c in late:
        take(2, 0, c)
        send(2, 0, c, "pair")
    relay(1, early)
    yield
    for c in early:
        take(2, 0, c)
    share(2, 0)
    for c in late:
        take(0, 1, c)
    share(0, 1)
    yield
    rest(1, early)
    for ring in (1, 3):
        for c in late:
            take(ring, 1, c)
        share(ring, 1)
    for c in early + late:
        take(2, 1, c)
    share(2, 1)
    yield
    if has_sib:
        for pair in (0, 1):
            for ring in (0, 1, 3, 2):
                slot = group.slot(ring, pair, 1)
                wire.take((tag, ring, pair, 1), whole(slot), group.peers["p"])


def add_rows(rows, step, body):
    def one(i, carry):
        body(pl.ds(pl.multiple_of(i * step, step), step))
        return carry

    lax.fori_loop(0, rows // step, one, 0)


def scatter_shapes(rows, width):
    return [
        pltpu.VMEM((2, rows, width), BF16),
        pltpu.VMEM((2, rows, width), BF16),
        pltpu.VMEM((2, rows, width), BF16),
        pltpu.VMEM((2, rows, width), BF16),
        pltpu.VMEM((4, rows, width), BF16),
    ]


def scatter(wire, group, terms, bufs, tag, prepare, parts):
    relay_m, relay_p, from_m, from_p, from_pair = bufs
    unit = terms.shape[1] // 8
    cut = [pl.ds(start * unit, size * unit) for start, size, _ in parts]
    late = [c for c in range(4) if parts[c][2]]
    early = [c for c in range(4) if not parts[c][2]]
    start = parts[late[0]][0]
    first = pl.ds(start * unit, sum(parts[c][1] for c in late) * unit)
    to_p, to_m, to_pair = group.peers["p"], group.peers["m"], group.peers["pair"]

    def at(ring, pair, rows):
        return terms.at[group.slot(ring, pair), rows]

    def add(target, *others):
        def body(rows):
            total = target[rows].astype(F32)
            for other in others:
                total = total + other[rows].astype(F32)
            target[rows] = total.astype(BF16)

        add_rows(target.shape[0], unit, body)

    def cross(ring):
        dst = from_pair.at[ring, first]
        wire.push((tag, "first", ring), at(ring, 1, first), dst, to_pair)

    def crossed(ring):
        src = from_pair.at[ring, first]
        wire.take((tag, "first", ring), src, to_pair)
        add(at(ring, 0, first), src)

    def far(q, which):
        for c in which:
            dst, to = ((relay_m, to_p), (relay_p, to_m))[c % 2]
            wire.push((tag, "far", q, c), at(2, q, cut[c]), dst.at[q, cut[c]], to)

    def single(q, which):
        for c in which:
            ring, dst, to = ((3, from_p, to_m), (1, from_m, to_p))[c % 2]
            wire.push((tag, "one", q, c), at(ring, q, cut[c]), dst.at[q, cut[c]], to)

    def double(q, which):
        for c in which:
            ring, via, dst, to = ((1, relay_m, from_m, to_p), (3, relay_p, from_p, to_m))[c % 2]
            wire.take((tag, "far", q, c), via.at[q, cut[c]], to)
            add(at(ring, q, cut[c]), via.at[q, cut[c]])
            wire.push((tag, "two", q, c), at(ring, q, cut[c]), dst.at[q, cut[c]], to)

    def arrive(q, which):
        for c in which:
            one, two = ((from_p, from_m), (from_m, from_p))[c % 2]
            wire.take((tag, "one", q, c), one.at[q, cut[c]], to_p)
            wire.take((tag, "two", q, c), two.at[q, cut[c]], to_p)

    prepare(2, 1)
    cross(2)
    far(1, early)
    prepare(2, 0)
    far(0, early)
    yield
    prepare(1, 1)
    cross(1)
    prepare(3, 1)
    cross(3)
    single(1, early)
    crossed(2)
    far(0, late)
    yield
    double(1, early)
    prepare(1, 0)
    prepare(3, 0)
    single(0, early)
    yield
    crossed(1)
    crossed(3)
    single(0, late)
    double(0, early + late)
    yield
    prepare(0, 1)
    cross(0)
    for c in early:
        arrive(1, [c])
        add(at(0, 1, cut[c]), from_m.at[1, cut[c]], from_p.at[1, cut[c]])
        wire.push((tag, "last", c), at(0, 1, cut[c]), from_pair.at[0, cut[c]], to_pair)
    yield
    prepare(0, 0)
    arrive(0, early + late)
    wire.take((tag, "first", 0), from_pair.at[0, first], to_pair)
    for c in early:
        wire.take((tag, "last", c), from_pair.at[0, cut[c]], to_pair)


def exchange(wire, tag, axis, place, part, dst):
    for d in (1, 2, 3):
        wire.push((tag, axis, d), part(d), dst(d), place.peer(**{axis: d}))


def block(index, rows):
    return pl.ds(pl.multiple_of(index * rows, rows), rows)


def total_near(wire, place, mine, result, in_core, in_x, tag):
    half, quarter = TOTAL_ROWS // 2, TOTAL_ROWS // 8
    core, x = place.core, place.x
    sib = place.peer(core=1)
    wire.push((tag, "core"), mine.at[block(1 - core, half)], in_core, sib)
    yield
    wire.take((tag, "core"), in_core, sib)

    def fold(i, carry):
        at = pl.ds(pl.multiple_of(core * half + i * 64, 64), 64)
        mine[at] += in_core[block(i, 64)]
        return carry

    lax.fori_loop(0, half // 64, fold, 0)

    def own(index):
        return mine.at[block(core * 4 + index, quarter)]

    exchange(
        wire, tag, "x", place, lambda d: own(lax.rem(x + d, 4)), lambda d: in_x.at[d - 1]
    )
    yield
    for d in (1, 2, 3):
        wire.take((tag, "x", d), in_x.at[d - 1], sib)
    at = block(x, quarter)
    result[at] = mine[block(core * 4 + x, quarter)] + in_x[0] + in_x[1] + in_x[2]
    exchange(wire, tag + "r", "x", place, lambda d: result.at[at], lambda d: result.at[at])
    yield
    for d in (1, 2, 3):
        wire.take((tag + "r", "x", d), result.at[block(lax.rem(x + 4 - d, 4), quarter)], sib)


def total_far(wire, place, mine, result, in_y, in_z, tag):
    piece, quarter = TOTAL_ROWS // 32, TOTAL_ROWS // 8
    core, x, y = place.core, place.x, place.y
    z = place.zh * 2 + place.zl
    sib = place.peer(core=1)

    def at(x_at, y_at):
        return block(core * 16 + y_at * 4 + x_at, piece)

    exchange(
        wire,
        tag,
        "y",
        place,
        lambda d: mine.at[block(lax.rem(y + d, 4) * 4 + x, piece)],
        lambda d: in_y.at[d - 1],
    )
    yield
    for d in (1, 2, 3):
        wire.take((tag, "y", d), in_y.at[d - 1], sib)
    in_z[z] = mine[block(y * 4 + x, piece)] + in_y[0] + in_y[1] + in_y[2]
    exchange(wire, tag, "z", place, lambda d: in_z.at[z], lambda d: in_z.at[z])
    yield
    for d in (1, 2, 3):
        wire.take((tag, "z", d), in_z.at[lax.rem(z + 4 - d, 4)], sib)
    result[at(x, y)] = in_z[0] + in_z[1] + in_z[2] + in_z[3]
    own = result.at[at(x, y)]
    exchange(wire, tag + "r", "x", place, lambda d: own, lambda d: own)
    yield
    for d in (1, 2, 3):
        wire.take((tag + "r", "x", d), result.at[at(lax.rem(x + 4 - d, 4), y)], sib)
    four = result.at[block(core * 4 + y, quarter)]
    exchange(wire, tag + "r", "y", place, lambda d: four, lambda d: four)
    yield
    for d in (1, 2, 3):
        there = block(core * 4 + lax.rem(y + 4 - d, 4), quarter)
        wire.take((tag + "r", "y", d), result.at[there], sib)
    half = block(core, TOTAL_ROWS // 2)
    wire.push((tag, "join"), result.at[half], result.at[half], sib)
    yield
    wire.take((tag, "join"), result.at[block(1 - core, TOTAL_ROWS // 2)], sib)


def run(steps):
    for _ in steps:
        pass


def dot(a, b, dims=((1,), (0,))):
    return lax.dot_general(a, b, (dims, ((), ())), preferred_element_type=F32)


ANY = pl.BlockSpec(memory_space=pl.ANY)
VM = pl.BlockSpec(memory_space=pltpu.VMEM)


def remote_params(collective_id):
    return pltpu.CompilerParams(
        collective_id=collective_id, has_side_effects=True, vmem_limit_bytes=VMEM_LIMIT
    )


ORDER = [(2, 1), (2, 0), (1, 1), (3, 1), (1, 0), (3, 0), (0, 1), (0, 0)]


def middle_kernel(
    cols, live, tiles, nodes_any, nodes, cot, w_in, bias, w_out, gain, shift,
    near0_out, near1_out, grads, updated, direct, part_sum,
    near0, near1, slots, terms0, terms1, *rest,
):
    bufs0, bufs1, rest = rest[:5], rest[5:10], rest[10:]
    msg_s, act_s, gproj_s, gpre_s, weights, in_core, in_x, send, recv, load = rest
    place = Place()
    across, along = RowGroup(place), ColGroup(place)
    width = nodes.shape[1]
    rows = nodes.shape[0]
    near, terms = (near0, near1), (terms0, terms1)

    mine = [
        pltpu.make_async_copy(
            nodes_any.at[:, :, pl.ds(h * 128, 128)],
            near[h].at[pl.ds(across.slot(0, 0) * 8, 8)],
            load.at[8 + h],
        )
        for h in (0, 1)
    ]
    for copy in mine:
        copy.start()

    def loader(ring, pair):
        at = pl.ds(along.slot(ring, pair) * 8, 8)
        return pltpu.make_async_copy(tiles.at[at], slots.at[at], load.at[ring * 2 + pair])

    for at in ORDER:
        loader(*at).start()
    greet(place.all_peers())
    wire = Wire(send, recv)
    for copy in mine:
        copy.wait()

    def mask(ring, pair):
        loader(ring, pair).wait()
        base = along.slot(ring, pair) * 8

        def one(i, carry):
            held = jnp.full((1, 128), live[base + i], jnp.int32)
            for k in range(4):
                keep = (held > k).astype(F32).astype(BF16)
                slots[base + i, k] = slots[base + i, k] * keep
            return carry

        lax.fori_loop(0, 8, one, 0)

    def product(h, ring, pair):
        slot = along.slot(ring, pair)

        def one(j, carry):
            for u in range(2):
                i = slot * 8 + j * 2 + u
                left = jnp.concatenate([slots[i, k] for k in range(4)], axis=1)
                right = []
                for k in range(4):
                    right.append(near[h][cols[i, k]])
                at = pl.ds(pl.multiple_of((j * 2 + u) * 128, 128), 128)
                terms[h][slot, at] = dot(left, jnp.concatenate(right, axis=0)).astype(BF16)
            return carry

        lax.fori_loop(0, 4, one, 0)

    gather0 = gather(wire, across, near0, "n0", MORE, 8)
    gather1 = gather(wire, across, near1, "n1", QUARTER, 8)
    next(gather0)
    for at in ORDER:
        mask(*at)
    for _ in range(4):
        next(gather0)
    next(gather1)
    run(gather0)

    def prepare0(ring, pair):
        product(0, ring, pair)
        next(gather1, None)

    scatter0 = scatter(wire, along, terms0, bufs0, "s0", prepare0, MORE)
    for _ in range(4):
        next(scatter0)
    run(gather1)
    leaving = [
        pltpu.make_async_copy(near[h], out, load.at[10 + h])
        for h, out in ((0, near0_out), (1, near1_out))
    ]
    for copy in leaving:
        copy.start()
    scatter1 = scatter(
        wire, along, terms1, bufs1, "s1", lambda *at: product(1, *at), MORE
    )
    for _ in scatter1:
        next(scatter0, None)
    run(scatter0)
    own = along.slot(0, 0)
    gsum = weights.at[pl.ds(3 * width, 8)]
    weights[3 * width :] = jnp.zeros((weights.shape[0] - 3 * width, width), F32)

    def chunk(i, carry):
        at = pl.ds(pl.multiple_of(i * 256, 256), 256)
        msg = jnp.concatenate(
            [
                (
                    terms[h][own, at].astype(F32)
                    + bufs[2][0, at].astype(F32)
                    + bufs[3][0, at].astype(F32)
                    + bufs[4][0, at].astype(F32)
                ).astype(BF16)
                for h, bufs in ((0, bufs0), (1, bufs1))
            ],
            axis=1,
        )
        msg_s[at] = msg
        mine = nodes[at]
        pre = dot(mine, w_in[:width]) + dot(msg, w_in[width:]) + bias[...]
        sig = jax.nn.sigmoid(pre)
        act = (pre * sig).astype(BF16)
        act_s[at] = act
        proj = dot(act, w_out[...])
        mean = jnp.mean(proj, axis=-1, keepdims=True)
        off = proj - mean
        var = jnp.mean(off * off, axis=-1, keepdims=True)
        rstd = 1.0 / jnp.sqrt(var + EPS)
        normed = off * rstd
        updated[at] = (mine.astype(F32) + normed * gain[...] + shift[...]).astype(BF16)
        grad_out = cot[at].astype(F32)
        gscaled = grad_out * gain[...]
        gproj = (
            (
                gscaled
                - jnp.mean(gscaled, axis=-1, keepdims=True)
                - normed * jnp.mean(gscaled * normed, axis=-1, keepdims=True)
            )
            * rstd
        ).astype(BF16)
        gproj_s[at] = gproj
        gact = dot(gproj, w_out[...], ((1,), (1,)))
        gpre = gact * sig * (1.0 + pre * (1.0 - sig))
        gpre_b = gpre.astype(BF16)
        gpre_s[at] = gpre_b
        grads[own, at] = dot(gpre_b, w_in[width:], ((1,), (1,))).astype(BF16)
        direct[at] = grad_out + dot(gpre_b, w_in[:width], ((1,), (1,)))
        gsum[0:1] += jnp.sum(gpre, axis=0, keepdims=True)
        gsum[1:2] += jnp.sum(grad_out * normed, axis=0, keepdims=True)
        gsum[2:3] += jnp.sum(grad_out, axis=0, keepdims=True)
        return carry

    lax.fori_loop(0, rows // 256, chunk, 0)
    steps = gather(wire, along, grads, "g", MORE)
    next(steps)
    weights[:width] = dot(nodes[...], gpre_s[...], ((0,), (0,)))
    weights[width : 2 * width] = dot(msg_s[...], gpre_s[...], ((0,), (0,)))
    weights[2 * width : 3 * width] = dot(act_s[...], gproj_s[...], ((0,), (0,)))
    sums = total_near(wire, place, weights, part_sum, in_core, in_x, "w")
    for following in (sums, steps, sums, steps, steps, sums, steps, steps):
        next(following)
    run(steps)
    run(sums)
    for copy in leaving:
        copy.wait()
    wire.drain()


def middle(cols, live, tiles, nodes, cot, w_in, bias, w_out, gain, shift):
    rows, width = nodes.shape
    one = functools.partial(pltpu.VMEM, (rows, width))
    smem = pl.BlockSpec(memory_space=pltpu.SMEM)
    near = jax.ShapeDtypeStruct((128, 128, 128), BF16)
    return pl.pallas_call(
        middle_kernel,
        out_shape=[
            near,
            near,
            jax.ShapeDtypeStruct((8, rows, width), BF16),
            jax.ShapeDtypeStruct((rows, width), BF16),
            jax.ShapeDtypeStruct((rows, width), F32),
            jax.ShapeDtypeStruct((TOTAL_ROWS // 2, width), F32),
        ],
        in_specs=[smem, smem, ANY, ANY] + [VM] * 7,
        out_specs=[ANY] * 2 + [VM] * 4,
        scratch_shapes=[pltpu.VMEM((128, 128, 128), BF16)] * 2
        + [pltpu.VMEM(tiles.shape, BF16)]
        + [pltpu.VMEM((8, rows, 128), BF16)] * 2
        + scatter_shapes(rows, 128) * 2
        + [one(BF16)] * 4
        + [
            pltpu.VMEM((TOTAL_ROWS, width), F32),
            pltpu.VMEM((TOTAL_ROWS // 2, width), F32),
            pltpu.VMEM((3, TOTAL_ROWS // 8, width), F32),
        ]
        + [
            pltpu.SemaphoreType.DMA((240,)),
            pltpu.SemaphoreType.DMA((240,)),
            pltpu.SemaphoreType.DMA((12,)),
        ],
        compiler_params=remote_params(2),
        name="middle",
    )(cols, live, tiles, nodes.reshape(8, 128, width), nodes, cot, w_in, bias, w_out, gain, shift)


def backward_kernel(
    cols, count, tiles, near0_any, near1_any, grads, updated_in,
    tile_grads, back_any, updated,
    acc, near0, near1, back, load, leave,
):
    step = pl.program_id(0)
    per = tiles.shape[0]
    updated[...] = updated_in[...]

    @pl.when(step == 0)
    def _():
        copies = [
            pltpu.make_async_copy(near0_any, near0, load.at[0]),
            pltpu.make_async_copy(near1_any, near1, load.at[1]),
        ]
        for copy in copies:
            copy.start()

        def clear(i, carry):
            acc[i] = jnp.zeros(acc.shape[1:], F32)
            return carry

        lax.fori_loop(0, acc.shape[0], clear, 0)
        for copy in copies:
            copy.wait()

    scale = F32(256.0) ** F32(-0.5)

    def work(i, at, slots):
        live = count[at]
        grad = grads[pl.ds(i * 128, 128)]
        which = [cols[at, k] for k in range(slots)]
        picked = jnp.concatenate(
            [jnp.concatenate([near0[c], near1[c]], axis=1) for c in which], axis=0
        )
        made = (dot(grad, picked, ((1,), (1,))) * scale).astype(BF16)
        zero = jnp.zeros((128, 128), BF16)
        for k in range(slots):
            tile_grads[i, k] = jnp.where(k < live, made[:, k * 128 : k * 128 + 128], zero)
        kept = jnp.concatenate([jnp.where(k < live, tiles[i, k], zero) for k in range(slots)], axis=1)
        return which, dot(kept, grad, ((0,), (0,)))

    def both(i, slots):
        found = [work(i + u, step * per + i + u, slots) for u in (0, 1)]
        for which, terms in found:
            for k in range(slots):
                acc[which[k]] += terms[k * 128 : k * 128 + 128]

    for i in range(0, per, 2):
        most = jnp.maximum(count[step * per + i], count[step * per + i + 1])

        @pl.when(most <= 2)
        def _():
            for u in (0, 1):
                tile_grads[i + u, 2:4] = jnp.zeros((2, 128, 128), BF16)

        @pl.when(most <= 0)
        def _():
            for u in (0, 1):
                tile_grads[i + u, 0:2] = jnp.zeros((2, 128, 128), BF16)

        @pl.when((most > 0) & (most <= 2))
        def _():
            both(i, 2)

        @pl.when(most > 2)
        def _():
            both(i, 4)

    @pl.when(step == pl.num_programs(0) - 1)
    def _():
        def put(i, carry):
            back[i] = acc[i].astype(BF16)
            return carry

        copies = []
        for part in range(8):
            lax.fori_loop(part * 16, part * 16 + 16, put, 0)
            at = pl.ds(part * 16, 16)
            copies.append(pltpu.make_async_copy(back.at[at], back_any.at[at], leave.at[part]))
            copies[-1].start()
        for copy in copies:
            copy.wait()


def backward(cols, count, tiles, near0, near1, grads, updated):
    row_blocks = tiles.shape[0]
    width = grads.shape[1]
    columns = (128, 128, width)
    per = 8
    steps = row_blocks // per

    passed = [pl.BlockSpec((updated.shape[0] // steps, width), lambda s, *_: (s, 0))]
    return pl.pallas_call(
        backward_kernel,
        out_shape=[
            jax.ShapeDtypeStruct(tiles.shape, BF16),
            jax.ShapeDtypeStruct(columns, BF16),
            jax.ShapeDtypeStruct(updated.shape, BF16),
        ],
        grid_spec=pltpu.PrefetchScalarGridSpec(
            num_scalar_prefetch=2,
            grid=(steps,),
            in_specs=[
                pl.BlockSpec((per, 4, 128, 128), lambda s, *_: (s, 0, 0, 0)),
                ANY,
                ANY,
                pl.BlockSpec((per * 128, width), lambda s, *_: (s, 0)),
            ]
            + passed,
            out_specs=[
                pl.BlockSpec((per, 4, 128, 128), lambda s, *_: (s, 0, 0, 0)),
                ANY,
            ]
            + passed,
            scratch_shapes=[
                pltpu.VMEM(columns, F32),
                pltpu.VMEM(near0.shape, BF16),
                pltpu.VMEM(near1.shape, BF16),
                pltpu.VMEM(columns, BF16),
                pltpu.SemaphoreType.DMA((2,)),
                pltpu.SemaphoreType.DMA((8,)),
            ],
        ),
        compiler_params=pltpu.CompilerParams(vmem_limit_bytes=VMEM_LIMIT),
        name="backward",
    )(cols, count, tiles, near0, near1, grads, updated)


def finish_kernel(
    back, direct, part_sum, out, result,
    terms, others, relay_m, relay_p, from_m, from_p, from_pair, mine, in_y, in_z, send, recv, load,
):
    place = Place()
    group = RowGroup(place)
    rows = terms.shape[1]

    def loader(ring, pair):
        slot = group.slot(ring, pair)
        return pltpu.make_async_copy(back.at[slot], terms.at[slot], load.at[ring * 2 + pair])

    held = pltpu.make_async_copy(part_sum, mine, load.at[8])
    held.start()
    for at in ORDER:
        loader(*at).start()
    greet(place.all_peers())
    wire = Wire(send, recv)
    held.wait()
    sums = total_far(wire, place, mine, result, in_y, in_z, "w")
    next(sums)
    for ring, pair in ORDER:
        wire.push(
            ("f", ring, pair),
            back.at[group.slot(ring, pair, 1)],
            others.at[ring * 2 + pair],
            group.peers["sib"],
        )

    def prepare(ring, pair):
        loader(ring, pair).wait()
        other = others.at[ring * 2 + pair]
        wire.take(("f", ring, pair), other, group.peers["sib"])
        slot = group.slot(ring, pair)

        def body(at):
            terms[slot, at] = (terms[slot, at].astype(F32) + other[at].astype(F32)).astype(BF16)

        add_rows(rows, 128, body)

    bufs = (relay_m, relay_p, from_m, from_p, from_pair)
    for point, _ in enumerate(scatter(wire, group, terms, bufs, "b", prepare, MORE)):
        if point in (0, 1, 3, 4):
            next(sums)
    own = group.slot(0, 0)

    def last(at):
        out[at] = (
            direct[at]
            + terms[own, at].astype(F32)
            + from_m[0, at].astype(F32)
            + from_p[0, at].astype(F32)
            + from_pair[0, at].astype(F32)
        ).astype(BF16)

    add_rows(rows, 128, last)
    run(sums)
    wire.drain()


def finish(back, direct, part_sum):
    rows, width = direct.shape
    return pl.pallas_call(
        finish_kernel,
        out_shape=[
            jax.ShapeDtypeStruct((rows, width), BF16),
            jax.ShapeDtypeStruct((TOTAL_ROWS, width), F32),
        ],
        in_specs=[ANY, VM, ANY],
        out_specs=[VM] * 2,
        scratch_shapes=[
            pltpu.VMEM((16, rows, width), BF16),
            pltpu.VMEM((8, rows, width), BF16),
        ]
        + scatter_shapes(rows, width)
        + [
            pltpu.VMEM((TOTAL_ROWS // 2, width), F32),
            pltpu.VMEM((3, TOTAL_ROWS // 32, width), F32),
            pltpu.VMEM((4, TOTAL_ROWS // 32, width), F32),
            pltpu.SemaphoreType.DMA((60,)),
            pltpu.SemaphoreType.DMA((60,)),
            pltpu.SemaphoreType.DMA((9,)),
        ],
        compiler_params=remote_params(3),
        name="finish",
    )(back.reshape(16, rows, width), direct, part_sum)


def write_kernel(grad, sums, grad_nodes, gw_in, gw_out, gvec):
    width = gw_out.shape[1]
    factor = F32(131072.0) ** F32(-0.5)
    grad_nodes[...] = grad[...]
    gw_in[...] = sums[: 2 * width] * factor
    gw_out[...] = sums[2 * width : 3 * width] * factor
    gvec[...] = sums[3 * width : 3 * width + 3] * factor


def write(grad, sums):
    width = grad.shape[1]
    return pl.pallas_call(
        write_kernel,
        out_shape=[
            jax.ShapeDtypeStruct(grad.shape, BF16),
            jax.ShapeDtypeStruct((2 * width, width), F32),
            jax.ShapeDtypeStruct((width, width), F32),
            jax.ShapeDtypeStruct((3, width), F32),
        ],
        in_specs=[VM] * 2,
        out_specs=[VM] * 4,
        name="write",
    )(grad, sums)


def body(nodes, tiles, tile_col, tile_count, w_in, bias_in, w_out, ln_gain, ln_shift, cotangent):
    rows, width = nodes.shape
    cols, count = tile_col[:, 0], tile_count[:, 0]
    slots = tiles[:, 0]
    cols = jnp.clip(cols, 0, 127)
    near0, near1, grads, updated, direct, part_sum = middle(
        cols, count, slots, nodes, cotangent, w_in, bias_in[None], w_out, ln_gain[None], ln_shift[None]
    )
    grads = grads.reshape(8 * rows, width)
    grad_tiles, back, updated = backward(cols, count, slots, near0, near1, grads, updated)
    grad_nodes, gw_in, gw_out, gvec = write(*finish(back, direct, part_sum))
    return updated, grad_nodes, grad_tiles[:, None], gw_in, gw_out, gvec


def solution(mesh):
    placed = (
        P(("row", "col"), None),
        P("row", "col", None, None, None),
        P("row", "col", None),
        P("row", "col"),
        P(),
        P(),
        P(),
        P(),
        P(),
        P(("row", "col"), None),
    )
    return jax.shard_map(
        body,
        mesh=mesh,
        in_specs=placed,
        out_specs=(
            P(("row", "col"), None),
            P(("row", "col"), None),
            P("row", "col", None, None, None),
            P(),
            P(),
            P(),
        ),
        check_vma=False,
    )
```

```python
import functools

import jax
import jax.numpy as jnp
from jax import lax
from jax.experimental import pallas as pl
from jax.experimental.pallas import tpu as pltpu
from jax.sharding import PartitionSpec as P

F32, BF16 = jnp.float32, jnp.bfloat16
MIB = 1024 * 1024
VMEM_LIMIT = 58 * MIB
EPS = 1e-05
TOTAL_ROWS = 1024


class Place:
    def __init__(self):
        self.row = lax.axis_index("row")
        self.col = lax.axis_index("col")
        self.x = lax.div(self.row, 4)
        self.zh = lax.rem(lax.div(self.row, 2), 2)
        self.core = lax.rem(self.row, 2)
        self.y = lax.div(self.col, 2)
        self.zl = lax.rem(self.col, 2)


    def peer(self, x=0, y=0, z=0, core=0):
        z_at = lax.rem(self.zh * 2 + self.zl + z, 4)
        row = lax.rem(self.x + x, 4) * 4 + lax.div(z_at, 2) * 2 + lax.rem(self.core + core, 2)
        return (row, lax.rem(self.y + y, 4) * 2 + lax.rem(z_at, 2))

    def all_peers(self):
        steps = [dict(core=1)] + [{axis: d} for axis in "xyz" for d in (1, 2, 3)]
        return [self.peer(**step) for step in steps]


class RowGroup:
    def __init__(self, place):
        self.place = place
        col = place.col
        self.peers = {
            "p": (self.slot(1, 0), col),
            "m": (self.slot(3, 0), col),
            "pair": (self.slot(0, 1), col),
            "sib": (self.slot(0, 0, 1), col),
        }

    def slot(self, ring, pair, sib=0):
        at = self.place
        return (
            lax.rem(at.x + ring, 4) * 4
            + lax.rem(at.zh + pair, 2) * 2
            + lax.rem(at.core + sib, 2)
        )


class ColGroup:
    def __init__(self, place):
        self.place = place
        row = place.row
        self.peers = {
            "p": (row, self.slot(1, 0)),
            "m": (row, self.slot(3, 0)),
            "pair": (row, self.slot(0, 1)),
        }

    def slot(self, ring, pair):
        at = self.place
        return lax.rem(at.y + ring, 4) * 2 + lax.rem(at.zl + pair, 2)


class Wire:
    def __init__(self, send, recv):
        self.send, self.recv = send, recv
        self.names = {}
        self.open = []

    def index(self, name):
        return self.names.setdefault(name, len(self.names))

    def push(self, name, src, dst, to):
        at = self.index(name)
        copy = pltpu.make_async_remote_copy(
            src_ref=src,
            dst_ref=dst,
            send_sem=self.send.at[at],
            recv_sem=self.recv.at[at],
            device_id=to,
            device_id_type=pl.DeviceIdType.MESH,
        )
        copy.start()
        self.open.append(copy)

    def take(self, name, dst, to):
        at = self.index(name)
        pltpu.make_async_remote_copy(
            src_ref=dst,
            dst_ref=dst,
            send_sem=self.send.at[at],
            recv_sem=self.recv.at[at],
            device_id=to,
            device_id_type=pl.DeviceIdType.MESH,
        ).wait_recv()

    def drain(self):
        for copy in self.open:
            copy.wait_send()
        self.open = []


def greet(devices):
    barrier = pltpu.get_barrier_semaphore()
    for device in devices:
        pl.semaphore_signal(barrier, inc=1, device_id=device, device_id_type=pl.DeviceIdType.MESH)
    pl.semaphore_wait(barrier, len(devices))


MOVES = {"p": (3, 0, 0), "m": (1, 0, 0), "pair": (0, 1, 0), "sib": (0, 0, 1)}


QUARTER = ((0, 3, False), (3, 3, False), (6, 1, True), (7, 1, True))
MORE = ((0, 3, False), (3, 2, False), (5, 1, True), (6, 2, True))


def gather(wire, group, buf, tag, parts, per=1):
    unit = buf.shape[1] // 8

    def view(slot, part):
        start, size, _ = parts[part]
        if per == 1:
            return buf.at[slot, pl.ds(start * unit, size * unit)]
        return buf.at[pl.ds(slot * per + start, size)]

    def whole(slot):
        return buf.at[slot] if per == 1 else buf.at[pl.ds(slot * per, per)]

    has_sib = "sib" in group.peers
    late = [c for c in range(4) if parts[c][2]]
    early = [c for c in range(4) if not parts[c][2]]

    def send(ring, pair, part, way):
        ref = view(group.slot(ring, pair), part)
        dr, dp, dk = MOVES[way]
        name = (tag, (ring + dr) % 4, (pair + dp) % 2, dk, part)
        wire.push(name, ref, ref, group.peers[way])

    def take(ring, pair, part):
        slot = group.slot(ring, pair)
        wire.take((tag, ring, pair, 0, part), view(slot, part), group.peers["p"])

    def share(ring, pair):
        if has_sib:
            ref = whole(group.slot(ring, pair))
            wire.push((tag, ring, pair, 1), ref, ref, group.peers["sib"])

    def relay(pair, which):
        for c in which:
            ring, way = ((3, "p"), (1, "m"))[c % 2]
            take(ring, pair, c)
            send(ring, pair, c, way)
            if c in late and pair == 0:
                send(ring, pair, c, "pair")

    def rest(pair, which):
        for c in which:
            ring = (1, 3)[c % 2]
            take(ring, pair, c)
            if c in late and pair == 0:
                send(ring, pair, c, "pair")

    for c in early:
        send(0, 0, c, "pair")
    for c in early + late:
        send(0, 0, c, ("p", "m")[c % 2])
    yield
    for c in early + late:
        send(0, 0, c, ("m", "p")[c % 2])
    for c in late:
        send(0, 0, c, "pair")
    share(0, 0)
    yield
    relay(0, early + late)
    yield
    for c in early:
        take(0, 1, c)
        send(0, 1, c, "p")
        send(0, 1, c, "m")
    yield
    rest(0, late + early)
    share(1, 0)
    share(3, 0)
    yield
    for c in late:
        take(2, 0, c)
        send(2, 0, c, "pair")
    relay(1, early)
    yield
    for c in early:
        take(2, 0, c)
    share(2, 0)
    for c in late:
        take(0, 1, c)
    share(0, 1)
    yield
    rest(1, early)
    for ring in (1, 3):
        for c in late:
            take(ring, 1, c)
        share(ring, 1)
    for c in early + late:
        take(2, 1, c)
    share(2, 1)
    yield
    if has_sib:
        for pair in (0, 1):
            for ring in (0, 1, 3, 2):
                slot = group.slot(ring, pair, 1)
                wire.take((tag, ring, pair, 1), whole(slot), group.peers["p"])


def add_rows(rows, step, body):
    def one(i, carry):
        body(pl.ds(pl.multiple_of(i * step, step), step))
        return carry

    lax.fori_loop(0, rows // step, one, 0)


def scatter_shapes(rows, width):
    return [
        pltpu.VMEM((2, rows, width), BF16),
        pltpu.VMEM((2, rows, width), BF16),
        pltpu.VMEM((2, rows, width), BF16),
        pltpu.VMEM((2, rows, width), BF16),
        pltpu.VMEM((4, rows, width), BF16),
    ]


def scatter(wire, group, terms, bufs, tag, prepare, parts):
    relay_m, relay_p, from_m, from_p, from_pair = bufs
    unit = terms.shape[1] // 8
    cut = [pl.ds(start * unit, size * unit) for start, size, _ in parts]
    late = [c for c in range(4) if parts[c][2]]
    early = [c for c in range(4) if not parts[c][2]]
    start = parts[late[0]][0]
    first = pl.ds(start * unit, sum(parts[c][1] for c in late) * unit)
    to_p, to_m, to_pair = group.peers["p"], group.peers["m"], group.peers["pair"]

    def at(ring, pair, rows):
        return terms.at[group.slot(ring, pair), rows]

    def add(target, *others):
        def body(rows):
            total = target[rows].astype(F32)
            for other in others:
                total = total + other[rows].astype(F32)
            target[rows] = total.astype(BF16)

        add_rows(target.shape[0], unit, body)

    def cross(ring):
        dst = from_pair.at[ring, first]
        wire.push((tag, "first", ring), at(ring, 1, first), dst, to_pair)

    def crossed(ring):
        src = from_pair.at[ring, first]
        wire.take((tag, "first", ring), src, to_pair)
        add(at(ring, 0, first), src)

    def far(q, which):
        for c in which:
            dst, to = ((relay_m, to_p), (relay_p, to_m))[c % 2]
            wire.push((tag, "far", q, c), at(2, q, cut[c]), dst.at[q, cut[c]], to)

    def single(q, which):
        for c in which:
            ring, dst, to = ((3, from_p, to_m), (1, from_m, to_p))[c % 2]
            wire.push((tag, "one", q, c), at(ring, q, cut[c]), dst.at[q, cut[c]], to)

    def double(q, which):
        for c in which:
            ring, via, dst, to = ((1, relay_m, from_m, to_p), (3, relay_p, from_p, to_m))[c % 2]
            wire.take((tag, "far", q, c), via.at[q, cut[c]], to)
            add(at(ring, q, cut[c]), via.at[q, cut[c]])
            wire.push((tag, "two", q, c), at(ring, q, cut[c]), dst.at[q, cut[c]], to)

    def arrive(q, which):
        for c in which:
            one, two = ((from_p, from_m), (from_m, from_p))[c % 2]
            wire.take((tag, "one", q, c), one.at[q, cut[c]], to_p)
            wire.take((tag, "two", q, c), two.at[q, cut[c]], to_p)

    prepare(2, 1)
    cross(2)
    far(1, early)
    prepare(2, 0)
    far(0, early)
    yield
    prepare(1, 1)
    cross(1)
    prepare(3, 1)
    cross(3)
    single(1, early)
    crossed(2)
    far(0, late)
    yield
    double(1, early)
    prepare(1, 0)
    prepare(3, 0)
    single(0, early)
    yield
    crossed(1)
    crossed(3)
    single(0, late)
    double(0, early + late)
    yield
    prepare(0, 1)
    cross(0)
    for c in early:
        arrive(1, [c])
        add(at(0, 1, cut[c]), from_m.at[1, cut[c]], from_p.at[1, cut[c]])
        wire.push((tag, "last", c), at(0, 1, cut[c]), from_pair.at[0, cut[c]], to_pair)
    yield
    prepare(0, 0)
    arrive(0, early + late)
    wire.take((tag, "first", 0), from_pair.at[0, first], to_pair)
    for c in early:
        wire.take((tag, "last", c), from_pair.at[0, cut[c]], to_pair)


def exchange(wire, tag, axis, place, part, dst):
    for d in (1, 2, 3):
        wire.push((tag, axis, d), part(d), dst(d), place.peer(**{axis: d}))


def block(index, rows):
    return pl.ds(pl.multiple_of(index * rows, rows), rows)


def total_near(wire, place, mine, result, in_core, in_x, tag):
    half, quarter = TOTAL_ROWS // 2, TOTAL_ROWS // 8
    core, x = place.core, place.x
    sib = place.peer(core=1)
    wire.push((tag, "core"), mine.at[block(1 - core, half)], in_core, sib)
    yield
    wire.take((tag, "core"), in_core, sib)

    def fold(i, carry):
        at = pl.ds(pl.multiple_of(core * half + i * 64, 64), 64)
        mine[at] += in_core[block(i, 64)]
        return carry

    lax.fori_loop(0, half // 64, fold, 0)

    def own(index):
        return mine.at[block(core * 4 + index, quarter)]

    exchange(
        wire, tag, "x", place, lambda d: own(lax.rem(x + d, 4)), lambda d: in_x.at[d - 1]
    )
    yield
    for d in (1, 2, 3):
        wire.take((tag, "x", d), in_x.at[d - 1], sib)
    at = block(x, quarter)
    result[at] = mine[block(core * 4 + x, quarter)] + in_x[0] + in_x[1] + in_x[2]
    exchange(wire, tag + "r", "x", place, lambda d: result.at[at], lambda d: result.at[at])
    yield
    for d in (1, 2, 3):
        wire.take((tag + "r", "x", d), result.at[block(lax.rem(x + 4 - d, 4), quarter)], sib)


def total_far(wire, place, mine, result, in_y, in_z, tag):
    piece, quarter = TOTAL_ROWS // 32, TOTAL_ROWS // 8
    core, x, y = place.core, place.x, place.y
    z = place.zh * 2 + place.zl
    sib = place.peer(core=1)

    def at(x_at, y_at):
        return block(core * 16 + y_at * 4 + x_at, piece)

    exchange(
        wire,
        tag,
        "y",
        place,
        lambda d: mine.at[block(lax.rem(y + d, 4) * 4 + x, piece)],
        lambda d: in_y.at[d - 1],
    )
    yield
    for d in (1, 2, 3):
        wire.take((tag, "y", d), in_y.at[d - 1], sib)
    in_z[z] = mine[block(y * 4 + x, piece)] + in_y[0] + in_y[1] + in_y[2]
    exchange(wire, tag, "z", place, lambda d: in_z.at[z], lambda d: in_z.at[z])
    yield
    for d in (1, 2, 3):
        wire.take((tag, "z", d), in_z.at[lax.rem(z + 4 - d, 4)], sib)
    result[at(x, y)] = in_z[0] + in_z[1] + in_z[2] + in_z[3]
    own = result.at[at(x, y)]
    exchange(wire, tag + "r", "x", place, lambda d: own, lambda d: own)
    yield
    for d in (1, 2, 3):
        wire.take((tag + "r", "x", d), result.at[at(lax.rem(x + 4 - d, 4), y)], sib)
    four = result.at[block(core * 4 + y, quarter)]
    exchange(wire, tag + "r", "y", place, lambda d: four, lambda d: four)
    yield
    for d in (1, 2, 3):
        there = block(core * 4 + lax.rem(y + 4 - d, 4), quarter)
        wire.take((tag + "r", "y", d), result.at[there], sib)
    half = block(core, TOTAL_ROWS // 2)
    wire.push((tag, "join"), result.at[half], result.at[half], sib)
    yield
    wire.take((tag, "join"), result.at[block(1 - core, TOTAL_ROWS // 2)], sib)


def run(steps):
    for _ in steps:
        pass


def dot(a, b, dims=((1,), (0,))):
    return lax.dot_general(a, b, (dims, ((), ())), preferred_element_type=F32)


ANY = pl.BlockSpec(memory_space=pl.ANY)
VM = pl.BlockSpec(memory_space=pltpu.VMEM)


def remote_params(collective_id):
    return pltpu.CompilerParams(
        collective_id=collective_id, has_side_effects=True, vmem_limit_bytes=VMEM_LIMIT
    )


ORDER = [(2, 1), (2, 0), (1, 1), (3, 1), (1, 0), (3, 0), (0, 1), (0, 0)]


def middle_kernel(
    cols, live, tiles, nodes_any, nodes, cot, w_in, bias, w_out, gain, shift,
    near0_out, near1_out, grads, updated, direct, part_sum,
    near0, near1, slots, terms0, terms1, *rest,
):
    bufs0, bufs1, rest = rest[:5], rest[5:10], rest[10:]
    msg_s, act_s, gproj_s, gpre_s, weights, in_core, in_x, send, recv, load = rest
    place = Place()
    across, along = RowGroup(place), ColGroup(place)
    width = nodes.shape[1]
    rows = nodes.shape[0]
    near, terms = (near0, near1), (terms0, terms1)

    mine = [
        pltpu.make_async_copy(
            nodes_any.at[:, :, pl.ds(h * 128, 128)],
            near[h].at[pl.ds(across.slot(0, 0) * 8, 8)],
            load.at[8 + h],
        )
        for h in (0, 1)
    ]
    for copy in mine:
        copy.start()

    def loader(ring, pair):
        at = pl.ds(along.slot(ring, pair) * 8, 8)
        return pltpu.make_async_copy(tiles.at[at], slots.at[at], load.at[ring * 2 + pair])

    for at in ORDER:
        loader(*at).start()
    greet(place.all_peers())
    wire = Wire(send, recv)
    for copy in mine:
        copy.wait()

    def mask(ring, pair):
        loader(ring, pair).wait()
        base = along.slot(ring, pair) * 8

        def one(i, carry):
            held = jnp.full((1, 128), live[base + i], jnp.int32)
            for k in range(4):
                keep = (held > k).astype(F32).astype(BF16)
                slots[base + i, k] = slots[base + i, k] * keep
            return carry

        lax.fori_loop(0, 8, one, 0)

    def product(h, ring, pair):
        slot = along.slot(ring, pair)

        def one(j, carry):
            for u in range(2):
                i = slot * 8 + j * 2 + u
                left = jnp.concatenate([slots[i, k] for k in range(4)], axis=1)
                right = []
                for k in range(4):
                    right.append(near[h][cols[i, k]])
                at = pl.ds(pl.multiple_of((j * 2 + u) * 128, 128), 128)
                terms[h][slot, at] = dot(left, jnp.concatenate(right, axis=0)).astype(BF16)
            return carry

        lax.fori_loop(0, 4, one, 0)

    gather0 = gather(wire, across, near0, "n0", MORE, 8)
    gather1 = gather(wire, across, near1, "n1", QUARTER, 8)
    next(gather0)
    for at in ORDER[:4]:
        mask(*at)
    next(gather0)
    for at in ORDER[4:]:
        mask(*at)
    for _ in range(4):
        next(gather0)
    next(gather1)
    next(gather1)
    run(gather0)

    def prepare0(ring, pair):
        product(0, ring, pair)
        next(gather1, None)

    scatter0 = scatter(wire, along, terms0, bufs0, "s0", prepare0, MORE)
    for _ in range(4):
        next(scatter0)
    run(gather1)
    leaving = [
        pltpu.make_async_copy(near[h], out, load.at[10 + h])
        for h, out in ((0, near0_out), (1, near1_out))
    ]
    for copy in leaving:
        copy.start()
    scatter1 = scatter(
        wire, along, terms1, bufs1, "s1", lambda *at: product(1, *at), MORE
    )
    for _ in scatter1:
        next(scatter0, None)
    run(scatter0)
    own = along.slot(0, 0)
    gsum = weights.at[pl.ds(3 * width, 8)]
    weights[3 * width :] = jnp.zeros((weights.shape[0] - 3 * width, width), F32)

    def chunk(i, carry):
        at = pl.ds(pl.multiple_of(i * 256, 256), 256)
        msg = jnp.concatenate(
            [
                (
                    terms[h][own, at].astype(F32)
                    + bufs[2][0, at].astype(F32)
                    + bufs[3][0, at].astype(F32)
                    + bufs[4][0, at].astype(F32)
                ).astype(BF16)
                for h, bufs in ((0, bufs0), (1, bufs1))
            ],
            axis=1,
        )
        msg_s[at] = msg
        mine = nodes[at]
        pre = dot(mine, w_in[:width]) + dot(msg, w_in[width:]) + bias[...]
        sig = jax.nn.sigmoid(pre)
        act = (pre * sig).astype(BF16)
        act_s[at] = act
        proj = dot(act, w_out[...])
        mean = jnp.mean(proj, axis=-1, keepdims=True)
        off = proj - mean
        var = jnp.mean(off * off, axis=-1, keepdims=True)
        rstd = 1.0 / jnp.sqrt(var + EPS)
        normed = off * rstd
        updated[at] = (mine.astype(F32) + normed * gain[...] + shift[...]).astype(BF16)
        grad_out = cot[at].astype(F32)
        gscaled = grad_out * gain[...]
        gproj = (
            (
                gscaled
                - jnp.mean(gscaled, axis=-1, keepdims=True)
                - normed * jnp.mean(gscaled * normed, axis=-1, keepdims=True)
            )
            * rstd
        ).astype(BF16)
        gproj_s[at] = gproj
        gact = dot(gproj, w_out[...], ((1,), (1,)))
        gpre = gact * sig * (1.0 + pre * (1.0 - sig))
        gpre_b = gpre.astype(BF16)
        gpre_s[at] = gpre_b
        grads[own, at] = dot(gpre_b, w_in[width:], ((1,), (1,))).astype(BF16)
        direct[at] = grad_out + dot(gpre_b, w_in[:width], ((1,), (1,)))
        gsum[0:1] += jnp.sum(gpre, axis=0, keepdims=True)
        gsum[1:2] += jnp.sum(grad_out * normed, axis=0, keepdims=True)
        gsum[2:3] += jnp.sum(grad_out, axis=0, keepdims=True)
        return carry

    lax.fori_loop(0, rows // 256, chunk, 0)
    steps = gather(wire, along, grads, "g", MORE)
    next(steps)
    weights[:width] = dot(nodes[...], gpre_s[...], ((0,), (0,)))
    next(steps)
    weights[width : 2 * width] = dot(msg_s[...], gpre_s[...], ((0,), (0,)))
    weights[2 * width : 3 * width] = dot(act_s[...], gproj_s[...], ((0,), (0,)))
    sums = total_near(wire, place, weights, part_sum, in_core, in_x, "w")
    for following in (sums, steps, sums, steps, steps, sums, steps, steps):
        next(following)
    run(steps)
    run(sums)
    for copy in leaving:
        copy.wait()
    wire.drain()


def middle(cols, live, tiles, nodes, cot, w_in, bias, w_out, gain, shift):
    rows, width = nodes.shape
    one = functools.partial(pltpu.VMEM, (rows, width))
    smem = pl.BlockSpec(memory_space=pltpu.SMEM)
    near = jax.ShapeDtypeStruct((128, 128, 128), BF16)
    return pl.pallas_call(
        middle_kernel,
        out_shape=[
            near,
            near,
            jax.ShapeDtypeStruct((8, rows, width), BF16),
            jax.ShapeDtypeStruct((rows, width), BF16),
            jax.ShapeDtypeStruct((rows, width), F32),
            jax.ShapeDtypeStruct((TOTAL_ROWS // 2, width), F32),
        ],
        in_specs=[smem, smem, ANY, ANY] + [VM] * 7,
        out_specs=[ANY] * 2 + [VM] * 4,
        scratch_shapes=[pltpu.VMEM((128, 128, 128), BF16)] * 2
        + [pltpu.VMEM(tiles.shape, BF16)]
        + [pltpu.VMEM((8, rows, 128), BF16)] * 2
        + scatter_shapes(rows, 128) * 2
        + [one(BF16)] * 4
        + [
            pltpu.VMEM((TOTAL_ROWS, width), F32),
            pltpu.VMEM((TOTAL_ROWS // 2, width), F32),
            pltpu.VMEM((3, TOTAL_ROWS // 8, width), F32),
        ]
        + [
            pltpu.SemaphoreType.DMA((240,)),
            pltpu.SemaphoreType.DMA((240,)),
            pltpu.SemaphoreType.DMA((12,)),
        ],
        compiler_params=remote_params(2),
        name="middle",
    )(cols, live, tiles, nodes.reshape(8, 128, width), nodes, cot, w_in, bias, w_out, gain, shift)


def backward_kernel(
    cols, count, tiles, near0_any, near1_any, grads, updated_in,
    tile_grads, back_any, updated,
    acc, near0, near1, back, load, leave,
):
    step = pl.program_id(0)
    per = tiles.shape[0]
    updated[...] = updated_in[...]

    @pl.when(step == 0)
    def _():
        copies = [
            pltpu.make_async_copy(near0_any, near0, load.at[0]),
            pltpu.make_async_copy(near1_any, near1, load.at[1]),
        ]
        for copy in copies:
            copy.start()

        def clear(i, carry):
            acc[i] = jnp.zeros(acc.shape[1:], F32)
            return carry

        lax.fori_loop(0, acc.shape[0], clear, 0)
        for copy in copies:
            copy.wait()

    scale = F32(256.0) ** F32(-0.5)

    def work(i, at, slots):
        live = count[at]
        grad = grads[pl.ds(i * 128, 128)]
        which = [cols[at, k] for k in range(slots)]
        picked = jnp.concatenate(
            [jnp.concatenate([near0[c], near1[c]], axis=1) for c in which], axis=0
        )
        made = (dot(grad, picked, ((1,), (1,))) * scale).astype(BF16)
        zero = jnp.zeros((128, 128), BF16)
        for k in range(slots):
            tile_grads[i, k] = jnp.where(k < live, made[:, k * 128 : k * 128 + 128], zero)
        kept = jnp.concatenate([jnp.where(k < live, tiles[i, k], zero) for k in range(slots)], axis=1)
        return which, dot(kept, grad, ((0,), (0,)))

    def both(i, slots):
        found = [work(i + u, step * per + i + u, slots) for u in (0, 1)]
        for which, terms in found:
            for k in range(slots):
                acc[which[k]] += terms[k * 128 : k * 128 + 128]

    for i in range(0, per, 2):
        most = jnp.maximum(count[step * per + i], count[step * per + i + 1])

        @pl.when(most <= 2)
        def _():
            for u in (0, 1):
                tile_grads[i + u, 2:4] = jnp.zeros((2, 128, 128), BF16)

        @pl.when(most <= 0)
        def _():
            for u in (0, 1):
                tile_grads[i + u, 0:2] = jnp.zeros((2, 128, 128), BF16)

        @pl.when((most > 0) & (most <= 2))
        def _():
            both(i, 2)

        @pl.when(most > 2)
        def _():
            both(i, 4)

    @pl.when(step == pl.num_programs(0) - 1)
    def _():
        def put(i, carry):
            back[i] = acc[i].astype(BF16)
            return carry

        copies = []
        for part in range(8):
            lax.fori_loop(part * 16, part * 16 + 16, put, 0)
            at = pl.ds(part * 16, 16)
            copies.append(pltpu.make_async_copy(back.at[at], back_any.at[at], leave.at[part]))
            copies[-1].start()
        for copy in copies:
            copy.wait()


def backward(cols, count, tiles, near0, near1, grads, updated):
    row_blocks = tiles.shape[0]
    width = grads.shape[1]
    columns = (128, 128, width)
    per = 8
    steps = row_blocks // per

    passed = [pl.BlockSpec((updated.shape[0] // steps, width), lambda s, *_: (s, 0))]
    return pl.pallas_call(
        backward_kernel,
        out_shape=[
            jax.ShapeDtypeStruct(tiles.shape, BF16),
            jax.ShapeDtypeStruct(columns, BF16),
            jax.ShapeDtypeStruct(updated.shape, BF16),
        ],
        grid_spec=pltpu.PrefetchScalarGridSpec(
            num_scalar_prefetch=2,
            grid=(steps,),
            in_specs=[
                pl.BlockSpec((per, 4, 128, 128), lambda s, *_: (s, 0, 0, 0)),
                ANY,
                ANY,
                pl.BlockSpec((per * 128, width), lambda s, *_: (s, 0)),
            ]
            + passed,
            out_specs=[
                pl.BlockSpec((per, 4, 128, 128), lambda s, *_: (s, 0, 0, 0)),
                ANY,
            ]
            + passed,
            scratch_shapes=[
                pltpu.VMEM(columns, F32),
                pltpu.VMEM(near0.shape, BF16),
                pltpu.VMEM(near1.shape, BF16),
                pltpu.VMEM(columns, BF16),
                pltpu.SemaphoreType.DMA((2,)),
                pltpu.SemaphoreType.DMA((8,)),
            ],
        ),
        compiler_params=pltpu.CompilerParams(vmem_limit_bytes=VMEM_LIMIT),
        name="backward",
    )(cols, count, tiles, near0, near1, grads, updated)


def finish_kernel(
    back, direct, part_sum, out, result,
    terms, others, relay_m, relay_p, from_m, from_p, from_pair, mine, in_y, in_z, send, recv, load,
):
    place = Place()
    group = RowGroup(place)
    rows = terms.shape[1]

    def loader(ring, pair):
        slot = group.slot(ring, pair)
        return pltpu.make_async_copy(back.at[slot], terms.at[slot], load.at[ring * 2 + pair])

    held = pltpu.make_async_copy(part_sum, mine, load.at[8])
    held.start()
    for at in ORDER:
        loader(*at).start()
    greet(place.all_peers())
    wire = Wire(send, recv)
    held.wait()
    sums = total_far(wire, place, mine, result, in_y, in_z, "w")
    next(sums)
    ahead = iter(ORDER)

    def swap():
        for ring, pair in ahead:
            wire.push(
                ("f", ring, pair),
                back.at[group.slot(ring, pair, 1)],
                others.at[ring * 2 + pair],
                group.peers["sib"],
            )
            return

    swap()
    swap()

    def prepare(ring, pair):
        swap()
        loader(ring, pair).wait()
        other = others.at[ring * 2 + pair]
        wire.take(("f", ring, pair), other, group.peers["sib"])
        slot = group.slot(ring, pair)

        def body(at):
            terms[slot, at] = (terms[slot, at].astype(F32) + other[at].astype(F32)).astype(BF16)

        add_rows(rows, 128, body)

    bufs = (relay_m, relay_p, from_m, from_p, from_pair)
    for point, _ in enumerate(scatter(wire, group, terms, bufs, "b", prepare, MORE)):
        if point in (0, 1, 3, 4):
            next(sums)
    own = group.slot(0, 0)

    def last(at):
        out[at] = (
            direct[at]
            + terms[own, at].astype(F32)
            + from_m[0, at].astype(F32)
            + from_p[0, at].astype(F32)
            + from_pair[0, at].astype(F32)
        ).astype(BF16)

    add_rows(rows, 128, last)
    run(sums)
    wire.drain()


def finish(back, direct, part_sum):
    rows, width = direct.shape
    return pl.pallas_call(
        finish_kernel,
        out_shape=[
            jax.ShapeDtypeStruct((rows, width), BF16),
            jax.ShapeDtypeStruct((TOTAL_ROWS, width), F32),
        ],
        in_specs=[ANY, VM, ANY],
        out_specs=[VM] * 2,
        scratch_shapes=[
            pltpu.VMEM((16, rows, width), BF16),
            pltpu.VMEM((8, rows, width), BF16),
        ]
        + scatter_shapes(rows, width)
        + [
            pltpu.VMEM((TOTAL_ROWS // 2, width), F32),
            pltpu.VMEM((3, TOTAL_ROWS // 32, width), F32),
            pltpu.VMEM((4, TOTAL_ROWS // 32, width), F32),
            pltpu.SemaphoreType.DMA((60,)),
            pltpu.SemaphoreType.DMA((60,)),
            pltpu.SemaphoreType.DMA((9,)),
        ],
        compiler_params=remote_params(3),
        name="finish",
    )(back.reshape(16, rows, width), direct, part_sum)


def write_kernel(grad, sums, grad_nodes, gw_in, gw_out, gvec):
    width = gw_out.shape[1]
    factor = F32(131072.0) ** F32(-0.5)
    grad_nodes[...] = grad[...]
    gw_in[...] = sums[: 2 * width] * factor
    gw_out[...] = sums[2 * width : 3 * width] * factor
    gvec[...] = sums[3 * width : 3 * width + 3] * factor


def write(grad, sums):
    width = grad.shape[1]
    return pl.pallas_call(
        write_kernel,
        out_shape=[
            jax.ShapeDtypeStruct(grad.shape, BF16),
            jax.ShapeDtypeStruct((2 * width, width), F32),
            jax.ShapeDtypeStruct((width, width), F32),
            jax.ShapeDtypeStruct((3, width), F32),
        ],
        in_specs=[VM] * 2,
        out_specs=[VM] * 4,
        name="write",
    )(grad, sums)


def body(nodes, tiles, tile_col, tile_count, w_in, bias_in, w_out, ln_gain, ln_shift, cotangent):
    rows, width = nodes.shape
    cols, count = tile_col[:, 0], tile_count[:, 0]
    slots = tiles[:, 0]
    cols = jnp.clip(cols, 0, 127)
    near0, near1, grads, updated, direct, part_sum = middle(
        cols, count, slots, nodes, cotangent, w_in, bias_in[None], w_out, ln_gain[None], ln_shift[None]
    )
    grads = grads.reshape(8 * rows, width)
    grad_tiles, back, updated = backward(cols, count, slots, near0, near1, grads, updated)
    grad_nodes, gw_in, gw_out, gvec = write(*finish(back, direct, part_sum))
    return updated, grad_nodes, grad_tiles[:, None], gw_in, gw_out, gvec


def solution(mesh):
    placed = (
        P(("row", "col"), None),
        P("row", "col", None, None, None),
        P("row", "col", None),
        P("row", "col"),
        P(),
        P(),
        P(),
        P(),
        P(),
        P(("row", "col"), None),
    )
    return jax.shard_map(
        body,
        mesh=mesh,
        in_specs=placed,
        out_specs=(
            P(("row", "col"), None),
            P(("row", "col"), None),
            P("row", "col", None, None, None),
            P(),
            P(),
            P(),
        ),
        check_vma=False,
    )
```

```python
import functools

import jax
import jax.numpy as jnp
from jax import lax
from jax.experimental import pallas as pl
from jax.experimental.pallas import tpu as pltpu
from jax.sharding import PartitionSpec as P

F32, BF16 = jnp.float32, jnp.bfloat16
MIB = 1024 * 1024
VMEM_LIMIT = 58 * MIB
EPS = 1e-05
TOTAL_ROWS = 1024


class Place:
    def __init__(self):
        self.row = lax.axis_index("row")
        self.col = lax.axis_index("col")
        self.x = lax.div(self.row, 4)
        self.zh = lax.rem(lax.div(self.row, 2), 2)
        self.core = lax.rem(self.row, 2)
        self.y = lax.div(self.col, 2)
        self.zl = lax.rem(self.col, 2)


    def peer(self, x=0, y=0, z=0, core=0):
        z_at = lax.rem(self.zh * 2 + self.zl + z, 4)
        row = lax.rem(self.x + x, 4) * 4 + lax.div(z_at, 2) * 2 + lax.rem(self.core + core, 2)
        return (row, lax.rem(self.y + y, 4) * 2 + lax.rem(z_at, 2))

    def all_peers(self):
        steps = [dict(core=1)] + [{axis: d} for axis in "xyz" for d in (1, 2, 3)]
        return [self.peer(**step) for step in steps]


class RowGroup:
    def __init__(self, place):
        self.place = place
        col = place.col
        self.peers = {
            "p": (self.slot(1, 0), col),
            "m": (self.slot(3, 0), col),
            "pair": (self.slot(0, 1), col),
            "sib": (self.slot(0, 0, 1), col),
        }

    def slot(self, ring, pair, sib=0):
        at = self.place
        return (
            lax.rem(at.x + ring, 4) * 4
            + lax.rem(at.zh + pair, 2) * 2
            + lax.rem(at.core + sib, 2)
        )


class ColGroup:
    def __init__(self, place):
        self.place = place
        row = place.row
        self.peers = {
            "p": (row, self.slot(1, 0)),
            "m": (row, self.slot(3, 0)),
            "pair": (row, self.slot(0, 1)),
        }

    def slot(self, ring, pair):
        at = self.place
        return lax.rem(at.y + ring, 4) * 2 + lax.rem(at.zl + pair, 2)


class Wire:
    def __init__(self, send, recv):
        self.send, self.recv = send, recv
        self.names = {}
        self.open = []

    def index(self, name):
        return self.names.setdefault(name, len(self.names))

    def push(self, name, src, dst, to):
        at = self.index(name)
        copy = pltpu.make_async_remote_copy(
            src_ref=src,
            dst_ref=dst,
            send_sem=self.send.at[at],
            recv_sem=self.recv.at[at],
            device_id=to,
            device_id_type=pl.DeviceIdType.MESH,
        )
        copy.start()
        self.open.append(copy)

    def take(self, name, dst, to):
        at = self.index(name)
        pltpu.make_async_remote_copy(
            src_ref=dst,
            dst_ref=dst,
            send_sem=self.send.at[at],
            recv_sem=self.recv.at[at],
            device_id=to,
            device_id_type=pl.DeviceIdType.MESH,
        ).wait_recv()

    def drain(self):
        for copy in self.open:
            copy.wait_send()
        self.open = []


def greet(devices):
    barrier = pltpu.get_barrier_semaphore()
    for device in devices:
        pl.semaphore_signal(barrier, inc=1, device_id=device, device_id_type=pl.DeviceIdType.MESH)
    pl.semaphore_wait(barrier, len(devices))


MOVES = {"p": (3, 0, 0), "m": (1, 0, 0), "pair": (0, 1, 0), "sib": (0, 0, 1)}


QUARTER = ((0, 3, False), (3, 3, False), (6, 1, True), (7, 1, True))
MORE = ((0, 3, False), (3, 2, False), (5, 1, True), (6, 2, True))


def gather(wire, group, buf, tag, parts, per=1):
    unit = buf.shape[1] // 8

    def view(slot, part):
        start, size, _ = parts[part]
        if per == 1:
            return buf.at[slot, pl.ds(start * unit, size * unit)]
        return buf.at[pl.ds(slot * per + start, size)]

    def whole(slot):
        return buf.at[slot] if per == 1 else buf.at[pl.ds(slot * per, per)]

    has_sib = "sib" in group.peers
    late = [c for c in range(4) if parts[c][2]]
    early = [c for c in range(4) if not parts[c][2]]

    def send(ring, pair, part, way):
        ref = view(group.slot(ring, pair), part)
        dr, dp, dk = MOVES[way]
        name = (tag, (ring + dr) % 4, (pair + dp) % 2, dk, part)
        wire.push(name, ref, ref, group.peers[way])

    def take(ring, pair, part):
        slot = group.slot(ring, pair)
        wire.take((tag, ring, pair, 0, part), view(slot, part), group.peers["p"])

    def share(ring, pair):
        if has_sib:
            ref = whole(group.slot(ring, pair))
            wire.push((tag, ring, pair, 1), ref, ref, group.peers["sib"])

    def relay(pair, which):
        for c in which:
            ring, way = ((3, "p"), (1, "m"))[c % 2]
            take(ring, pair, c)
            send(ring, pair, c, way)
            if c in late and pair == 0:
                send(ring, pair, c, "pair")

    def rest(pair, which):
        for c in which:
            ring = (1, 3)[c % 2]
            take(ring, pair, c)
            if c in late and pair == 0:
                send(ring, pair, c, "pair")

    for c in early:
        send(0, 0, c, "pair")
    for c in early + late:
        send(0, 0, c, ("p", "m")[c % 2])
    yield
    for c in early + late:
        send(0, 0, c, ("m", "p")[c % 2])
    for c in late:
        send(0, 0, c, "pair")
    share(0, 0)
    yield
    relay(0, early + late)
    yield
    for c in early:
        take(0, 1, c)
        send(0, 1, c, "p")
        send(0, 1, c, "m")
    yield
    rest(0, late + early)
    share(1, 0)
    share(3, 0)
    yield
    for c in late:
        take(2, 0, c)
        send(2, 0, c, "pair")
    relay(1, early)
    yield
    for c in early:
        take(2, 0, c)
    share(2, 0)
    for c in late:
        take(0, 1, c)
    share(0, 1)
    yield
    rest(1, early)
    for ring in (1, 3):
        for c in late:
            take(ring, 1, c)
        share(ring, 1)
    for c in early + late:
        take(2, 1, c)
    share(2, 1)
    yield
    if has_sib:
        for pair in (0, 1):
            for ring in (0, 1, 3, 2):
                slot = group.slot(ring, pair, 1)
                wire.take((tag, ring, pair, 1), whole(slot), group.peers["p"])


def add_rows(rows, step, body):
    def one(i, carry):
        body(pl.ds(pl.multiple_of(i * step, step), step))
        return carry

    lax.fori_loop(0, rows // step, one, 0)


def scatter_shapes(rows, width):
    return [
        pltpu.VMEM((2, rows, width), BF16),
        pltpu.VMEM((2, rows, width), BF16),
        pltpu.VMEM((2, rows, width), BF16),
        pltpu.VMEM((2, rows, width), BF16),
        pltpu.VMEM((4, rows, width), BF16),
    ]


def scatter(wire, group, terms, bufs, tag, prepare, parts):
    relay_m, relay_p, from_m, from_p, from_pair = bufs
    unit = terms.shape[1] // 8
    cut = [pl.ds(start * unit, size * unit) for start, size, _ in parts]
    late = [c for c in range(4) if parts[c][2]]
    early = [c for c in range(4) if not parts[c][2]]
    start = parts[late[0]][0]
    first = pl.ds(start * unit, sum(parts[c][1] for c in late) * unit)
    to_p, to_m, to_pair = group.peers["p"], group.peers["m"], group.peers["pair"]

    def at(ring, pair, rows):
        return terms.at[group.slot(ring, pair), rows]

    def add(target, *others):
        def body(rows):
            total = target[rows].astype(F32)
            for other in others:
                total = total + other[rows].astype(F32)
            target[rows] = total.astype(BF16)

        add_rows(target.shape[0], unit, body)

    def cross(ring):
        dst = from_pair.at[ring, first]
        wire.push((tag, "first", ring), at(ring, 1, first), dst, to_pair)

    def crossed(ring):
        src = from_pair.at[ring, first]
        wire.take((tag, "first", ring), src, to_pair)
        add(at(ring, 0, first), src)

    def far(q, which):
        for c in which:
            dst, to = ((relay_m, to_p), (relay_p, to_m))[c % 2]
            wire.push((tag, "far", q, c), at(2, q, cut[c]), dst.at[q, cut[c]], to)

    def single(q, which):
        for c in which:
            ring, dst, to = ((3, from_p, to_m), (1, from_m, to_p))[c % 2]
            wire.push((tag, "one", q, c), at(ring, q, cut[c]), dst.at[q, cut[c]], to)

    def double(q, which):
        for c in which:
            ring, via, dst, to = ((1, relay_m, from_m, to_p), (3, relay_p, from_p, to_m))[c % 2]
            wire.take((tag, "far", q, c), via.at[q, cut[c]], to)
            add(at(ring, q, cut[c]), via.at[q, cut[c]])
            wire.push((tag, "two", q, c), at(ring, q, cut[c]), dst.at[q, cut[c]], to)

    def arrive(q, which):
        for c in which:
            one, two = ((from_p, from_m), (from_m, from_p))[c % 2]
            wire.take((tag, "one", q, c), one.at[q, cut[c]], to_p)
            wire.take((tag, "two", q, c), two.at[q, cut[c]], to_p)

    prepare(2, 1)
    cross(2)
    far(1, early)
    prepare(2, 0)
    far(0, early)
    yield
    prepare(1, 1)
    cross(1)
    prepare(3, 1)
    cross(3)
    single(1, early)
    crossed(2)
    far(0, late)
    yield
    double(1, early)
    prepare(1, 0)
    prepare(3, 0)
    single(0, early)
    yield
    crossed(1)
    crossed(3)
    single(0, late)
    double(0, early + late)
    yield
    prepare(0, 1)
    cross(0)
    for c in early:
        arrive(1, [c])
        add(at(0, 1, cut[c]), from_m.at[1, cut[c]], from_p.at[1, cut[c]])
        wire.push((tag, "last", c), at(0, 1, cut[c]), from_pair.at[0, cut[c]], to_pair)
    yield
    prepare(0, 0)
    arrive(0, early + late)
    wire.take((tag, "first", 0), from_pair.at[0, first], to_pair)
    for c in early:
        wire.take((tag, "last", c), from_pair.at[0, cut[c]], to_pair)


def exchange(wire, tag, axis, place, part, dst):
    for d in (1, 2, 3):
        wire.push((tag, axis, d), part(d), dst(d), place.peer(**{axis: d}))


def block(index, rows):
    return pl.ds(pl.multiple_of(index * rows, rows), rows)


def total_near(wire, place, mine, result, in_core, in_x, tag):
    half, quarter = TOTAL_ROWS // 2, TOTAL_ROWS // 8
    core, x = place.core, place.x
    sib = place.peer(core=1)
    wire.push((tag, "core"), mine.at[block(1 - core, half)], in_core, sib)
    yield
    wire.take((tag, "core"), in_core, sib)

    def fold(i, carry):
        at = pl.ds(pl.multiple_of(core * half + i * 64, 64), 64)
        mine[at] += in_core[block(i, 64)]
        return carry

    lax.fori_loop(0, half // 64, fold, 0)

    def own(index):
        return mine.at[block(core * 4 + index, quarter)]

    exchange(
        wire, tag, "x", place, lambda d: own(lax.rem(x + d, 4)), lambda d: in_x.at[d - 1]
    )
    yield
    for d in (1, 2, 3):
        wire.take((tag, "x", d), in_x.at[d - 1], sib)
    at = block(x, quarter)
    result[at] = mine[block(core * 4 + x, quarter)] + in_x[0] + in_x[1] + in_x[2]
    exchange(wire, tag + "r", "x", place, lambda d: result.at[at], lambda d: result.at[at])
    yield
    for d in (1, 2, 3):
        wire.take((tag + "r", "x", d), result.at[block(lax.rem(x + 4 - d, 4), quarter)], sib)


def total_far(wire, place, mine, result, in_y, in_z, tag):
    piece, quarter = TOTAL_ROWS // 32, TOTAL_ROWS // 8
    core, x, y = place.core, place.x, place.y
    z = place.zh * 2 + place.zl
    sib = place.peer(core=1)

    def at(x_at, y_at):
        return block(core * 16 + y_at * 4 + x_at, piece)

    exchange(
        wire,
        tag,
        "y",
        place,
        lambda d: mine.at[block(lax.rem(y + d, 4) * 4 + x, piece)],
        lambda d: in_y.at[d - 1],
    )
    yield
    for d in (1, 2, 3):
        wire.take((tag, "y", d), in_y.at[d - 1], sib)
    in_z[z] = mine[block(y * 4 + x, piece)] + in_y[0] + in_y[1] + in_y[2]
    exchange(wire, tag, "z", place, lambda d: in_z.at[z], lambda d: in_z.at[z])
    yield
    for d in (1, 2, 3):
        wire.take((tag, "z", d), in_z.at[lax.rem(z + 4 - d, 4)], sib)
    result[at(x, y)] = in_z[0] + in_z[1] + in_z[2] + in_z[3]
    own = result.at[at(x, y)]
    exchange(wire, tag + "r", "x", place, lambda d: own, lambda d: own)
    yield
    for d in (1, 2, 3):
        wire.take((tag + "r", "x", d), result.at[at(lax.rem(x + 4 - d, 4), y)], sib)
    four = result.at[block(core * 4 + y, quarter)]
    exchange(wire, tag + "r", "y", place, lambda d: four, lambda d: four)
    yield
    for d in (1, 2, 3):
        there = block(core * 4 + lax.rem(y + 4 - d, 4), quarter)
        wire.take((tag + "r", "y", d), result.at[there], sib)
    half = block(core, TOTAL_ROWS // 2)
    wire.push((tag, "join"), result.at[half], result.at[half], sib)
    yield
    wire.take((tag, "join"), result.at[block(1 - core, TOTAL_ROWS // 2)], sib)


def run(steps):
    for _ in steps:
        pass


def dot(a, b, dims=((1,), (0,))):
    return lax.dot_general(a, b, (dims, ((), ())), preferred_element_type=F32)


ANY = pl.BlockSpec(memory_space=pl.ANY)
VM = pl.BlockSpec(memory_space=pltpu.VMEM)


def remote_params(collective_id):
    return pltpu.CompilerParams(
        collective_id=collective_id, has_side_effects=True, vmem_limit_bytes=VMEM_LIMIT
    )


ORDER = [(2, 1), (2, 0), (1, 1), (3, 1), (1, 0), (3, 0), (0, 1), (0, 0)]


def middle_kernel(
    cols, live, tiles, nodes_any, nodes, cot, w_in, bias, w_out, gain, shift,
    near0_out, near1_out, grads, updated, direct, part_sum,
    near0, near1, slots, terms0, terms1, *rest,
):
    bufs0, bufs1, rest = rest[:5], rest[5:10], rest[10:]
    msg_s, act_s, gproj_s, gpre_s, weights, in_core, in_x, send, recv, load = rest
    place = Place()
    across, along = RowGroup(place), ColGroup(place)
    width = nodes.shape[1]
    rows = nodes.shape[0]
    near, terms = (near0, near1), (terms0, terms1)

    mine = [
        pltpu.make_async_copy(
            nodes_any.at[:, :, pl.ds(h * 128, 128)],
            near[h].at[pl.ds(across.slot(0, 0) * 8, 8)],
            load.at[8 + h],
        )
        for h in (0, 1)
    ]
    for copy in mine:
        copy.start()

    def loader(ring, pair):
        at = pl.ds(along.slot(ring, pair) * 8, 8)
        return pltpu.make_async_copy(tiles.at[at], slots.at[at], load.at[ring * 2 + pair])

    for at in ORDER:
        loader(*at).start()
    greet(place.all_peers())
    wire = Wire(send, recv)
    for copy in mine:
        copy.wait()

    def mask(ring, pair):
        loader(ring, pair).wait()
        base = along.slot(ring, pair) * 8

        def one(i, carry):
            held = jnp.full((1, 128), live[base + i], jnp.int32)
            for k in range(4):
                keep = (held > k).astype(F32).astype(BF16)
                slots[base + i, k] = slots[base + i, k] * keep
            return carry

        lax.fori_loop(0, 8, one, 0)

    def product(h, ring, pair):
        slot = along.slot(ring, pair)

        def one(j, carry):
            for u in range(2):
                i = slot * 8 + j * 2 + u
                left = jnp.concatenate([slots[i, k] for k in range(4)], axis=1)
                right = []
                for k in range(4):
                    right.append(near[h][cols[i, k]])
                at = pl.ds(pl.multiple_of((j * 2 + u) * 128, 128), 128)
                terms[h][slot, at] = dot(left, jnp.concatenate(right, axis=0)).astype(BF16)
            return carry

        lax.fori_loop(0, 4, one, 0)

    gather0 = gather(wire, across, near0, "n0", MORE, 8)
    gather1 = gather(wire, across, near1, "n1", QUARTER, 8)
    next(gather0)
    for at in ORDER[:4]:
        mask(*at)
    next(gather0)
    for at in ORDER[4:]:
        mask(*at)
    for _ in range(4):
        next(gather0)
    next(gather1)
    next(gather1)
    run(gather0)

    gather_steps = {(3, 1): 1, (1, 0): 2, (3, 0): 2}

    def prepare0(ring, pair):
        product(0, ring, pair)
        for _ in range(gather_steps.get((ring, pair), 0)):
            next(gather1, None)

    scatter0 = scatter(wire, along, terms0, bufs0, "s0", prepare0, MORE)
    for _ in range(4):
        next(scatter0)
    run(gather1)
    leaving = [
        pltpu.make_async_copy(near[h], out, load.at[10 + h])
        for h, out in ((0, near0_out), (1, near1_out))
    ]
    for copy in leaving:
        copy.start()
    scatter1 = scatter(
        wire, along, terms1, bufs1, "s1", lambda *at: product(1, *at), MORE
    )
    for _ in scatter1:
        next(scatter0, None)
    run(scatter0)
    own = along.slot(0, 0)
    gsum = weights.at[pl.ds(3 * width, 8)]
    weights[3 * width :] = jnp.zeros((weights.shape[0] - 3 * width, width), F32)

    def chunk(i, carry):
        at = pl.ds(pl.multiple_of(i * 256, 256), 256)
        msg = jnp.concatenate(
            [
                (
                    terms[h][own, at].astype(F32)
                    + bufs[2][0, at].astype(F32)
                    + bufs[3][0, at].astype(F32)
                    + bufs[4][0, at].astype(F32)
                ).astype(BF16)
                for h, bufs in ((0, bufs0), (1, bufs1))
            ],
            axis=1,
        )
        msg_s[at] = msg
        mine = nodes[at]
        pre = dot(mine, w_in[:width]) + dot(msg, w_in[width:]) + bias[...]
        sig = jax.nn.sigmoid(pre)
        act = (pre * sig).astype(BF16)
        act_s[at] = act
        proj = dot(act, w_out[...])
        mean = jnp.mean(proj, axis=-1, keepdims=True)
        off = proj - mean
        var = jnp.mean(off * off, axis=-1, keepdims=True)
        rstd = 1.0 / jnp.sqrt(var + EPS)
        normed = off * rstd
        updated[at] = (mine.astype(F32) + normed * gain[...] + shift[...]).astype(BF16)
        grad_out = cot[at].astype(F32)
        gscaled = grad_out * gain[...]
        gproj = (
            (
                gscaled
                - jnp.mean(gscaled, axis=-1, keepdims=True)
                - normed * jnp.mean(gscaled * normed, axis=-1, keepdims=True)
            )
            * rstd
        ).astype(BF16)
        gproj_s[at] = gproj
        gact = dot(gproj, w_out[...], ((1,), (1,)))
        gpre = gact * sig * (1.0 + pre * (1.0 - sig))
        gpre_b = gpre.astype(BF16)
        gpre_s[at] = gpre_b
        grads[own, at] = dot(gpre_b, w_in[width:], ((1,), (1,))).astype(BF16)
        direct[at] = grad_out + dot(gpre_b, w_in[:width], ((1,), (1,)))
        gsum[0:1] += jnp.sum(gpre, axis=0, keepdims=True)
        gsum[1:2] += jnp.sum(grad_out * normed, axis=0, keepdims=True)
        gsum[2:3] += jnp.sum(grad_out, axis=0, keepdims=True)
        return carry

    lax.fori_loop(0, rows // 256, chunk, 0)
    steps = gather(wire, along, grads, "g", MORE)
    next(steps)
    weights[:width] = dot(nodes[...], gpre_s[...], ((0,), (0,)))
    next(steps)
    weights[width : 2 * width] = dot(msg_s[...], gpre_s[...], ((0,), (0,)))
    weights[2 * width : 3 * width] = dot(act_s[...], gproj_s[...], ((0,), (0,)))
    sums = total_near(wire, place, weights, part_sum, in_core, in_x, "w")
    for following in (sums, steps, sums, steps, steps, sums, steps, steps):
        next(following)
    run(steps)
    run(sums)
    for copy in leaving:
        copy.wait()
    wire.drain()


def middle(cols, live, tiles, nodes, cot, w_in, bias, w_out, gain, shift):
    rows, width = nodes.shape
    one = functools.partial(pltpu.VMEM, (rows, width))
    smem = pl.BlockSpec(memory_space=pltpu.SMEM)
    near = jax.ShapeDtypeStruct((128, 128, 128), BF16)
    return pl.pallas_call(
        middle_kernel,
        out_shape=[
            near,
            near,
            jax.ShapeDtypeStruct((8, rows, width), BF16),
            jax.ShapeDtypeStruct((rows, width), BF16),
            jax.ShapeDtypeStruct((rows, width), F32),
            jax.ShapeDtypeStruct((TOTAL_ROWS // 2, width), F32),
        ],
        in_specs=[smem, smem, ANY, ANY] + [VM] * 7,
        out_specs=[ANY] * 2 + [VM] * 4,
        scratch_shapes=[pltpu.VMEM((128, 128, 128), BF16)] * 2
        + [pltpu.VMEM(tiles.shape, BF16)]
        + [pltpu.VMEM((8, rows, 128), BF16)] * 2
        + scatter_shapes(rows, 128) * 2
        + [one(BF16)] * 4
        + [
            pltpu.VMEM((TOTAL_ROWS, width), F32),
            pltpu.VMEM((TOTAL_ROWS // 2, width), F32),
            pltpu.VMEM((3, TOTAL_ROWS // 8, width), F32),
        ]
        + [
            pltpu.SemaphoreType.DMA((240,)),
            pltpu.SemaphoreType.DMA((240,)),
            pltpu.SemaphoreType.DMA((12,)),
        ],
        compiler_params=remote_params(2),
        name="middle",
    )(cols, live, tiles, nodes.reshape(8, 128, width), nodes, cot, w_in, bias, w_out, gain, shift)


def backward_kernel(
    cols, count, tiles, near0_any, near1_any, grads, updated_in,
    tile_grads, back_any, updated,
    acc, near0, near1, back, load, leave,
):
    step = pl.program_id(0)
    per = tiles.shape[0]
    updated[...] = updated_in[...]

    @pl.when(step == 0)
    def _():
        copies = [
            pltpu.make_async_copy(near0_any, near0, load.at[0]),
            pltpu.make_async_copy(near1_any, near1, load.at[1]),
        ]
        for copy in copies:
            copy.start()

        def clear(i, carry):
            acc[i] = jnp.zeros(acc.shape[1:], F32)
            return carry

        lax.fori_loop(0, acc.shape[0], clear, 0)
        for copy in copies:
            copy.wait()

    scale = F32(256.0) ** F32(-0.5)

    def work(i, at, slots):
        live = count[at]
        grad = grads[pl.ds(i * 128, 128)]
        which = [cols[at, k] for k in range(slots)]
        picked = jnp.concatenate(
            [jnp.concatenate([near0[c], near1[c]], axis=1) for c in which], axis=0
        )
        made = (dot(grad, picked, ((1,), (1,))) * scale).astype(BF16)
        zero = jnp.zeros((128, 128), BF16)
        for k in range(slots):
            tile_grads[i, k] = jnp.where(k < live, made[:, k * 128 : k * 128 + 128], zero)
        kept = jnp.concatenate([jnp.where(k < live, tiles[i, k], zero) for k in range(slots)], axis=1)
        return which, dot(kept, grad, ((0,), (0,)))

    def both(i, slots):
        found = [work(i + u, step * per + i + u, slots) for u in (0, 1)]
        for which, terms in found:
            for k in range(slots):
                acc[which[k]] += terms[k * 128 : k * 128 + 128]

    for i in range(0, per, 2):
        most = jnp.maximum(count[step * per + i], count[step * per + i + 1])

        @pl.when(most <= 2)
        def _():
            for u in (0, 1):
                tile_grads[i + u, 2:4] = jnp.zeros((2, 128, 128), BF16)

        @pl.when(most <= 0)
        def _():
            for u in (0, 1):
                tile_grads[i + u, 0:2] = jnp.zeros((2, 128, 128), BF16)

        @pl.when((most > 0) & (most <= 2))
        def _():
            both(i, 2)

        @pl.when(most > 2)
        def _():
            both(i, 4)

    @pl.when(step == pl.num_programs(0) - 1)
    def _():
        def put(i, carry):
            back[i] = acc[i].astype(BF16)
            return carry

        copies = []
        for part in range(8):
            lax.fori_loop(part * 16, part * 16 + 16, put, 0)
            at = pl.ds(part * 16, 16)
            copies.append(pltpu.make_async_copy(back.at[at], back_any.at[at], leave.at[part]))
            copies[-1].start()
        for copy in copies:
            copy.wait()


def backward(cols, count, tiles, near0, near1, grads, updated):
    row_blocks = tiles.shape[0]
    width = grads.shape[1]
    columns = (128, 128, width)
    per = 8
    steps = row_blocks // per

    passed = [pl.BlockSpec((updated.shape[0] // steps, width), lambda s, *_: (s, 0))]
    return pl.pallas_call(
        backward_kernel,
        out_shape=[
            jax.ShapeDtypeStruct(tiles.shape, BF16),
            jax.ShapeDtypeStruct(columns, BF16),
            jax.ShapeDtypeStruct(updated.shape, BF16),
        ],
        grid_spec=pltpu.PrefetchScalarGridSpec(
            num_scalar_prefetch=2,
            grid=(steps,),
            in_specs=[
                pl.BlockSpec((per, 4, 128, 128), lambda s, *_: (s, 0, 0, 0)),
                ANY,
                ANY,
                pl.BlockSpec((per * 128, width), lambda s, *_: (s, 0)),
            ]
            + passed,
            out_specs=[
                pl.BlockSpec((per, 4, 128, 128), lambda s, *_: (s, 0, 0, 0)),
                ANY,
            ]
            + passed,
            scratch_shapes=[
                pltpu.VMEM(columns, F32),
                pltpu.VMEM(near0.shape, BF16),
                pltpu.VMEM(near1.shape, BF16),
                pltpu.VMEM(columns, BF16),
                pltpu.SemaphoreType.DMA((2,)),
                pltpu.SemaphoreType.DMA((8,)),
            ],
        ),
        compiler_params=pltpu.CompilerParams(vmem_limit_bytes=VMEM_LIMIT),
        name="backward",
    )(cols, count, tiles, near0, near1, grads, updated)


def finish_kernel(
    back, direct, part_sum, out, result,
    terms, others, relay_m, relay_p, from_m, from_p, from_pair, mine, in_y, in_z, send, recv, load,
):
    place = Place()
    group = RowGroup(place)
    rows = terms.shape[1]

    def loader(ring, pair):
        slot = group.slot(ring, pair)
        return pltpu.make_async_copy(back.at[slot], terms.at[slot], load.at[ring * 2 + pair])

    held = pltpu.make_async_copy(part_sum, mine, load.at[8])
    held.start()
    for at in ORDER:
        loader(*at).start()
    greet(place.all_peers())
    wire = Wire(send, recv)
    held.wait()
    sums = total_far(wire, place, mine, result, in_y, in_z, "w")
    next(sums)
    ahead = iter(ORDER)

    def swap():
        for ring, pair in ahead:
            wire.push(
                ("f", ring, pair),
                back.at[group.slot(ring, pair, 1)],
                others.at[ring * 2 + pair],
                group.peers["sib"],
            )
            return

    swap()
    swap()

    def prepare(ring, pair):
        swap()
        loader(ring, pair).wait()
        other = others.at[ring * 2 + pair]
        wire.take(("f", ring, pair), other, group.peers["sib"])
        slot = group.slot(ring, pair)

        def body(at):
            terms[slot, at] = (terms[slot, at].astype(F32) + other[at].astype(F32)).astype(BF16)

        add_rows(rows, 128, body)

    bufs = (relay_m, relay_p, from_m, from_p, from_pair)
    for point, _ in enumerate(scatter(wire, group, terms, bufs, "b", prepare, MORE)):
        if point in (0, 1, 3, 4):
            next(sums)
    own = group.slot(0, 0)

    def last(at):
        out[at] = (
            direct[at]
            + terms[own, at].astype(F32)
            + from_m[0, at].astype(F32)
            + from_p[0, at].astype(F32)
            + from_pair[0, at].astype(F32)
        ).astype(BF16)

    add_rows(rows, 128, last)
    run(sums)
    wire.drain()


def finish(back, direct, part_sum):
    rows, width = direct.shape
    return pl.pallas_call(
        finish_kernel,
        out_shape=[
            jax.ShapeDtypeStruct((rows, width), BF16),
            jax.ShapeDtypeStruct((TOTAL_ROWS, width), F32),
        ],
        in_specs=[ANY, VM, ANY],
        out_specs=[VM] * 2,
        scratch_shapes=[
            pltpu.VMEM((16, rows, width), BF16),
            pltpu.VMEM((8, rows, width), BF16),
        ]
        + scatter_shapes(rows, width)
        + [
            pltpu.VMEM((TOTAL_ROWS // 2, width), F32),
            pltpu.VMEM((3, TOTAL_ROWS // 32, width), F32),
            pltpu.VMEM((4, TOTAL_ROWS // 32, width), F32),
            pltpu.SemaphoreType.DMA((60,)),
            pltpu.SemaphoreType.DMA((60,)),
            pltpu.SemaphoreType.DMA((9,)),
        ],
        compiler_params=remote_params(3),
        name="finish",
    )(back.reshape(16, rows, width), direct, part_sum)


def write_kernel(grad, sums, grad_nodes, gw_in, gw_out, gvec):
    width = gw_out.shape[1]
    factor = F32(131072.0) ** F32(-0.5)
    grad_nodes[...] = grad[...]
    gw_in[...] = sums[: 2 * width] * factor
    gw_out[...] = sums[2 * width : 3 * width] * factor
    gvec[...] = sums[3 * width : 3 * width + 3] * factor


def write(grad, sums):
    width = grad.shape[1]
    return pl.pallas_call(
        write_kernel,
        out_shape=[
            jax.ShapeDtypeStruct(grad.shape, BF16),
            jax.ShapeDtypeStruct((2 * width, width), F32),
            jax.ShapeDtypeStruct((width, width), F32),
            jax.ShapeDtypeStruct((3, width), F32),
        ],
        in_specs=[VM] * 2,
        out_specs=[VM] * 4,
        name="write",
    )(grad, sums)


def body(nodes, tiles, tile_col, tile_count, w_in, bias_in, w_out, ln_gain, ln_shift, cotangent):
    rows, width = nodes.shape
    cols, count = tile_col[:, 0], tile_count[:, 0]
    slots = tiles[:, 0]
    cols = jnp.clip(cols, 0, 127)
    near0, near1, grads, updated, direct, part_sum = middle(
        cols, count, slots, nodes, cotangent, w_in, bias_in[None], w_out, ln_gain[None], ln_shift[None]
    )
    grads = grads.reshape(8 * rows, width)
    grad_tiles, back, updated = backward(cols, count, slots, near0, near1, grads, updated)
    grad_nodes, gw_in, gw_out, gvec = write(*finish(back, direct, part_sum))
    return updated, grad_nodes, grad_tiles[:, None], gw_in, gw_out, gvec


def solution(mesh):
    placed = (
        P(("row", "col"), None),
        P("row", "col", None, None, None),
        P("row", "col", None),
        P("row", "col"),
        P(),
        P(),
        P(),
        P(),
        P(),
        P(("row", "col"), None),
    )
    return jax.shard_map(
        body,
        mesh=mesh,
        in_specs=placed,
        out_specs=(
            P(("row", "col"), None),
            P(("row", "col"), None),
            P("row", "col", None, None, None),
            P(),
            P(),
            P(),
        ),
        check_vma=False,
    )
```

```python
import functools

import jax
import jax.numpy as jnp
from jax import lax
from jax.experimental import pallas as pl
from jax.experimental.pallas import tpu as pltpu
from jax.sharding import PartitionSpec as P

F32, BF16 = jnp.float32, jnp.bfloat16
MIB = 1024 * 1024
VMEM_LIMIT = 58 * MIB
EPS = 1e-05
TOTAL_ROWS = 1024


class Place:
    def __init__(self):
        self.row = lax.axis_index("row")
        self.col = lax.axis_index("col")
        self.x = lax.div(self.row, 4)
        self.zh = lax.rem(lax.div(self.row, 2), 2)
        self.core = lax.rem(self.row, 2)
        self.y = lax.div(self.col, 2)
        self.zl = lax.rem(self.col, 2)


    def peer(self, x=0, y=0, z=0, core=0):
        z_at = lax.rem(self.zh * 2 + self.zl + z, 4)
        row = lax.rem(self.x + x, 4) * 4 + lax.div(z_at, 2) * 2 + lax.rem(self.core + core, 2)
        return (row, lax.rem(self.y + y, 4) * 2 + lax.rem(z_at, 2))

    def all_peers(self):
        steps = [dict(core=1)] + [{axis: d} for axis in "xyz" for d in (1, 2, 3)]
        return [self.peer(**step) for step in steps]


class RowGroup:
    def __init__(self, place):
        self.place = place
        col = place.col
        self.peers = {
            "p": (self.slot(1, 0), col),
            "m": (self.slot(3, 0), col),
            "pair": (self.slot(0, 1), col),
            "sib": (self.slot(0, 0, 1), col),
        }

    def slot(self, ring, pair, sib=0):
        at = self.place
        return (
            lax.rem(at.x + ring, 4) * 4
            + lax.rem(at.zh + pair, 2) * 2
            + lax.rem(at.core + sib, 2)
        )


class ColGroup:
    def __init__(self, place):
        self.place = place
        row = place.row
        self.peers = {
            "p": (row, self.slot(1, 0)),
            "m": (row, self.slot(3, 0)),
            "pair": (row, self.slot(0, 1)),
        }

    def slot(self, ring, pair):
        at = self.place
        return lax.rem(at.y + ring, 4) * 2 + lax.rem(at.zl + pair, 2)


class Wire:
    def __init__(self, send, recv):
        self.send, self.recv = send, recv
        self.names = {}
        self.open = []

    def index(self, name):
        return self.names.setdefault(name, len(self.names))

    def push(self, name, src, dst, to):
        at = self.index(name)
        copy = pltpu.make_async_remote_copy(
            src_ref=src,
            dst_ref=dst,
            send_sem=self.send.at[at],
            recv_sem=self.recv.at[at],
            device_id=to,
            device_id_type=pl.DeviceIdType.MESH,
        )
        copy.start()
        self.open.append(copy)

    def take(self, name, dst, to):
        at = self.index(name)
        pltpu.make_async_remote_copy(
            src_ref=dst,
            dst_ref=dst,
            send_sem=self.send.at[at],
            recv_sem=self.recv.at[at],
            device_id=to,
            device_id_type=pl.DeviceIdType.MESH,
        ).wait_recv()

    def drain(self):
        for copy in self.open:
            copy.wait_send()
        self.open = []


def greet(devices):
    barrier = pltpu.get_barrier_semaphore()
    for device in devices:
        pl.semaphore_signal(barrier, inc=1, device_id=device, device_id_type=pl.DeviceIdType.MESH)
    pl.semaphore_wait(barrier, len(devices))


MOVES = {"p": (3, 0, 0), "m": (1, 0, 0), "pair": (0, 1, 0), "sib": (0, 0, 1)}


QUARTER = ((0, 3, False), (3, 3, False), (6, 1, True), (7, 1, True))
MORE = ((0, 3, False), (3, 2, False), (5, 1, True), (6, 2, True))


def gather(wire, group, buf, tag, parts, per=1):
    unit = buf.shape[1] // 8

    def view(slot, part):
        start, size, _ = parts[part]
        if per == 1:
            return buf.at[slot, pl.ds(start * unit, size * unit)]
        return buf.at[pl.ds(slot * per + start, size)]

    def whole(slot):
        return buf.at[slot] if per == 1 else buf.at[pl.ds(slot * per, per)]

    has_sib = "sib" in group.peers
    late = [c for c in range(4) if parts[c][2]]
    early = [c for c in range(4) if not parts[c][2]]

    def send(ring, pair, part, way):
        ref = view(group.slot(ring, pair), part)
        dr, dp, dk = MOVES[way]
        name = (tag, (ring + dr) % 4, (pair + dp) % 2, dk, part)
        wire.push(name, ref, ref, group.peers[way])

    def take(ring, pair, part):
        slot = group.slot(ring, pair)
        wire.take((tag, ring, pair, 0, part), view(slot, part), group.peers["p"])

    def share(ring, pair):
        if has_sib:
            ref = whole(group.slot(ring, pair))
            wire.push((tag, ring, pair, 1), ref, ref, group.peers["sib"])

    def relay(pair, which):
        for c in which:
            ring, way = ((3, "p"), (1, "m"))[c % 2]
            take(ring, pair, c)
            send(ring, pair, c, way)
            if c in late and pair == 0:
                send(ring, pair, c, "pair")

    def rest(pair, which):
        for c in which:
            ring = (1, 3)[c % 2]
            take(ring, pair, c)
            if c in late and pair == 0:
                send(ring, pair, c, "pair")

    for c in early:
        send(0, 0, c, "pair")
    for c in early + late:
        send(0, 0, c, ("p", "m")[c % 2])
    yield
    for c in early + late:
        send(0, 0, c, ("m", "p")[c % 2])
    for c in late:
        send(0, 0, c, "pair")
    share(0, 0)
    yield
    relay(0, early + late)
    yield
    for c in early:
        take(0, 1, c)
        send(0, 1, c, "p")
        send(0, 1, c, "m")
    yield
    rest(0, late + early)
    share(1, 0)
    share(3, 0)
    yield
    for c in late:
        take(2, 0, c)
        send(2, 0, c, "pair")
    relay(1, early)
    yield
    for c in early:
        take(2, 0, c)
    share(2, 0)
    for c in late:
        take(0, 1, c)
    share(0, 1)
    yield
    rest(1, early)
    for ring in (1, 3):
        for c in late:
            take(ring, 1, c)
        share(ring, 1)
    for c in early + late:
        take(2, 1, c)
    share(2, 1)
    yield
    if has_sib:
        for pair in (0, 1):
            for ring in (0, 1, 3, 2):
                slot = group.slot(ring, pair, 1)
                wire.take((tag, ring, pair, 1), whole(slot), group.peers["p"])


def add_rows(rows, step, body):
    def one(i, carry):
        body(pl.ds(pl.multiple_of(i * step, step), step))
        return carry

    lax.fori_loop(0, rows // step, one, 0)


def scatter_shapes(rows, width):
    return [
        pltpu.VMEM((2, rows, width), BF16),
        pltpu.VMEM((2, rows, width), BF16),
        pltpu.VMEM((2, rows, width), BF16),
        pltpu.VMEM((2, rows, width), BF16),
        pltpu.VMEM((4, rows, width), BF16),
    ]


def scatter(wire, group, terms, bufs, tag, prepare, parts):
    relay_m, relay_p, from_m, from_p, from_pair = bufs
    unit = terms.shape[1] // 8
    cut = [pl.ds(start * unit, size * unit) for start, size, _ in parts]
    late = [c for c in range(4) if parts[c][2]]
    early = [c for c in range(4) if not parts[c][2]]
    start = parts[late[0]][0]
    first = pl.ds(start * unit, sum(parts[c][1] for c in late) * unit)
    to_p, to_m, to_pair = group.peers["p"], group.peers["m"], group.peers["pair"]

    def at(ring, pair, rows):
        return terms.at[group.slot(ring, pair), rows]

    def add(target, *others):
        def body(rows):
            total = target[rows].astype(F32)
            for other in others:
                total = total + other[rows].astype(F32)
            target[rows] = total.astype(BF16)

        add_rows(target.shape[0], unit, body)

    def cross(ring):
        dst = from_pair.at[ring, first]
        wire.push((tag, "first", ring), at(ring, 1, first), dst, to_pair)

    def crossed(ring):
        src = from_pair.at[ring, first]
        wire.take((tag, "first", ring), src, to_pair)
        add(at(ring, 0, first), src)

    def far(q, which):
        for c in which:
            dst, to = ((relay_m, to_p), (relay_p, to_m))[c % 2]
            wire.push((tag, "far", q, c), at(2, q, cut[c]), dst.at[q, cut[c]], to)

    def single(q, which):
        for c in which:
            ring, dst, to = ((3, from_p, to_m), (1, from_m, to_p))[c % 2]
            wire.push((tag, "one", q, c), at(ring, q, cut[c]), dst.at[q, cut[c]], to)

    def double(q, which):
        for c in which:
            ring, via, dst, to = ((1, relay_m, from_m, to_p), (3, relay_p, from_p, to_m))[c % 2]
            wire.take((tag, "far", q, c), via.at[q, cut[c]], to)
            add(at(ring, q, cut[c]), via.at[q, cut[c]])
            wire.push((tag, "two", q, c), at(ring, q, cut[c]), dst.at[q, cut[c]], to)

    def arrive(q, which):
        for c in which:
            one, two = ((from_p, from_m), (from_m, from_p))[c % 2]
            wire.take((tag, "one", q, c), one.at[q, cut[c]], to_p)
            wire.take((tag, "two", q, c), two.at[q, cut[c]], to_p)

    prepare(2, 1)
    cross(2)
    far(1, early)
    prepare(2, 0)
    far(0, early)
    yield
    prepare(1, 1)
    cross(1)
    prepare(3, 1)
    cross(3)
    single(1, early)
    crossed(2)
    far(0, late)
    yield
    double(1, early)
    prepare(1, 0)
    prepare(3, 0)
    single(0, early)
    yield
    crossed(1)
    crossed(3)
    single(0, late)
    double(0, early + late)
    yield
    prepare(0, 1)
    cross(0)
    for c in early:
        arrive(1, [c])
        add(at(0, 1, cut[c]), from_m.at[1, cut[c]], from_p.at[1, cut[c]])
        wire.push((tag, "last", c), at(0, 1, cut[c]), from_pair.at[0, cut[c]], to_pair)
    yield
    prepare(0, 0)
    arrive(0, early + late)
    wire.take((tag, "first", 0), from_pair.at[0, first], to_pair)
    for c in early:
        wire.take((tag, "last", c), from_pair.at[0, cut[c]], to_pair)


def exchange(wire, tag, axis, place, part, dst):
    for d in (1, 2, 3):
        wire.push((tag, axis, d), part(d), dst(d), place.peer(**{axis: d}))


def block(index, rows):
    return pl.ds(pl.multiple_of(index * rows, rows), rows)


def total_near(wire, place, mine, result, in_core, in_x, tag):
    half, quarter = TOTAL_ROWS // 2, TOTAL_ROWS // 8
    core, x = place.core, place.x
    sib = place.peer(core=1)
    wire.push((tag, "core"), mine.at[block(1 - core, half)], in_core, sib)
    yield
    wire.take((tag, "core"), in_core, sib)

    def fold(i, carry):
        at = pl.ds(pl.multiple_of(core * half + i * 64, 64), 64)
        mine[at] += in_core[block(i, 64)]
        return carry

    lax.fori_loop(0, half // 64, fold, 0)

    def own(index):
        return mine.at[block(core * 4 + index, quarter)]

    exchange(
        wire, tag, "x", place, lambda d: own(lax.rem(x + d, 4)), lambda d: in_x.at[d - 1]
    )
    yield
    for d in (1, 2, 3):
        wire.take((tag, "x", d), in_x.at[d - 1], sib)
    at = block(x, quarter)
    result[at] = mine[block(core * 4 + x, quarter)] + in_x[0] + in_x[1] + in_x[2]
    exchange(wire, tag + "r", "x", place, lambda d: result.at[at], lambda d: result.at[at])
    yield
    for d in (1, 2, 3):
        wire.take((tag + "r", "x", d), result.at[block(lax.rem(x + 4 - d, 4), quarter)], sib)


def total_far(wire, place, mine, result, in_y, in_z, tag):
    piece, quarter = TOTAL_ROWS // 32, TOTAL_ROWS // 8
    core, x, y = place.core, place.x, place.y
    z = place.zh * 2 + place.zl
    sib = place.peer(core=1)

    def at(x_at, y_at):
        return block(core * 16 + y_at * 4 + x_at, piece)

    exchange(
        wire,
        tag,
        "y",
        place,
        lambda d: mine.at[block(lax.rem(y + d, 4) * 4 + x, piece)],
        lambda d: in_y.at[d - 1],
    )
    yield
    for d in (1, 2, 3):
        wire.take((tag, "y", d), in_y.at[d - 1], sib)
    in_z[z] = mine[block(y * 4 + x, piece)] + in_y[0] + in_y[1] + in_y[2]
    exchange(wire, tag, "z", place, lambda d: in_z.at[z], lambda d: in_z.at[z])
    yield
    for d in (1, 2, 3):
        wire.take((tag, "z", d), in_z.at[lax.rem(z + 4 - d, 4)], sib)
    result[at(x, y)] = in_z[0] + in_z[1] + in_z[2] + in_z[3]
    own = result.at[at(x, y)]
    exchange(wire, tag + "r", "x", place, lambda d: own, lambda d: own)
    yield
    for d in (1, 2, 3):
        wire.take((tag + "r", "x", d), result.at[at(lax.rem(x + 4 - d, 4), y)], sib)
    four = result.at[block(core * 4 + y, quarter)]
    exchange(wire, tag + "r", "y", place, lambda d: four, lambda d: four)
    yield
    for d in (1, 2, 3):
        there = block(core * 4 + lax.rem(y + 4 - d, 4), quarter)
        wire.take((tag + "r", "y", d), result.at[there], sib)
    half = block(core, TOTAL_ROWS // 2)
    wire.push((tag, "join"), result.at[half], result.at[half], sib)
    yield
    wire.take((tag, "join"), result.at[block(1 - core, TOTAL_ROWS // 2)], sib)


def run(steps):
    for _ in steps:
        pass


def dot(a, b, dims=((1,), (0,))):
    return lax.dot_general(a, b, (dims, ((), ())), preferred_element_type=F32)


ANY = pl.BlockSpec(memory_space=pl.ANY)
VM = pl.BlockSpec(memory_space=pltpu.VMEM)


def remote_params(collective_id):
    return pltpu.CompilerParams(
        collective_id=collective_id, has_side_effects=True, vmem_limit_bytes=VMEM_LIMIT
    )


ORDER = [(2, 1), (2, 0), (1, 1), (3, 1), (1, 0), (3, 0), (0, 1), (0, 0)]


def middle_kernel(
    cols, live, tiles, nodes_any, nodes, cot, w_in, bias, w_out, gain, shift,
    near0_out, near1_out, grads, updated, direct, part_sum,
    near0, near1, slots, terms0, terms1, *rest,
):
    bufs0, bufs1, rest = rest[:5], rest[5:10], rest[10:]
    msg_s, act_s, gproj_s, gpre_s, weights, in_core, in_x, send, recv, load = rest
    place = Place()
    across, along = RowGroup(place), ColGroup(place)
    width = nodes.shape[1]
    rows = nodes.shape[0]
    near, terms = (near0, near1), (terms0, terms1)

    mine = [
        pltpu.make_async_copy(
            nodes_any.at[:, :, pl.ds(h * 128, 128)],
            near[h].at[pl.ds(across.slot(0, 0) * 8, 8)],
            load.at[8 + h],
        )
        for h in (0, 1)
    ]
    for copy in mine:
        copy.start()

    def loader(ring, pair):
        at = pl.ds(along.slot(ring, pair) * 8, 8)
        return pltpu.make_async_copy(tiles.at[at], slots.at[at], load.at[ring * 2 + pair])

    for at in ORDER:
        loader(*at).start()
    greet(place.all_peers())
    wire = Wire(send, recv)
    for copy in mine:
        copy.wait()

    def mask(ring, pair):
        loader(ring, pair).wait()
        base = along.slot(ring, pair) * 8

        def one(i, carry):
            held = jnp.full((1, 128), live[base + i], jnp.int32)
            for k in range(4):
                keep = (held > k).astype(F32).astype(BF16)
                slots[base + i, k] = slots[base + i, k] * keep
            return carry

        lax.fori_loop(0, 8, one, 0)

    def product(h, ring, pair):
        slot = along.slot(ring, pair)

        def one(j, carry):
            for u in range(2):
                i = slot * 8 + j * 2 + u
                left = jnp.concatenate([slots[i, k] for k in range(4)], axis=1)
                right = []
                for k in range(4):
                    right.append(near[h][cols[i, k]])
                at = pl.ds(pl.multiple_of((j * 2 + u) * 128, 128), 128)
                terms[h][slot, at] = dot(left, jnp.concatenate(right, axis=0)).astype(BF16)
            return carry

        lax.fori_loop(0, 4, one, 0)

    gather0 = gather(wire, across, near0, "n0", MORE, 8)
    gather1 = gather(wire, across, near1, "n1", QUARTER, 8)
    next(gather0)
    for at in ORDER[:4]:
        mask(*at)
    next(gather0)
    for at in ORDER[4:]:
        mask(*at)
    for _ in range(3):
        next(gather0)
    next(gather1)
    next(gather0)
    next(gather1)
    run(gather0)

    def prepare0(ring, pair):
        product(0, ring, pair)
        next(gather1, None)

    scatter0 = scatter(wire, along, terms0, bufs0, "s0", prepare0, MORE)
    for _ in range(4):
        next(scatter0)
    run(gather1)
    leaving = [
        pltpu.make_async_copy(near[h], out, load.at[10 + h])
        for h, out in ((0, near0_out), (1, near1_out))
    ]
    for copy in leaving:
        copy.start()
    scatter1 = scatter(
        wire, along, terms1, bufs1, "s1", lambda *at: product(1, *at), MORE
    )
    for _ in scatter1:
        next(scatter0, None)
    run(scatter0)
    own = along.slot(0, 0)
    gsum = weights.at[pl.ds(3 * width, 8)]
    weights[3 * width :] = jnp.zeros((weights.shape[0] - 3 * width, width), F32)

    def chunk(i, carry):
        at = pl.ds(pl.multiple_of(i * 256, 256), 256)
        msg = jnp.concatenate(
            [
                (
                    terms[h][own, at].astype(F32)
                    + bufs[2][0, at].astype(F32)
                    + bufs[3][0, at].astype(F32)
                    + bufs[4][0, at].astype(F32)
                ).astype(BF16)
                for h, bufs in ((0, bufs0), (1, bufs1))
            ],
            axis=1,
        )
        msg_s[at] = msg
        mine = nodes[at]
        pre = dot(mine, w_in[:width]) + dot(msg, w_in[width:]) + bias[...]
        sig = jax.nn.sigmoid(pre)
        act = (pre * sig).astype(BF16)
        act_s[at] = act
        proj = dot(act, w_out[...])
        mean = jnp.mean(proj, axis=-1, keepdims=True)
        off = proj - mean
        var = jnp.mean(off * off, axis=-1, keepdims=True)
        rstd = 1.0 / jnp.sqrt(var + EPS)
        normed = off * rstd
        updated[at] = (mine.astype(F32) + normed * gain[...] + shift[...]).astype(BF16)
        grad_out = cot[at].astype(F32)
        gscaled = grad_out * gain[...]
        gproj = (
            (
                gscaled
                - jnp.mean(gscaled, axis=-1, keepdims=True)
                - normed * jnp.mean(gscaled * normed, axis=-1, keepdims=True)
            )
            * rstd
        ).astype(BF16)
        gproj_s[at] = gproj
        gact = dot(gproj, w_out[...], ((1,), (1,)))
        gpre = gact * sig * (1.0 + pre * (1.0 - sig))
        gpre_b = gpre.astype(BF16)
        gpre_s[at] = gpre_b
        grads[own, at] = dot(gpre_b, w_in[width:], ((1,), (1,))).astype(BF16)
        direct[at] = grad_out + dot(gpre_b, w_in[:width], ((1,), (1,)))
        gsum[0:1] += jnp.sum(gpre, axis=0, keepdims=True)
        gsum[1:2] += jnp.sum(grad_out * normed, axis=0, keepdims=True)
        gsum[2:3] += jnp.sum(grad_out, axis=0, keepdims=True)
        return carry

    lax.fori_loop(0, rows // 256, chunk, 0)
    steps = gather(wire, along, grads, "g", MORE)
    next(steps)
    weights[:width] = dot(nodes[...], gpre_s[...], ((0,), (0,)))
    next(steps)
    weights[width : 2 * width] = dot(msg_s[...], gpre_s[...], ((0,), (0,)))
    weights[2 * width : 3 * width] = dot(act_s[...], gproj_s[...], ((0,), (0,)))
    sums = total_near(wire, place, weights, part_sum, in_core, in_x, "w")
    for following in (sums, steps, sums, steps, steps, sums, steps, steps):
        next(following)
    run(steps)
    run(sums)
    for copy in leaving:
        copy.wait()
    wire.drain()


def middle(cols, live, tiles, nodes, cot, w_in, bias, w_out, gain, shift):
    rows, width = nodes.shape
    one = functools.partial(pltpu.VMEM, (rows, width))
    smem = pl.BlockSpec(memory_space=pltpu.SMEM)
    near = jax.ShapeDtypeStruct((128, 128, 128), BF16)
    return pl.pallas_call(
        middle_kernel,
        out_shape=[
            near,
            near,
            jax.ShapeDtypeStruct((8, rows, width), BF16),
            jax.ShapeDtypeStruct((rows, width), BF16),
            jax.ShapeDtypeStruct((rows, width), F32),
            jax.ShapeDtypeStruct((TOTAL_ROWS // 2, width), F32),
        ],
        in_specs=[smem, smem, ANY, ANY] + [VM] * 7,
        out_specs=[ANY] * 2 + [VM] * 4,
        scratch_shapes=[pltpu.VMEM((128, 128, 128), BF16)] * 2
        + [pltpu.VMEM(tiles.shape, BF16)]
        + [pltpu.VMEM((8, rows, 128), BF16)] * 2
        + scatter_shapes(rows, 128) * 2
        + [one(BF16)] * 4
        + [
            pltpu.VMEM((TOTAL_ROWS, width), F32),
            pltpu.VMEM((TOTAL_ROWS // 2, width), F32),
            pltpu.VMEM((3, TOTAL_ROWS // 8, width), F32),
        ]
        + [
            pltpu.SemaphoreType.DMA((240,)),
            pltpu.SemaphoreType.DMA((240,)),
            pltpu.SemaphoreType.DMA((12,)),
        ],
        compiler_params=remote_params(2),
        name="middle",
    )(cols, live, tiles, nodes.reshape(8, 128, width), nodes, cot, w_in, bias, w_out, gain, shift)


def backward_kernel(
    cols, count, tiles, near0_any, near1_any, grads, updated_in,
    tile_grads, back_any, updated,
    acc, near0, near1, back, load, leave,
):
    step = pl.program_id(0)
    per = tiles.shape[0]
    updated[...] = updated_in[...]

    @pl.when(step == 0)
    def _():
        copies = [
            pltpu.make_async_copy(near0_any, near0, load.at[0]),
            pltpu.make_async_copy(near1_any, near1, load.at[1]),
        ]
        for copy in copies:
            copy.start()

        def clear(i, carry):
            acc[i] = jnp.zeros(acc.shape[1:], F32)
            return carry

        lax.fori_loop(0, acc.shape[0], clear, 0)
        for copy in copies:
            copy.wait()

    scale = F32(256.0) ** F32(-0.5)

    def work(i, at, slots):
        live = count[at]
        grad = grads[pl.ds(i * 128, 128)]
        which = [cols[at, k] for k in range(slots)]
        picked = jnp.concatenate(
            [jnp.concatenate([near0[c], near1[c]], axis=1) for c in which], axis=0
        )
        made = (dot(grad, picked, ((1,), (1,))) * scale).astype(BF16)
        zero = jnp.zeros((128, 128), BF16)
        for k in range(slots):
            tile_grads[i, k] = jnp.where(k < live, made[:, k * 128 : k * 128 + 128], zero)
        kept = jnp.concatenate([jnp.where(k < live, tiles[i, k], zero) for k in range(slots)], axis=1)
        return which, dot(kept, grad, ((0,), (0,)))

    def both(i, slots):
        found = [work(i + u, step * per + i + u, slots) for u in (0, 1)]
        for which, terms in found:
            for k in range(slots):
                acc[which[k]] += terms[k * 128 : k * 128 + 128]

    for i in range(0, per, 2):
        most = jnp.maximum(count[step * per + i], count[step * per + i + 1])

        @pl.when(most <= 2)
        def _():
            for u in (0, 1):
                tile_grads[i + u, 2:4] = jnp.zeros((2, 128, 128), BF16)

        @pl.when(most <= 0)
        def _():
            for u in (0, 1):
                tile_grads[i + u, 0:2] = jnp.zeros((2, 128, 128), BF16)

        @pl.when((most > 0) & (most <= 2))
        def _():
            both(i, 2)

        @pl.when(most > 2)
        def _():
            both(i, 4)

    @pl.when(step == pl.num_programs(0) - 1)
    def _():
        def put(i, carry):
            back[i] = acc[i].astype(BF16)
            return carry

        copies = []
        for part in range(8):
            lax.fori_loop(part * 16, part * 16 + 16, put, 0)
            at = pl.ds(part * 16, 16)
            copies.append(pltpu.make_async_copy(back.at[at], back_any.at[at], leave.at[part]))
            copies[-1].start()
        for copy in copies:
            copy.wait()


def backward(cols, count, tiles, near0, near1, grads, updated):
    row_blocks = tiles.shape[0]
    width = grads.shape[1]
    columns = (128, 128, width)
    per = 8
    steps = row_blocks // per

    passed = [pl.BlockSpec((updated.shape[0] // steps, width), lambda s, *_: (s, 0))]
    return pl.pallas_call(
        backward_kernel,
        out_shape=[
            jax.ShapeDtypeStruct(tiles.shape, BF16),
            jax.ShapeDtypeStruct(columns, BF16),
            jax.ShapeDtypeStruct(updated.shape, BF16),
        ],
        grid_spec=pltpu.PrefetchScalarGridSpec(
            num_scalar_prefetch=2,
            grid=(steps,),
            in_specs=[
                pl.BlockSpec((per, 4, 128, 128), lambda s, *_: (s, 0, 0, 0)),
                ANY,
                ANY,
                pl.BlockSpec((per * 128, width), lambda s, *_: (s, 0)),
            ]
            + passed,
            out_specs=[
                pl.BlockSpec((per, 4, 128, 128), lambda s, *_: (s, 0, 0, 0)),
                ANY,
            ]
            + passed,
            scratch_shapes=[
                pltpu.VMEM(columns, F32),
                pltpu.VMEM(near0.shape, BF16),
                pltpu.VMEM(near1.shape, BF16),
                pltpu.VMEM(columns, BF16),
                pltpu.SemaphoreType.DMA((2,)),
                pltpu.SemaphoreType.DMA((8,)),
            ],
        ),
        compiler_params=pltpu.CompilerParams(vmem_limit_bytes=VMEM_LIMIT),
        name="backward",
    )(cols, count, tiles, near0, near1, grads, updated)


def finish_kernel(
    back, direct, part_sum, out, result,
    terms, others, relay_m, relay_p, from_m, from_p, from_pair, mine, in_y, in_z, send, recv, load,
):
    place = Place()
    group = RowGroup(place)
    rows = terms.shape[1]

    def loader(ring, pair):
        slot = group.slot(ring, pair)
        return pltpu.make_async_copy(back.at[slot], terms.at[slot], load.at[ring * 2 + pair])

    held = pltpu.make_async_copy(part_sum, mine, load.at[8])
    held.start()
    for at in ORDER:
        loader(*at).start()
    greet(place.all_peers())
    wire = Wire(send, recv)
    held.wait()
    sums = total_far(wire, place, mine, result, in_y, in_z, "w")
    next(sums)
    ahead = iter(ORDER)

    def swap():
        for ring, pair in ahead:
            wire.push(
                ("f", ring, pair),
                back.at[group.slot(ring, pair, 1)],
                others.at[ring * 2 + pair],
                group.peers["sib"],
            )
            return

    swap()
    swap()

    def prepare(ring, pair):
        swap()
        loader(ring, pair).wait()
        other = others.at[ring * 2 + pair]
        wire.take(("f", ring, pair), other, group.peers["sib"])
        slot = group.slot(ring, pair)

        def body(at):
            terms[slot, at] = (terms[slot, at].astype(F32) + other[at].astype(F32)).astype(BF16)

        add_rows(rows, 128, body)

    bufs = (relay_m, relay_p, from_m, from_p, from_pair)
    for point, _ in enumerate(scatter(wire, group, terms, bufs, "b", prepare, MORE)):
        if point in (0, 1, 3, 4):
            next(sums)
    own = group.slot(0, 0)

    def last(at):
        out[at] = (
            direct[at]
            + terms[own, at].astype(F32)
            + from_m[0, at].astype(F32)
            + from_p[0, at].astype(F32)
            + from_pair[0, at].astype(F32)
        ).astype(BF16)

    add_rows(rows, 128, last)
    run(sums)
    wire.drain()


def finish(back, direct, part_sum):
    rows, width = direct.shape
    return pl.pallas_call(
        finish_kernel,
        out_shape=[
            jax.ShapeDtypeStruct((rows, width), BF16),
            jax.ShapeDtypeStruct((TOTAL_ROWS, width), F32),
        ],
        in_specs=[ANY, VM, ANY],
        out_specs=[VM] * 2,
        scratch_shapes=[
            pltpu.VMEM((16, rows, width), BF16),
            pltpu.VMEM((8, rows, width), BF16),
        ]
        + scatter_shapes(rows, width)
        + [
            pltpu.VMEM((TOTAL_ROWS // 2, width), F32),
            pltpu.VMEM((3, TOTAL_ROWS // 32, width), F32),
            pltpu.VMEM((4, TOTAL_ROWS // 32, width), F32),
            pltpu.SemaphoreType.DMA((60,)),
            pltpu.SemaphoreType.DMA((60,)),
            pltpu.SemaphoreType.DMA((9,)),
        ],
        compiler_params=remote_params(3),
        name="finish",
    )(back.reshape(16, rows, width), direct, part_sum)


def write_kernel(grad, sums, grad_nodes, gw_in, gw_out, gvec):
    width = gw_out.shape[1]
    factor = F32(131072.0) ** F32(-0.5)
    grad_nodes[...] = grad[...]
    gw_in[...] = sums[: 2 * width] * factor
    gw_out[...] = sums[2 * width : 3 * width] * factor
    gvec[...] = sums[3 * width : 3 * width + 3] * factor


def write(grad, sums):
    width = grad.shape[1]
    return pl.pallas_call(
        write_kernel,
        out_shape=[
            jax.ShapeDtypeStruct(grad.shape, BF16),
            jax.ShapeDtypeStruct((2 * width, width), F32),
            jax.ShapeDtypeStruct((width, width), F32),
            jax.ShapeDtypeStruct((3, width), F32),
        ],
        in_specs=[VM] * 2,
        out_specs=[VM] * 4,
        name="write",
    )(grad, sums)


def body(nodes, tiles, tile_col, tile_count, w_in, bias_in, w_out, ln_gain, ln_shift, cotangent):
    rows, width = nodes.shape
    cols, count = tile_col[:, 0], tile_count[:, 0]
    slots = tiles[:, 0]
    cols = jnp.clip(cols, 0, 127)
    near0, near1, grads, updated, direct, part_sum = middle(
        cols, count, slots, nodes, cotangent, w_in, bias_in[None], w_out, ln_gain[None], ln_shift[None]
    )
    grads = grads.reshape(8 * rows, width)
    grad_tiles, back, updated = backward(cols, count, slots, near0, near1, grads, updated)
    grad_nodes, gw_in, gw_out, gvec = write(*finish(back, direct, part_sum))
    return updated, grad_nodes, grad_tiles[:, None], gw_in, gw_out, gvec


def solution(mesh):
    placed = (
        P(("row", "col"), None),
        P("row", "col", None, None, None),
        P("row", "col", None),
        P("row", "col"),
        P(),
        P(),
        P(),
        P(),
        P(),
        P(("row", "col"), None),
    )
    return jax.shard_map(
        body,
        mesh=mesh,
        in_specs=placed,
        out_specs=(
            P(("row", "col"), None),
            P(("row", "col"), None),
            P("row", "col", None, None, None),
            P(),
            P(),
            P(),
        ),
        check_vma=False,
    )
```
